32 devices in a mesh: dp: 2 (over y), expert: 16 (over z, x, core).
Axes of the slice: x: 2, y: 2, z: 4, core: 2. Of those that a mesh axis runs over, the one named last changes fastest.
Arguments:
- tokens: bfloat16 [4096, 2048], P(('dp', 'expert')), may hold values from -6 to 6
- lengths: int32 [64, 4], P(('dp', 'expert')), may hold values from 1 to 32, 64 in all within a row
- routes: int32 [4096, 6], P(('dp', 'expert')), may hold values from 0 to 15, all different within a row; in each aligned block of 64 rows (0 to 63, 64 to 127, ...) at most 32 rows name the same one
- gates: float32 [4096, 6], P(('dp', 'expert')), may hold values from 0.25 to 1
- norm_in: bfloat16 [2048], P(('dp', 'expert')), may hold values from 0.25 to 1.75
- latent_gain: bfloat16 [512], P(('dp', 'expert')), may hold values from 0.25 to 1.75
- norm_mid: bfloat16 [2048], P(('dp', 'expert')), may hold values from 0.25 to 1.75
- w_query: bfloat16 [2048, 3072], P(('dp', 'expert')), may hold values from -0.125 to 0.125
- w_latent: bfloat16 [2048, 576], P(('dp', 'expert')), may hold values from -0.125 to 0.125
- w_expand: bfloat16 [512, 4096], P(('dp', 'expert')), may hold values from -0.25 to 0.25
- w_output: bfloat16 [2048, 2048], P(None, ('dp', 'expert')), may hold values from -0.375 to 0.375
- shared_gate: bfloat16 [2048, 2816], P(('dp', 'expert')), may hold values from -0.125 to 0.125
- shared_up: bfloat16 [2048, 2816], P(('dp', 'expert')), may hold values from -0.125 to 0.125
- shared_down: bfloat16 [2816, 2048], P(None, ('dp', 'expert')), may hold values from -0.109375 to 0.109375
- expert_gate: bfloat16 [16, 2048, 1408], P('expert', 'dp'), may hold values from -0.125 to 0.125
- expert_up: bfloat16 [16, 2048, 1408], P('expert', 'dp'), may hold values from -0.125 to 0.125
- expert_down: bfloat16 [16, 1408, 2048], P('expert', None, 'dp'), may hold values from -0.15625 to 0.15625
- cotangent: float32 [4096, 2048], P(('dp', 'expert')), may hold values from -6 to 6
Outputs:
- out: bfloat16 [4096, 2048], P(('dp', 'expert'))
- d_tokens: float32 [4096, 2048], P(('dp', 'expert'))
- d_norm_in: float32 [2048], P(('dp', 'expert'))
- d_latent_gain: float32 [512], P(('dp', 'expert'))
- d_norm_mid: float32 [2048], P(('dp', 'expert'))
- d_w_query: float32 [2048, 3072], P(('dp', 'expert'))
- d_w_latent: float32 [2048, 576], P(('dp', 'expert'))
- d_w_expand: float32 [512, 4096], P(('dp', 'expert'))
- d_w_output: float32 [2048, 2048], P(None, ('dp', 'expert'))
- d_shared_gate: float32 [2048, 2816], P(('dp', 'expert'))
- d_shared_up: float32 [2048, 2816], P(('dp', 'expert'))
- d_shared_down: float32 [2816, 2048], P(None, ('dp', 'expert'))
- d_expert_gate: float32 [16, 2048, 1408], P('expert', 'dp')
- d_expert_up: float32 [16, 2048, 1408], P('expert', 'dp')
- d_expert_down: float32 [16, 1408, 2048], P('expert', None, 'dp')
The draws below stay inside these ranges and needn't reach their ends.
Inputs may be any that keep to these rules, and one draw needn't show every extreme that they name: `routes`: each row names 6 different experts; in each aligned block of 64 rows (one micro-batch of one device) no expert is named by more than 32 rows, a bound that some block reaches. `lengths`: each row sums to 64; its longest sequence has exactly 32 tokens.
All inputs are finite; a program needn't handle non-finite values.
Results may differ from the reference program's by a relative error of at most 0.019.
Values may be sent and summed in bfloat16 or wider, within the bound.
No kernel may reach another device: no remote copies, remote signals or barrier semaphores. Data moves between devices by JAX's collectives and lax.ppermute only.
A program may use at most 448 MiB of HBM per device.

```python
import math
import jax
import jax.numpy as jnp
import numpy as np
from jax import lax

D = 2048
HEADS = 16
HD = 128
RD = 64
VD = 128
LAT = 512
FF_E = 1408
FF_S = 2816
TOP = 6
MB_TOK = 64
SEQS = 4
EXPERTS = 16
CAP = 32
MAXLEN = 32
TOKENS = 4096
BLOCKS = 64


def levels(own_key, dims, cuts, smallest, high):
    def one(dim, shards_of):
        draws = jax.random.uniform(jax.random.fold_in(jax.random.fold_in(own_key, 6), dim), (shards_of,), jnp.float32, smallest / len(cuts), high / len(cuts))
        return jnp.repeat(jnp.exp(draws), dims[dim] // shards_of).reshape((-1,) + (1,) * (len(dims) - dim - 1))

    loudness = one(*cuts[0])
    for cut in cuts[1:]:
        loudness = loudness * one(*cut)
    return loudness


def profile(count, total, bound, lean):
    loads = [(1 << 20) // math.isqrt(rank ** lean) + 1 for rank in range(2, count + 1)]
    surplus, counts = total - bound - (count - 1), [1] * (count - 1)
    while surplus > 0:
        movable = [i for i in range(count - 1) if counts[i] < bound]
        mass, left = sum([loads[i] for i in movable]), surplus
        for i in movable:
            addition = min(bound - counts[i], max(1, left * loads[i] // mass), surplus)
            counts[i] = counts[i] + addition
            surplus = surplus - addition
    return np.array([bound] + counts)


def ragged_sizes(key, count, total, most, skew):
    if count == 2:
        one = jax.random.randint(key, (), max(1, total - most), min(most, total - 1) + 1)
        return jnp.stack([one, total - one])
    sizes = jnp.asarray(profile(count, total, most, skew), jnp.int32)
    twos = (count - 1) // 2
    donor, sink = sizes[1:1 + 2 * twos:2], sizes[2:2 + 2 * twos:2]
    margin = jnp.minimum(donor - 1, most - sink)
    moved = jax.random.randint(jax.random.fold_in(key, 1), (twos,), 0, 1 << 20) % (margin + 1)
    sizes = sizes.at[1:1 + 2 * twos:2].set(donor - moved).at[2:2 + 2 * twos:2].set(sink + moved)
    return sizes[jax.random.permutation(jax.random.fold_in(key, 2), count)]


def routed_block(rng, own, number, rows, amount, top, reach, slope):
    sequence = jax.random.permutation(rng, amount)
    crowded, usual = portions_of(amount, rows * top, reach, slope, True), portions_of(amount, rows * top, reach, slope, False)
    places = jnp.arange(amount)

    def named(sizes, rotation):
        used = int((sizes > 0).sum())
        fixed = max(1, used // 4)
        shifted = fixed + (places - fixed + rotation * (used - fixed)) % max(1, amount - fixed)
        return jnp.zeros((amount,), jnp.int32).at[sequence[jnp.where(places < fixed, places, shifted)]].set(jnp.asarray(sizes, jnp.int32))

    sizes = jnp.where(number % 4 == 0, named(crowded, number // 4), named(usual, number - number // 4 - 1))
    mixed = jax.random.permutation(jax.random.fold_in(own, 3), amount)
    source_of, taker = mixed[0:amount // 2 * 2:2], mixed[1:amount // 2 * 2:2]
    room = jnp.minimum(sizes[source_of] - 1, reach - sizes[taker]) // 2
    room = jnp.where((source_of == sequence[0]) | (taker == sequence[0]) | (sizes[taker] == 0), 0, jnp.maximum(room, 0))
    shifted = jax.random.randint(jax.random.fold_in(own, 4), (amount // 2,), 0, 1 << 20) % (room + 1)
    sizes = sizes.at[source_of].add(-shifted).at[taker].add(shifted)
    items = jnp.searchsorted(jnp.cumsum(sizes), jnp.arange(rows * top), side="right").astype(jnp.int32)
    listing = items.reshape(top, rows).T
    listing = listing[jax.random.permutation(jax.random.fold_in(own, 1), rows)]
    rotation = jax.random.randint(jax.random.fold_in(own, 2), (rows, 1), 0, top)
    return jnp.take_along_axis(listing, (jnp.arange(top)[None, :] + rotation) % top, axis=1)


def portions_of(amount, total, reach, slope, full):
    weights = [(1 << 20) // math.isqrt(grade ** slope) + 1 for grade in range(1, amount + 1)]
    largest = reach if full else min(reach, max(-(-total // amount), total * weights[0] // sum(weights)))
    least = 1 if total - largest >= amount - 1 else 0
    given, spare = [largest] + [least] * (amount - 1), total - largest - least * (amount - 1)
    while spare > 0:
        candidates = [i for i in range(1, amount) if given[i] < largest] or [i for i in range(1, amount) if given[i] < reach]
        mass, remaining = sum([weights[i] for i in candidates]), spare
        for i in candidates:
            extra = min(reach - given[i], max(1, remaining * weights[i] // mass), spare)
            given[i] = given[i] + extra
            spare = spare - extra
    return np.array(given)


def scatter_about(own_key, shape, width, most, split=(), kind=jnp.bfloat16):
    entries = width * jax.random.normal(own_key, shape, jnp.float32)
    if split:
        entries = entries * levels(own_key, shape, split, -0.22, 0.18)
    return jnp.clip(entries, -most, most).astype(kind)


def setup_inputs(seed: int = 0) -> dict:
    splits = jax.random.split(jax.random.key(seed), 19)
    tokens = scatter_about(splits[0], (TOKENS, D), 1.0, 6.0, ((0, 32),))
    lengths = jax.vmap(lambda own: ragged_sizes(own, SEQS, MB_TOK, MAXLEN, 1))(jax.random.split(splits[1], BLOCKS)).reshape((BLOCKS, SEQS)).astype(jnp.int32)
    routes_keys = jax.random.split(jax.random.fold_in(splits[2], 1), TOKENS // MB_TOK)
    routes_turns = jax.random.permutation(jax.random.fold_in(splits[2], 3), TOKENS // MB_TOK)
    routes = jax.vmap(lambda own, number: routed_block(jax.random.fold_in(splits[2], 2), own, number, MB_TOK, EXPERTS, TOP, CAP, 1))(routes_keys, routes_turns).reshape((TOKENS, TOP))
    gates = jnp.clip(0.25 + 0.75 * jax.random.uniform(splits[3], (TOKENS, TOP), jnp.float32) ** levels(splits[3], (TOKENS, TOP), ((0, 32),), -0.2, 0.2), 0.25, 1.0)
    norm_in = jnp.clip(1.0 + 0.15 * jax.random.normal(splits[4], (D,), jnp.float32), 0.25, 1.75).astype(jnp.bfloat16)
    latent_gain = jnp.clip(1.0 + 0.15 * jax.random.normal(splits[5], (LAT,), jnp.float32), 0.25, 1.75).astype(jnp.bfloat16)
    norm_mid = jnp.clip(1.0 + 0.15 * jax.random.normal(splits[6], (D,), jnp.float32), 0.25, 1.75).astype(jnp.bfloat16)
    w_query = scatter_about(splits[7], (D, HEADS * (HD + RD)), D ** -0.5, 0.125, ((0, 32),))
    w_latent = scatter_about(splits[8], (D, LAT + RD), D ** -0.5, 0.125, ((0, 32),))
    w_expand = scatter_about(splits[9], (LAT, HEADS * (HD + VD)), LAT ** -0.5, 0.25, ((0, 32),))
    w_output = scatter_about(splits[10], (HEADS * VD, D), (HEADS * VD // 8) ** -0.5, 0.375, ((1, 32),))
    shared_gate = scatter_about(splits[11], (D, FF_S), D ** -0.5, 0.125, ((0, 32),))
    shared_up = scatter_about(splits[12], (D, FF_S), D ** -0.5, 0.125, ((0, 32),))
    shared_down = scatter_about(splits[13], (FF_S, D), FF_S ** -0.5, 0.109375, ((1, 32),))
    expert_gate = scatter_about(splits[14], (EXPERTS, D, FF_E), D ** -0.5, 0.125, ((0, 16), (1, 2)))
    expert_up = scatter_about(splits[15], (EXPERTS, D, FF_E), D ** -0.5, 0.125, ((0, 16), (1, 2)))
    expert_down = scatter_about(splits[16], (EXPERTS, FF_E, D), FF_E ** -0.5, 0.15625, ((0, 16), (2, 2)))
    cotangent = scatter_about(splits[17], (TOKENS, D), 1.0, 6.0, ((0, 32),), jnp.float32)
    return dict(tokens=tokens, lengths=lengths, routes=routes, gates=gates, norm_in=norm_in, latent_gain=latent_gain, norm_mid=norm_mid, w_query=w_query, w_latent=w_latent, w_expand=w_expand, w_output=w_output, shared_gate=shared_gate, shared_up=shared_up, shared_down=shared_down, expert_gate=expert_gate, expert_up=expert_up, expert_down=expert_down, cotangent=cotangent)


EPS = 1e-06
HIGH = lax.Precision.HIGHEST

@jax.custom_vjp
def low(v):
    return lax.optimization_barrier(v.astype(jnp.bfloat16)).astype(jnp.float32)

@jax.custom_vjp
def low_back(v):
    return v

def low_keep(v):
    return (low(v), None)

def low_pass(kept, grad):
    return (grad,)

def back_keep(v):
    return (v, None)

def back_low(kept, grad):
    return (low(grad),)
low.defvjp(low_keep, low_pass)
low_back.defvjp(back_keep, back_low)

def matmul(left, right):
    return jnp.dot(left, right, precision=HIGH, preferred_element_type=jnp.float32)

def rms(values):
    return values * lax.rsqrt(lax.optimization_barrier(jnp.mean(values * values, axis=-1, keepdims=True)) + EPS)

def layout(lengths, rows):
    ends = jnp.cumsum(lengths, axis=-1)
    place = jnp.arange(rows, dtype=jnp.int32)
    passed = (place[None, :, None] >= ends[:, None, :]).astype(jnp.int32)
    doc = lax.optimization_barrier(jnp.sum(passed, axis=-1))
    start = lax.optimization_barrier(jnp.sum(passed * lengths[:, None, :], axis=-1))
    return ((place[None, :] - start).astype(jnp.float32), doc)

def angles(position, size):
    freq = jnp.power(10000.0, -2.0 * jnp.arange(size // 2, dtype=jnp.float32) / size)
    theta = position[..., None] * freq
    return (jnp.cos(theta), jnp.sin(theta))

def rotate(values, cosine, sine):
    half = values.shape[-1] // 2
    first, second = (values[..., :half], values[..., half:])
    return jnp.concatenate([first * cosine - second * sine, second * cosine + first * sine], axis=-1)

def forward(position, same_seq, routes, gates, tokens, norm_in, latent_gain, norm_mid, w_query, w_latent, w_expand, w_output, shared_gate, shared_up, shared_down, expert_gate, expert_up, expert_down):
    rows = tokens.shape[0]
    blocks = rows // MB_TOK
    normed = low(rms(tokens) * norm_in)
    query = low_back(matmul(normed, w_query)).reshape(rows, HEADS, HD + RD)
    latent = low_back(matmul(normed, w_latent))
    compressed = low(rms(latent[:, :LAT]) * latent_gain)
    expanded = low_back(matmul(compressed, w_expand)).reshape(rows, HEADS, HD + VD)
    cosine, sine = angles(position.reshape(rows), RD)
    q_rot = rotate(query[..., HD:], cosine[:, None, :], sine[:, None, :])
    q_all = low(jnp.concatenate([query[..., :HD], q_rot], axis=-1))
    k_rot = rotate(latent[:, LAT:], cosine, sine)
    k_all = low(jnp.concatenate([expanded[..., :HD], jnp.broadcast_to(k_rot[:, None, :], (rows, HEADS, RD))], axis=-1))
    values = low(expanded[..., HD:])
    q_blocks = q_all.reshape(blocks, MB_TOK, HEADS, HD + RD)
    k_blocks = k_all.reshape(blocks, MB_TOK, HEADS, HD + RD)
    v_blocks = values.reshape(blocks, MB_TOK, HEADS, VD)
    scores = low_back(jnp.einsum('bqhd,bkhd->bhqk', q_blocks, k_blocks, precision=HIGH) * (HD + RD) ** (-0.5))
    scores = jnp.where(same_seq[:, None], scores, -1e+30)
    probs = low(jax.nn.softmax(scores, axis=-1))
    attended = jnp.einsum('bhqk,bkhd->bqhd', probs, v_blocks, precision=HIGH).reshape(rows, HEADS * VD)
    attended = low(low_back(attended))
    mid = tokens + low_back(matmul(attended, w_output))
    normed_mid = low(rms(mid) * norm_mid)
    s_gate = low_back(matmul(normed_mid, shared_gate))
    s_up = low_back(matmul(normed_mid, shared_up))
    shared_out = low_back(matmul(low(jax.nn.silu(s_gate) * s_up), shared_down))

    def one_expert(inputs_mid, gate_w, up_w, down_w, share):
        inputs = low_back(inputs_mid)
        e_gate = low_back(matmul(inputs, gate_w))
        e_up = low_back(matmul(inputs, up_w))
        e_out = low(low_back(matmul(low(jax.nn.silu(e_gate) * e_up), down_w)))
        return share[:, None] * e_out
    checked = jax.checkpoint(one_expert)
    routed = jnp.zeros((rows, D), jnp.float32)
    for index in range(EXPERTS):
        share = lax.optimization_barrier(jnp.sum(jnp.where(routes == index, gates, 0.0), axis=1))
        routed = routed + checked(normed_mid, expert_gate[index], expert_up[index], expert_down[index], share)
    return mid + shared_out + routed

def reference(tokens, lengths, routes, gates, norm_in, latent_gain, norm_mid, w_query, w_latent, w_expand, w_output, shared_gate, shared_up, shared_down, expert_gate, expert_up, expert_down, cotangent):
    position, doc = layout(lengths, MB_TOK)
    place = jnp.arange(MB_TOK, dtype=jnp.int32)
    same_seq = (doc[:, :, None] == doc[:, None, :]) & (place[None, None, :] <= place[None, :, None])

    def fixed(*floats):
        return forward(position, same_seq, routes, gates, *floats)
    primals = tuple((a.astype(jnp.float32) for a in (tokens, norm_in, latent_gain, norm_mid, w_query, w_latent, w_expand, w_output, shared_gate, shared_up, shared_down, expert_gate, expert_up, expert_down)))
    result, pullback = jax.vjp(fixed, *primals)
    grads = pullback(cotangent.astype(jnp.float32))
    return (result.astype(jnp.bfloat16), grads[0], grads[1], grads[2], grads[3], grads[4], grads[5], grads[6], grads[7], grads[8], grads[9], grads[10], grads[11], grads[12], grads[13])
```

```python
import functools

import jax
import jax.numpy as jnp
from jax import lax
from jax.experimental import pallas as pl
from jax.experimental.pallas import tpu as pltpu
from jax.sharding import PartitionSpec as P

HEADS = 16
HD = 128
RD = 64
VD = 128
LAT = 512
TOP = 6
EPS = 1e-06
CHUNK = 256
SCALE = (HD + RD) ** (-0.5)
BF = jnp.bfloat16
F32 = jnp.float32
VMEM_LIMIT = 56 * 1024 * 1024


def matmul(left, right):
    return jnp.dot(left, right, preferred_element_type=F32)


def mat_trans(left, right):
    return lax.dot_general(left, right, (((1,), (1,)), ((), ())), preferred_element_type=F32)


def contract(left, right):
    return lax.dot_general(left, right, (((0,), (0,)), ((), ())), preferred_element_type=F32)


def rms_scale(values):
    return lax.rsqrt(jnp.mean(values * values, axis=-1, keepdims=True) + EPS)


def rms_back(incoming, values, scale, gain):
    scaled = incoming * gain
    inner = jnp.mean(scaled * values, axis=-1, keepdims=True)
    grad_in = scale * (scaled - values * scale * scale * inner)
    grad_gain = jnp.sum(incoming * values * scale, axis=0)
    return (grad_in, grad_gain)


def layout(lengths, rows):
    ends = jnp.cumsum(lengths, axis=-1)
    place = jnp.arange(rows, dtype=jnp.int32)
    passed = (place[None, :, None] >= ends[:, None, :]).astype(jnp.int32)
    doc = jnp.sum(passed, axis=-1)
    start = jnp.sum(passed * lengths[:, None, :], axis=-1)
    return ((place[None, :] - start).astype(F32), doc)


def move(value, to):
    return lax.ppermute(value, "expert", [(i, to(i)) for i in range(16)])


def z_up(value):
    return move(value, lambda i: (i + 4) % 16)


def z_down(value):
    return move(value, lambda i: (i + 12) % 16)


def z_two(value):
    return move(value, lambda i: (i + 8) % 16)


def x_swap(value):
    return move(value, lambda i: i ^ 2)


def core_swap(value):
    return move(value, lambda i: i ^ 1)


def gather_rows(own):
    pieces = [own]
    for _ in range(3):
        pieces.append(z_up(pieces[-1]))
    near = jnp.concatenate(pieces, axis=0)
    far = jnp.concatenate([x_swap(piece) for piece in pieces], axis=0)
    return jnp.concatenate([near, far, core_swap(near), core_swap(far)], axis=0)


def scatter_rows(partial):
    quarter = partial.shape[0] // 4
    rows = quarter // 4
    far = core_swap(partial[3 * quarter :])
    near = core_swap(partial[2 * quarter : 3 * quarter])
    far = (far.astype(F32) + partial[quarter : 2 * quarter].astype(F32)).astype(BF)
    near = near.astype(F32) + partial[:quarter].astype(F32)
    total = None
    for step in (3, 2, 1, 0):
        part = slice(step * rows, (step + 1) * rows)
        term = near[part] + x_swap(far[part]).astype(F32)
        if total is not None:
            term = term + z_down(total.astype(BF)).astype(F32)
        total = term
    return total


def exchange(blocks, place):
    z, x, core = place
    rest = blocks.shape[1:]
    view = blocks.reshape((4, 2, 2) + rest)

    def at(value, index, axis):
        return lax.dynamic_index_in_dim(value, index, axis, keepdims=False)

    view = jnp.stack([at(view, core, 2), core_swap(at(view, 1 - core, 2))], axis=2)
    view = jnp.stack([at(view, x, 1), x_swap(at(view, 1 - x, 1))], axis=1)
    view = jnp.stack(
        [
            at(view, z, 0),
            z_up(at(view, (z + 1) % 4, 0)),
            z_two(at(view, (z + 2) % 4, 0)),
            z_down(at(view, (z + 3) % 4, 0)),
        ],
        axis=0,
    )
    return view.reshape(blocks.shape)


def reorder_kernel(index_ref, in_ref, out_ref):
    out_ref[...] = in_ref[...]


def reorder(blocks, index):
    shape = blocks.shape
    block = (1,) + shape[1:]
    return pl.pallas_call(
        reorder_kernel,
        grid_spec=pltpu.PrefetchScalarGridSpec(
            num_scalar_prefetch=1,
            grid=(shape[0],),
            in_specs=[pl.BlockSpec(block, lambda i, index: (index[i], 0, 0))],
            out_specs=pl.BlockSpec(block, lambda i, index: (i, 0, 0)),
        ),
        out_shape=jax.ShapeDtypeStruct(shape, blocks.dtype),
        compiler_params=pltpu.CompilerParams(vmem_limit_bytes=VMEM_LIMIT),
    )(index, blocks)


def swap_halves(values):
    lane = lax.broadcasted_iota(jnp.int32, values.shape, 1)
    return jnp.where(
        lane % RD < RD // 2, pltpu.roll(values, 2 * RD - RD // 2, 1), pltpu.roll(values, RD // 2, 1)
    )


def attend(proj, cosine, sine, id_col, id_row, lat_gain, w_exp):
    mixed = proj[:, HD : 2 * HD]
    turned = (mixed * cosine + swap_halves(mixed) * sine).astype(BF)
    q_rope, k_rope = turned[:, :RD], turned[:, RD:]
    q_main = proj[:, :HD].astype(BF)
    lat = proj[:, 2 * HD :]
    compressed = (lat * rms_scale(lat) * lat_gain).astype(BF)
    expanded = matmul(compressed, w_exp).astype(BF)
    k_main, values = expanded[:, :HD], expanded[:, HD:]
    scores = (mat_trans(q_main, k_main) + mat_trans(q_rope, k_rope)) * SCALE
    above = lax.broadcasted_iota(jnp.int32, scores.shape, 1)
    below = lax.broadcasted_iota(jnp.int32, scores.shape, 0)
    allowed = (id_col == id_row) & (above <= below)
    scores = jnp.where(allowed, scores, -1e30)
    expo = jnp.exp(scores - jnp.max(scores, axis=-1, keepdims=True))
    probs = expo / jnp.sum(expo, axis=-1, keepdims=True)
    return q_main, q_rope, k_main, k_rope, values, compressed, probs


def forward_kernel(
    x_ref, gain_ref, wp_ref, cos_ref, sin_ref, idc_ref, idr_ref, lg_ref, we_ref, wo_ref, part_ref, proj_ref, att_ref
):
    xf = x_ref[...].astype(F32)
    normed = (xf * rms_scale(xf) * gain_ref[...]).astype(BF)
    proj = matmul(normed, wp_ref[...])
    proj_ref[...] = proj
    values, probs = attend(
        proj, cos_ref[...], sin_ref[...], idc_ref[...], idr_ref[0], lg_ref[...], we_ref[...]
    )[4::2]
    attended = matmul(probs.astype(BF), values).astype(BF)
    att_ref[...] = attended
    part_ref[...] = mat_trans(attended, wo_ref[...]).astype(BF)


def backward_kernel(
    x_ref, g_ref, proj_ref, att_ref, gain_ref, wp_ref, cos_ref, sin_ref, idc_ref, idr_ref, lg_ref, we_ref, wo_ref,
    dn_ref, dl_ref, dwq_ref, dwo_ref, dwe_ref, dg_ref, acc_q, acc_o, acc_e, acc_g,
):
    step = pl.program_id(0)

    @pl.when(step == 0)
    def _():
        acc_q[...] = jnp.zeros_like(acc_q)
        acc_o[...] = jnp.zeros_like(acc_o)
        acc_e[...] = jnp.zeros_like(acc_e)
        acc_g[...] = jnp.zeros_like(acc_g)

    xf = x_ref[...].astype(F32)
    whitened = xf * rms_scale(xf)
    normed = (whitened * gain_ref[...]).astype(BF)
    grad = g_ref[...]
    cosine, sine = cos_ref[...], sin_ref[...]
    w_exp = we_ref[...]
    q_main, q_rope, k_main, k_rope, values, compressed, probs = attend(
        proj_ref[...], cosine, sine, idc_ref[...], idr_ref[0], lg_ref[...], w_exp
    )
    prob_low = probs.astype(BF)
    d_att = matmul(grad, wo_ref[...]).astype(BF)
    d_prob = mat_trans(d_att, values)
    d_values = contract(prob_low, d_att)
    d_scores = (probs * (d_prob - jnp.sum(probs * d_prob, axis=-1, keepdims=True))).astype(BF)
    d_mixed = jnp.concatenate([matmul(d_scores, k_rope), contract(d_scores, q_rope)], axis=1) * SCALE
    d_mixed = d_mixed * cosine - swap_halves(d_mixed) * sine
    d_query = jnp.concatenate([matmul(d_scores, k_main) * SCALE, d_mixed[:, :RD]], axis=1).astype(BF)
    d_expanded = jnp.concatenate([contract(d_scores, q_main) * SCALE, d_values], axis=1).astype(BF)
    dl_ref[...] = jnp.concatenate([mat_trans(d_expanded, w_exp), d_mixed[:, RD:]], axis=1).astype(BF)
    d_normed = mat_trans(d_query, wp_ref[...][:, : HD + RD])
    dn_ref[...] = d_normed.astype(BF)
    acc_g[...] += jnp.sum(d_normed * whitened, axis=0, keepdims=True)
    acc_q[...] += contract(d_query, normed)
    acc_o[...] += contract(att_ref[...], grad)
    acc_e[...] += contract(compressed, d_expanded)

    @pl.when(step == pl.num_programs(0) - 1)
    def _():
        dwq_ref[...] = acc_q[...].T.astype(BF)
        dwo_ref[...] = acc_o[...].T.astype(BF)
        dwe_ref[...] = acc_e[...].astype(BF)
        dg_ref[...] = acc_g[...]


def chunk_spec(width):
    return pl.BlockSpec((CHUNK, width), lambda i: (i, 0))


def whole_spec(array):
    return pl.BlockSpec(array.shape, lambda i: (0,) * array.ndim)


def row_spec():
    return pl.BlockSpec((1, 1, CHUNK), lambda i: (i, 0, 0))


def call(kernel, rows, args, specs, outs, out_specs, scratch=(), flops=0):
    size = sum(a.size * a.dtype.itemsize for a in list(args) + list(outs))
    return pl.pallas_call(
        kernel,
        grid=(rows // CHUNK,),
        in_specs=specs,
        out_specs=out_specs,
        out_shape=outs,
        scratch_shapes=list(scratch),
        compiler_params=pltpu.CompilerParams(vmem_limit_bytes=VMEM_LIMIT),
        cost_estimate=pl.CostEstimate(flops=flops, bytes_accessed=size, transcendentals=0),
    )(*args)


def attention_forward(x_all, gain, w_proj, tables, lat_gain, w_exp, w_out):
    rows, width = x_all.shape
    cosine, sine, id_col, id_row = tables
    args = (x_all, gain, w_proj, cosine, sine, id_col, id_row, lat_gain, w_exp, w_out)
    specs = [
        chunk_spec(width), whole_spec(gain), whole_spec(w_proj), chunk_spec(HD), chunk_spec(HD), chunk_spec(1),
        row_spec(), whole_spec(lat_gain), whole_spec(w_exp), whole_spec(w_out),
    ]
    outs = (
        jax.ShapeDtypeStruct((rows, width), BF),
        jax.ShapeDtypeStruct((rows, w_proj.shape[1]), F32),
        jax.ShapeDtypeStruct((rows, VD), BF),
    )
    out_specs = (chunk_spec(width), chunk_spec(w_proj.shape[1]), chunk_spec(VD))
    return call(forward_kernel, rows, args, specs, outs, out_specs, flops=2 * rows * width * 1024)


def attention_backward(x_all, grad, proj, attended, gain, w_proj, tables, lat_gain, w_exp, w_out):
    rows, width = x_all.shape
    cosine, sine, id_col, id_row = tables
    args = (x_all, grad, proj, attended, gain, w_proj, cosine, sine, id_col, id_row, lat_gain, w_exp, w_out)
    specs = [
        chunk_spec(width), chunk_spec(width), chunk_spec(proj.shape[1]), chunk_spec(VD), whole_spec(gain),
        whole_spec(w_proj), chunk_spec(HD), chunk_spec(HD), chunk_spec(1), row_spec(), whole_spec(lat_gain),
        whole_spec(w_exp), whole_spec(w_out),
    ]
    outs = (
        jax.ShapeDtypeStruct((rows, width), BF),
        jax.ShapeDtypeStruct((rows, LAT + RD), BF),
        jax.ShapeDtypeStruct((width, HD + RD), BF),
        jax.ShapeDtypeStruct((width, VD), BF),
        jax.ShapeDtypeStruct((LAT, HD + VD), BF),
        jax.ShapeDtypeStruct((1, width), F32),
    )
    out_specs = (chunk_spec(width), chunk_spec(LAT + RD)) + tuple(whole_spec(o) for o in outs[2:])
    scratch = (
        pltpu.VMEM((HD + RD, width), F32),
        pltpu.VMEM((VD, width), F32),
        pltpu.VMEM((LAT, HD + VD), F32),
        pltpu.VMEM((1, width), F32),
    )
    return call(backward_kernel, rows, args, specs, outs, out_specs, scratch, flops=2 * rows * width * 1024)


def enter_kernel(slots, tok_ref, g_ref, target_ref, gate_ref, sw_ref, rx_ref, rg_ref, rs_ref, act_ref, pre_ref):
    tok, grad = tok_ref[...], g_ref[...]
    slot = lax.broadcasted_iota(jnp.int32, (slots, CHUNK), 0)
    chosen = slot == target_ref[0]
    hot = chosen.astype(BF)
    share = jnp.sum(jnp.where(chosen, gate_ref[0], 0.0), axis=1, keepdims=True)
    rs_ref[...] = share
    rx_ref[...] = matmul(hot, tok).astype(BF)
    rg_ref[...] = (matmul(hot, grad) * share).astype(BF)
    third = sw_ref.shape[1] // 3
    gate_pre = matmul(tok, sw_ref[:, :third])
    up = matmul(tok, sw_ref[:, third : 2 * third])
    d_act = matmul(grad, sw_ref[:, 2 * third :])
    sigma = jax.nn.sigmoid(gate_pre)
    swish = gate_pre * sigma
    act_ref[...] = (swish * up).astype(BF)
    slope = sigma * (1.0 + gate_pre * (1.0 - sigma))
    pre_ref[:, :third] = (d_act * up * slope).astype(BF)
    pre_ref[:, third:] = (d_act * swish).astype(BF)


def enter_experts(tok, grad, target, gate, shared_w, slots):
    rows, width = tok.shape
    third = shared_w.shape[1] // 3
    per = slots * CHUNK // rows
    args = (tok, grad, target.reshape(-1, 1, CHUNK), gate.reshape(-1, 1, CHUNK), shared_w)
    specs = [chunk_spec(width), chunk_spec(width), row_spec(), row_spec(), whole_spec(shared_w)]
    outs = (
        jax.ShapeDtypeStruct((slots, width), BF),
        jax.ShapeDtypeStruct((slots, width), BF),
        jax.ShapeDtypeStruct((slots, 1), F32),
        jax.ShapeDtypeStruct((rows, third), BF),
        jax.ShapeDtypeStruct((rows, 2 * third), BF),
    )
    out_specs = (
        pl.BlockSpec((per, width), lambda i: (i, 0)),
        pl.BlockSpec((per, width), lambda i: (i, 0)),
        pl.BlockSpec((per, 1), lambda i: (i, 0)),
        chunk_spec(third),
        chunk_spec(2 * third),
    )
    flops = 2 * rows * width * (3 * third + 2 * per)
    return call(functools.partial(enter_kernel, per), rows, args, specs, outs, out_specs, flops=flops)


def leave_kernel(slots, rows_ref, target_ref, left_ref, right_ref, out_ref):
    slot = lax.broadcasted_iota(jnp.int32, (CHUNK, slots), 1)
    hot = (slot == target_ref[...]).astype(BF)
    out_ref[...] = (matmul(hot, rows_ref[...]) + mat_trans(left_ref[...], right_ref[...])).astype(BF)


def leave_experts(slot_rows, target, left, right):
    slots, width = slot_rows.shape
    rows = left.shape[0]
    per = slots * CHUNK // rows
    args = (slot_rows, target.reshape(-1, 1), left, right)
    specs = [
        pl.BlockSpec((per, width), lambda i: (i, 0)), chunk_spec(1), chunk_spec(left.shape[1]), whole_spec(right)
    ]
    outs = jax.ShapeDtypeStruct((rows, width), BF)
    flops = 2 * rows * width * (per + left.shape[1])
    return call(
        functools.partial(leave_kernel, per), rows, args, specs, (outs,), (chunk_spec(width),), flops=flops
    )[0]


def local(
    tokens, lengths, routes, gates, norm_in, latent_gain, norm_mid, w_query, w_latent, w_expand, w_output,
    shared_gate, shared_up, shared_down, expert_gate, expert_up, expert_down, cotangent,
):
    micro = lengths.shape[0]
    own_rows, width = tokens.shape
    rows = own_rows // micro
    experts = lax.axis_size("expert")
    ndp = lax.axis_size("dp")
    cap = rows * TOP * 4 // (3 * experts)
    blocks = experts * micro
    all_rows = experts * own_rows
    shard = width // (ndp * experts)
    ff_s = shared_gate.shape[1]
    ff_part = ff_s // experts
    ff_pad = -(-ff_part // 128) * 128
    ff_e = expert_gate.shape[2]
    half = width // 2
    me = lax.axis_index("expert")
    dp = lax.axis_index("dp")
    core, x, z = me % 2, (me // 2) % 2, me // 4
    place = (z, x, core)

    def turn(value):
        if ndp != 2:
            return value
        swapped = jnp.concatenate([value[..., half:], value[..., :half]], axis=-1)
        return jnp.where(dp == 1, swapped, value)

    def dp_swap(value):
        return lax.ppermute(value, "dp", [(0, 1), (1, 0)])

    def dp_gather(value):
        if ndp == 2:
            return jnp.stack([value, dp_swap(value)])
        return lax.all_gather(value, "dp", axis=0)

    def dp_scatter(value):
        if ndp == 2:
            return value[0].astype(F32) + dp_swap(value[1].astype(BF)).astype(F32)
        return lax.psum_scatter(value.astype(BF), "dp", scatter_dimension=0, tiled=False).astype(F32)

    number = jnp.arange(experts, dtype=jnp.int32)
    near_z, near_x, near_c = number % 4, (number // 4) % 2, number // 8
    row_index = ((z - near_z) % 4) * 4 + (near_x ^ x) * 2 + (near_c ^ core)
    n_z, n_x, n_c = number // 4, (number // 2) % 2, number % 2
    block_index = ((z - n_z) % 4) * 4 + (n_x ^ x) * 2 + (n_c ^ core)

    by_expert = jnp.sum(
        jnp.where(routes.T[None] == number[:, None, None], gates.T[None], 0.0), axis=1
    )
    facts = jnp.concatenate(
        [by_expert, jnp.pad(lengths.reshape(1, -1).astype(F32), ((0, 7), (0, own_rows - lengths.size)))], axis=0
    )
    facts = lax.all_gather(facts, "expert", axis=0)
    facts = jnp.take(facts, row_index, axis=0)
    gate_all = lax.dynamic_index_in_dim(facts, me, 1, keepdims=False).reshape(blocks, rows)
    lengths_all = facts[:, experts, : lengths.size].astype(jnp.int32).reshape(blocks, lengths.shape[1])

    gains = jnp.concatenate([norm_in, norm_mid, latent_gain])
    w_lat_rows = jnp.concatenate(
        [w_latent, jnp.pad(gains[None], ((0, 15), (0, w_latent.shape[1] - gains.shape[0])))], axis=0
    )
    w_lat_all = lax.all_gather(w_lat_rows, ("dp", "expert"), axis=0)
    gains = w_lat_all[:, shard].astype(F32)
    gain_in = turn(gains[:, :shard].reshape(1, width))
    gain_mid = turn(gains[:, shard : 2 * shard].reshape(1, width))
    gain_lat = gains[:, 2 * shard : 2 * shard + latent_gain.shape[0]].reshape(1, LAT)
    w_lat = w_lat_all[:, :shard].reshape(width, LAT + RD)
    w_lat_near = w_lat
    if ndp == 2:
        w_lat_near = jnp.where(dp == 1, jnp.concatenate([w_lat[half:], w_lat[:half]]), w_lat)

    lat_rows = w_expand.shape[0]
    groups = shard // lat_rows
    exp_cols = (HD + VD) // groups
    piece = jnp.concatenate(
        [
            w_query.reshape(shard, HEADS, HD + RD).transpose(1, 0, 2),
            w_expand.reshape(lat_rows, HEADS, groups, exp_cols).transpose(1, 2, 0, 3).reshape(HEADS, shard, exp_cols),
            w_output.reshape(HEADS, VD, shard).transpose(0, 2, 1),
        ],
        axis=2,
    )
    piece = reorder(exchange(piece, place), block_index)
    head_w = dp_gather(piece)
    exp_at = HD + RD
    out_at = exp_at + exp_cols
    w_exp = head_w[..., exp_at:out_at]
    if ndp == 2:
        w_exp = jnp.where(dp == 1, w_exp[::-1], w_exp)
    w_exp = w_exp.reshape(ndp * experts, groups, lat_rows, exp_cols).transpose(0, 2, 1, 3).reshape(LAT, HD + VD)
    w_out = head_w[..., out_at:].reshape(width, VD)
    w_proj = jnp.concatenate(
        [head_w[..., :exp_at].reshape(width, exp_at), w_lat_near[:, LAT:], w_lat_near[:, :LAT]], axis=1
    )

    piece = jnp.concatenate(
        [
            shared_gate.reshape(shard, experts, ff_part).transpose(1, 0, 2),
            shared_up.reshape(shard, experts, ff_part).transpose(1, 0, 2),
            shared_down.reshape(experts, ff_part, shard).transpose(0, 2, 1),
        ],
        axis=2,
    )
    piece = reorder(exchange(piece, place), block_index)
    shared_w = dp_gather(piece).reshape(width, 3 * ff_part)
    spare = jnp.zeros((width, ff_pad - ff_part), BF)
    shared_w = jnp.concatenate(
        [
            shared_w[:, :ff_part], spare, shared_w[:, ff_part : 2 * ff_part], spare, shared_w[:, 2 * ff_part :], spare
        ],
        axis=1,
    )

    gate_up = jnp.concatenate([expert_gate[0], expert_up[0]], axis=1)
    gate_up = dp_gather(gate_up).reshape(width, 2 * ff_e)
    down = dp_gather(expert_down[0])
    down = jnp.concatenate([down[i] for i in range(ndp)], axis=1)

    position, doc = layout(lengths_all, rows)
    freq = jnp.power(10000.0, -2.0 * jnp.arange(RD // 2, dtype=F32) / RD)
    theta = position.reshape(all_rows, 1) * freq
    cosine, sine = jnp.cos(theta), jnp.sin(theta)
    cosine = jnp.concatenate([cosine] * 4, axis=1)
    sine = jnp.concatenate([-sine, sine, -sine, sine], axis=1)
    ids = doc + 4 * jnp.arange(blocks, dtype=jnp.int32)[:, None]
    tables = (cosine, sine, ids.reshape(all_rows, 1), ids.reshape(-1, 1, CHUNK))
    routed = (gate_all > 0.0).astype(jnp.int32)
    in_chunk = jnp.arange(blocks, dtype=jnp.int32)[:, None] % (CHUNK // rows)
    target = jnp.where(routed > 0, in_chunk * cap + jnp.cumsum(routed, axis=1) - 1, -1)

    x_near = turn(tokens)
    x_all = gather_rows(x_near)
    part, proj, attended = attention_forward(x_all, gain_in, w_proj, tables, gain_lat, w_exp, w_out)
    xf = x_near.astype(F32)
    mid = xf + scatter_rows(part)
    scale_mid = rms_scale(mid)
    normed_mid = (mid * scale_mid * gain_mid).astype(BF)
    grad_near = turn(cotangent)

    tok_all = gather_rows(normed_mid)
    grad_all = gather_rows(grad_near.astype(BF))
    rows_x, rows_g, share, s_act, d_s_pre = enter_experts(
        tok_all, grad_all, target, gate_all, shared_w, blocks * cap
    )
    pre = matmul(rows_x, gate_up)
    e_gate, e_up = pre[:, :ff_e], pre[:, ff_e:]
    sigma = jax.nn.sigmoid(e_gate)
    e_swish = e_gate * sigma
    e_slope = sigma * (1.0 + e_gate * (1.0 - sigma))
    e_act = (e_swish * e_up).astype(BF)
    d_e_act = mat_trans(rows_g, down)
    d_pre = jnp.concatenate([(d_e_act * e_up * e_slope).astype(BF), (d_e_act * e_swish).astype(BF)], axis=1)
    d_rows = mat_trans(d_pre, gate_up).astype(BF)
    d_part = leave_experts(d_rows, target, d_s_pre, shared_w[:, : 2 * ff_pad])
    d_mid_normed = scatter_rows(d_part)
    e_out = (matmul(e_act, down) * share).astype(BF)
    out_part = leave_experts(e_out, target, s_act, shared_w[:, 2 * ff_pad :])
    out = turn(mid + scatter_rows(out_part)).astype(BF)

    if ndp == 2:
        d_down = matmul(e_act.T, rows_g[:, :half]) + dp_swap(contract(e_act, rows_g[:, half:]).astype(BF)).astype(F32)
        d_gu = contract(rows_x[:, :half], d_pre) + dp_swap(contract(rows_x[:, half:], d_pre).astype(BF)).astype(F32)
    else:
        d_down = lax.psum_scatter(
            contract(e_act, rows_g).astype(BF), "dp", scatter_dimension=1, tiled=True
        ).astype(F32)
        d_gu = lax.psum_scatter(contract(rows_x, d_pre).astype(BF), "dp", scatter_dimension=0, tiled=True).astype(F32)
    d_shared = jnp.concatenate([contract(tok_all, d_s_pre), contract(grad_all, s_act)], axis=1).astype(BF)
    d_shared = jnp.concatenate(
        [d_shared[:, i * ff_pad : i * ff_pad + ff_part] for i in range(3)], axis=1
    ).reshape(ndp, experts, shard, 3 * ff_part)
    d_shared = dp_scatter(d_shared).astype(BF)
    d_shared = reorder(exchange(d_shared, place), block_index).astype(F32)
    grad_sg, grad_su = (
        d_shared[:, :, i * ff_part : (i + 1) * ff_part].transpose(1, 0, 2).reshape(shard, ff_s) for i in range(2)
    )
    grad_sd = d_shared[:, :, 2 * ff_part :].transpose(0, 2, 1).reshape(ff_s, shard)

    d_mid_in, d_gain_mid = rms_back(d_mid_normed, mid, scale_mid, gain_mid)
    d_mid = grad_near + d_mid_in
    grad_attn = gather_rows(d_mid.astype(BF))
    d_norm_part, d_lat_part, d_wq, d_wo, d_we, d_gain_part = attention_backward(
        x_all, grad_attn, proj, attended, gain_in, w_proj, tables, gain_lat, w_exp, w_out
    )
    d_lat_own = scatter_rows(d_lat_part)
    lat_own = proj[:own_rows, 2 * HD :]
    d_lat_in, d_gain_lat = rms_back(d_lat_own[:, :LAT], lat_own, rms_scale(lat_own), gain_lat)
    d_latent = jnp.concatenate([d_lat_in, d_lat_own[:, LAT:]], axis=1).astype(BF)
    scale_in = rms_scale(xf)
    normed_own = turn((xf * scale_in * gain_in).astype(BF))
    d_wl = contract(normed_own, d_latent).astype(BF).reshape(ndp * experts, shard, LAT + RD)
    d_normed_own = mat_trans(d_latent, w_lat_near)
    d_gain_in = turn(d_gain_part[0] + jnp.sum(d_normed_own * xf * scale_in, axis=0))
    d_gains = jnp.concatenate(
        [
            d_gain_in.reshape(ndp * experts, shard),
            turn(d_gain_mid).reshape(ndp * experts, shard),
            d_gain_lat.reshape(ndp * experts, LAT // (ndp * experts)),
        ],
        axis=1,
    ).astype(BF)
    d_gains = jnp.pad(d_gains[:, None], ((0, 0), (0, 15), (0, LAT + RD - d_gains.shape[1])))
    d_wl = lax.psum_scatter(
        jnp.concatenate([d_wl, d_gains], axis=1), ("dp", "expert"), scatter_dimension=0, tiled=False
    ).astype(F32)
    d_normed = scatter_rows(d_norm_part) + d_normed_own
    d_in, _ = rms_back(d_normed, xf, scale_in, gain_in)
    d_tokens = turn(d_mid + d_in)

    d_we = d_we.reshape(ndp * experts, lat_rows, groups, exp_cols).transpose(0, 2, 1, 3)
    d_we = d_we.reshape(ndp, experts, shard, exp_cols)
    if ndp == 2:
        d_we = jnp.where(dp == 1, d_we[::-1], d_we)
    d_head = jnp.concatenate(
        [d_wq.reshape(ndp, experts, shard, HD + RD), d_we, d_wo.reshape(ndp, experts, shard, VD)], axis=3
    )
    d_head = dp_scatter(d_head).astype(BF)
    d_head = reorder(exchange(d_head, place), block_index).astype(F32)
    grad_wq = d_head[:, :, :exp_at].transpose(1, 0, 2).reshape(shard, HEADS * (HD + RD))
    grad_we = d_head[:, :, exp_at:out_at].reshape(HEADS, groups, lat_rows, exp_cols).transpose(2, 0, 1, 3)
    grad_we = grad_we.reshape(lat_rows, HEADS * (HD + VD))
    grad_wo = d_head[:, :, out_at:].transpose(0, 2, 1).reshape(HEADS * VD, shard)

    last = 2 * shard + latent_gain.shape[0]
    return (
        out,
        d_tokens,
        d_wl[shard, :shard],
        d_wl[shard, 2 * shard : last],
        d_wl[shard, shard : 2 * shard],
        grad_wq,
        d_wl[:shard],
        grad_we,
        grad_wo,
        grad_sg,
        grad_su,
        grad_sd,
        d_gu[None, :, :ff_e],
        d_gu[None, :, ff_e:],
        d_down[None],
    )


def solution(mesh):
    rows = P(("dp", "expert"), None)
    vector = P(("dp", "expert"))
    columns = P(None, ("dp", "expert"))
    by_row = P("expert", "dp", None)
    by_column = P("expert", None, "dp")
    return jax.shard_map(
        local,
        mesh=mesh,
        in_specs=(
            rows, rows, rows, rows, vector, vector, vector, rows, rows, rows, columns, rows, rows, columns, by_row,
            by_row, by_column, rows,
        ),
        out_specs=(
            rows, rows, vector, vector, vector, rows, rows, rows, columns, rows, rows, columns, by_row, by_row,
            by_column,
        ),
        check_vma=False,
    )
```

```python
import functools

import jax
import jax.numpy as jnp
from jax import lax
from jax.experimental import pallas as pl
from jax.experimental.pallas import tpu as pltpu
from jax.sharding import PartitionSpec as P

HEADS = 16
HD = 128
RD = 64
VD = 128
LAT = 512
TOP = 6
EPS = 1e-06
CHUNK = 256
SCALE = (HD + RD) ** (-0.5)
BF = jnp.bfloat16
F32 = jnp.float32
VMEM_LIMIT = 60 * 1024 * 1024
Q_COLS = 2 * (HD + RD)
O_COLS = 2 * VD
E_COLS = 128
LAT_AT = Q_COLS
ROT_AT = Q_COLS + LAT
PROJ = ROT_AT + 128
W_COLS = Q_COLS + O_COLS + E_COLS
HIDDEN_TILE = 256


def matmul(left, right):
    return jnp.dot(left, right, preferred_element_type=F32)


def mat_trans(left, right):
    return lax.dot_general(left, right, (((1,), (1,)), ((), ())), preferred_element_type=F32)


def contract(left, right):
    return lax.dot_general(left, right, (((0,), (0,)), ((), ())), preferred_element_type=F32)


def rms_scale(values):
    return lax.rsqrt(jnp.mean(values * values, axis=-1, keepdims=True) + EPS)


def rms_back(incoming, values, scale, gain):
    scaled = incoming * gain
    inner = jnp.mean(scaled * values, axis=-1, keepdims=True)
    grad_in = scale * (scaled - values * scale * scale * inner)
    grad_gain = jnp.sum(incoming * values * scale, axis=0)
    return (grad_in, grad_gain)


def layout(lengths, rows):
    ends = jnp.cumsum(lengths, axis=-1)
    place = jnp.arange(rows, dtype=jnp.int32)
    passed = (place[None, :, None] >= ends[:, None, :]).astype(jnp.int32)
    doc = jnp.sum(passed, axis=-1)
    start = jnp.sum(passed * lengths[:, None, :], axis=-1)
    return ((place[None, :] - start).astype(F32), doc)


def after(value, *others):
    return lax.optimization_barrier((value,) + others)[0]


def low(value):
    return value.astype(BF)


def wide(value):
    return value.astype(F32)


def move(value, to):
    return lax.ppermute(value, "expert", [(i, to(i)) for i in range(16)])


def z_up(value):
    return move(value, lambda i: (i + 4) % 16)


def z_down(value):
    return move(value, lambda i: (i + 12) % 16)


def z_two(value):
    return move(value, lambda i: (i + 8) % 16)


def x_swap(value):
    return move(value, lambda i: i ^ 2)


def core_swap(value):
    return move(value, lambda i: i ^ 1)


class Clock:
    def __init__(self, go):
        self.last = ()
        self.go = go
        self.queue = []

    def add(self, array):
        self.queue.append([array, 0, []])
        return self.queue[-1]

    def next_rows(self, size):
        moves, entries = [], []
        for entry in self.queue:
            array, start, _ = entry
            total = array.shape[0]
            line = array.size // total * array.dtype.itemsize
            count = round(size / line / 32) * 32
            if start == total or count < 64:
                continue
            stop = start + count
            stop = total if total - stop < 64 else stop
            entry[1] = stop
            moves.append((self.go, array[start:stop]))
            entries.append(entry)
            size -= (stop - start) * line
        return moves, entries

    def slot(self, *moves, begin=(), end=(), work=(), feed=0):
        fed, entries = self.next_rows(feed * 1e6)
        moves = fed + list(moves)
        count, late = len(moves), len(moves) + len(begin)
        args, tree = jax.tree.flatten([list(rest) for _, *rest in work])
        values = [value for _, value in moves + list(begin)]
        tied = lax.optimization_barrier(tuple(values + args) + self.last)
        moved = [go(value) for (go, _), value in zip(moves, tied)]
        begun = [go(value) for (go, _), value in zip(begin, tied[count:])]
        args = jax.tree.unflatten(tree, tied[late : late + len(args)])
        made = [job[0](*some) for job, some in zip(work, args)]
        flat, tree = jax.tree.flatten(made)
        self.last = lax.optimization_barrier(tuple(moved) + tuple(end) + tuple(flat))
        moved, ended = list(self.last[:count]), list(self.last[count : count + len(end)])
        for entry in entries:
            entry[2].append(moved.pop(0))
        return moved, begun, ended, jax.tree.unflatten(tree, self.last[count + len(end) :])


    def tie(self, value):
        return lax.optimization_barrier((value,) + self.last)[0]


def joined(entry):
    assert entry[1] == entry[0].shape[0]
    return jnp.concatenate(entry[2], axis=0)


def at(value, index, axis):
    return lax.dynamic_index_in_dim(value, index, axis, keepdims=False)


def whole_call(kernel, args, outs, scratch=(), flops=0, scalars=None):
    size = sum(a.size * a.dtype.itemsize for a in list(args) + list(outs))
    vmem = pl.BlockSpec(memory_space=pltpu.VMEM)
    specs = [vmem] * len(args)
    if scalars is not None:
        args = [scalars] + list(args)
        specs = [pl.BlockSpec(memory_space=pltpu.SMEM)] + specs
    return pl.pallas_call(
        kernel,
        in_specs=specs,
        out_specs=[vmem] * len(outs),
        out_shape=list(outs),
        scratch_shapes=list(scratch),
        compiler_params=pltpu.CompilerParams(vmem_limit_bytes=VMEM_LIMIT),
        cost_estimate=pl.CostEstimate(flops=flops, bytes_accessed=size, transcendentals=0),
    )(*args)


def shaped(shape, kind):
    return jax.ShapeDtypeStruct(shape, kind)


def reorder_kernel(count, parts, index_ref, *refs):
    for in_ref, out_ref in zip(refs[: len(refs) // 2], refs[len(refs) // 2 :]):
        pad = out_ref.shape[2] // parts
        width = in_ref.shape[2] // parts
        for i in range(count):
            value = in_ref[index_ref[i]]
            if pad == width:
                out_ref[i] = value
            else:
                spare = jnp.zeros((value.shape[0], pad - width), value.dtype)
                for part in range(parts):
                    cut = value[:, part * width : (part + 1) * width]
                    out_ref[i, :, part * pad : (part + 1) * pad] = jnp.concatenate([cut, spare], axis=1)


def shared_kernel_in(count, parts, index_ref, *refs):
    in_refs, (both_ref, down_ref) = refs[:-2], refs[-2:]
    pad = down_ref.shape[1]
    for k, in_ref in enumerate(in_refs):
        rows, columns = in_ref.shape[1], in_ref.shape[2] // parts
        spare = jnp.zeros((rows, pad - columns), in_ref.dtype)
        for i in range(count):
            value = in_ref[index_ref[i]]
            line = slice((k * count + i) * rows, (k * count + i + 1) * rows)
            for part in range(parts):
                cut = jnp.concatenate([value[:, part * columns : (part + 1) * columns], spare], axis=1)
                if part < parts - 1:
                    both_ref[line, part * pad : (part + 1) * pad] = cut
                else:
                    down_ref[line, :] = cut


def shared_weights(arrays, index, pad):
    rows = sum(a.shape[0] * a.shape[1] for a in arrays)
    outs = [shaped((rows, 2 * pad), BF), shaped((rows, pad), BF)]
    return whole_call(functools.partial(shared_kernel_in, index.shape[0], 3), arrays, outs, scalars=index)


def reorder(arrays, index, parts=1, pad=0):
    count = index.shape[0]
    outs = [shaped(a.shape[:2] + (a.shape[2] if not pad else parts * pad,), a.dtype) for a in arrays]
    return whole_call(functools.partial(reorder_kernel, count, parts), arrays, outs, scalars=index)


def swap_halves(values):
    lane = lax.broadcasted_iota(jnp.int32, values.shape, 1)
    return jnp.where(
        lane % RD < RD // 2, pltpu.roll(values, 2 * RD - RD // 2, 1), pltpu.roll(values, RD // 2, 1)
    )


def probabilities(q_main, q_rot, k_main, k_rot, allowed):
    scores = (mat_trans(q_main, k_main) + mat_trans(q_rot, k_rot)) * SCALE
    scores = jnp.where(allowed, scores, -1e30)
    expo = jnp.exp(scores - jnp.max(scores, axis=-1, keepdims=True))
    return expo / jnp.sum(expo, axis=-1, keepdims=True)


def allowed_pairs(id_col, id_row):
    shape = (id_col.shape[0], id_row.shape[1])
    key = lax.broadcasted_iota(jnp.int32, shape, 1)
    query = lax.broadcasted_iota(jnp.int32, shape, 0)
    return (id_col == id_row) & (key <= query)


def pair(refs, j):
    pieces, start = [], 0
    for ref in refs:
        low_row, high_row = max(start, CHUNK * j), min(start + ref.shape[0], CHUNK * (j + 1))
        if low_row < high_row:
            pieces.append(ref[low_row - start : high_row - start, :])
        start += ref.shape[0]
    return pieces[0] if len(pieces) == 1 else jnp.concatenate(pieces, axis=0)


def forward_kernel(ndp, layout_of, count, split, place_ref, *refs):
    x_refs, refs = refs[:8], refs[8:]
    w_refs, refs = refs[: len(layout_of)], refs[len(layout_of) :]
    wl_refs, refs = refs[:count], refs[count:]
    we_ref, gain_ref, lg_ref, cos_ref, sin_ref, idc_ref, idr_ref = refs[:7]
    near_ref, far_ref, q_ref, kr_ref, lat_ref, kv_ref, att_ref, wp_ref, wo_ref, exp_ref = refs[7:]
    other_rows = [(ref, i) for ref in wl_refs for i in range(ref.shape[0])]
    dp, z, x, core = place_ref[0], place_ref[1], place_ref[2], place_ref[3]
    block = w_refs[0].shape[1]
    shard = block // 2
    spare = jnp.zeros((shard, 128 - RD), BF)
    turn = 0
    for w_ref, (far, j, first) in zip(w_refs, layout_of):
        y = j ^ dp if ndp == 2 else j
        for k in range(w_ref.shape[0]):
            row = ((y * 4 + lax.rem(z + 4 - first - k, 4)) * 2 + (x ^ far)) * block
            row = pl.multiple_of(row, block)
            wp_ref[pl.ds(row, block), :Q_COLS] = w_ref[k, :, :Q_COLS]
            wo_ref[pl.ds(row, block), :] = w_ref[k, :, Q_COLS : Q_COLS + O_COLS]
            if not split:
                continue
            here = pl.multiple_of(row + core * shard, shard)
            there = pl.multiple_of(row + (1 - core) * shard, shard)
            for at_row, lat in ((here, w_ref[k, :, W_COLS:]), (there, other_rows[turn][0][other_rows[turn][1]])):
                wp_ref[pl.ds(at_row, shard), LAT_AT : LAT_AT + 384] = lat[:shard, :]
                wp_ref[pl.ds(at_row, shard), LAT_AT + 384 :] = lat[shard:, :256]
            turn += 1
            small = shard // 4
            for c in range(2):
                for g in range(4):
                    at_row = pl.multiple_of(row // 4 + c * small, small)
                    exp_ref[pl.ds(at_row, small), g * HD : (g + 1) * HD] = w_ref[
                        k, c * shard + g * small : c * shard + (g + 1) * small, Q_COLS + O_COLS : W_COLS
                    ]
    if not split:
        for i, (wl_ref, _) in enumerate(other_rows):
            wp_ref[i * shard : (i + 1) * shard, LAT_AT:] = jnp.concatenate([wl_ref[i, :shard, :], spare], axis=1)
        exp_ref[...] = we_ref[...]
    gain, lat_gain = gain_ref[...], lg_ref[...]
    for j in range(4):
        rows = slice(CHUNK * j, CHUNK * (j + 1))
        xf = wide(pair(x_refs, j))
        normed = low(xf * rms_scale(xf) * gain)
        proj = matmul(normed, wp_ref[...])
        cosine, sine = cos_ref[rows, :], sin_ref[rows, :]
        q_mix = proj[:, 2 * HD : Q_COLS]
        k_mix = proj[:, ROT_AT:]
        q_rot = low(q_mix * cosine + swap_halves(q_mix) * sine)
        k_rot = k_mix * cosine + swap_halves(k_mix) * sine
        k_turned = low(pltpu.roll(k_rot, RD, 1))
        k_rot = low(k_rot)
        q_main = low(proj[:, : 2 * HD])
        lat = proj[:, LAT_AT:ROT_AT]
        lat_ref[rows, :] = lat
        compressed = low(lat * rms_scale(lat) * lat_gain)
        expanded = low(matmul(compressed, exp_ref[...]))
        q_ref[rows, : 2 * HD] = q_main
        q_ref[rows, 2 * HD :] = q_rot
        kr_ref[rows, :] = k_rot
        kv_ref[rows, :] = expanded
        allowed = allowed_pairs(idc_ref[rows, :], idr_ref[j])
        attended = []
        for head, k_side in ((0, k_rot), (1, k_turned)):
            k_main = expanded[:, 2 * head * HD : (2 * head + 1) * HD]
            values = expanded[:, (2 * head + 1) * HD : (2 * head + 2) * HD]
            probs = probabilities(q_main[:, head * HD : (head + 1) * HD], q_rot, k_main, k_side, allowed)
            attended.append(low(matmul(low(probs), values)))
        attended = jnp.concatenate(attended, axis=1)
        att_ref[rows, :] = attended
        put_half(near_ref, far_ref, j, 4, low(mat_trans(attended, wo_ref[...])))


def put_half(near_ref, far_ref, j, count, value):
    ref = near_ref if j < count // 2 else far_ref
    j = j % (count // 2)
    ref[j * CHUNK : (j + 1) * CHUNK, :] = value


def attention_forward(place, x_pieces, weights, layout_of, w_lat, w_exp, gain, lat_gain, tables, split):
    own, width = x_pieces[0].shape
    rows = 8 * own
    args = list(x_pieces) + list(weights) + list(w_lat) + [w_exp, gain, lat_gain] + list(tables)
    outs = [shaped((rows // 2, width), BF)] * 2 + [
        shaped((rows, Q_COLS), BF),
        shaped((rows, 128), BF),
        shaped((rows, LAT), F32),
        shaped((rows, 4 * HD), BF),
        shaped((rows, O_COLS), BF),
        shaped((width, PROJ), BF),
        shaped((width, O_COLS), BF),
        shaped((LAT, 4 * HD), BF),
    ]
    kernel = functools.partial(forward_kernel, lax.axis_size("dp"), layout_of, len(w_lat), split)
    flops = 2 * rows * width * (PROJ + O_COLS)
    out = whole_call(kernel, args, outs, flops=flops, scalars=place)
    return out[:2], out[2:]


def backward_kernel(count, place_ref, *refs):
    x_refs, g_refs, refs = refs[:8], refs[8 : 8 + count], refs[8 + count :]
    q_ref, kr_ref, lat_ref, kv_ref, att_ref, wp_ref, wo_ref, we_ref, gain_ref, lg_ref = refs[:10]
    cos_ref, sin_ref, idc_ref, idr_ref = refs[10:14]
    dn_ref, dw_ref, dl_ref, de_ref, dg_ref, dlg_ref, acc_q, acc_o, acc_e = refs[14:]
    z, core = place_ref[1], place_ref[3]
    own = x_refs[0].shape[0]
    gain, w_exp, lat_gain = gain_ref[...], we_ref[...], lg_ref[...]

    def add(acc, value, first):
        acc[...] = value if first else acc[...] + value

    for j in range(4):
        rows = slice(CHUNK * j, CHUNK * (j + 1))
        xf = wide(pair(x_refs, j))
        whitened = xf * rms_scale(xf)
        normed = low(whitened * gain)
        lat = lat_ref[rows, :]
        lat_scale = rms_scale(lat)
        white_lat = lat * lat_scale
        grad = pair(g_refs, j)
        cosine, sine = cos_ref[rows, :], sin_ref[rows, :]
        d_att = low(matmul(grad, wo_ref[...]))
        q_rot, k_rot = q_ref[rows, 2 * HD :], kr_ref[rows, :]
        k_turned = low(pltpu.roll(wide(k_rot), RD, 1))
        allowed = allowed_pairs(idc_ref[rows, :], idr_ref[j])
        d_main, d_expanded = [], []
        dq_mix = None
        dk_mix = None
        for head, k_side in ((0, k_rot), (1, k_turned)):
            q_main = q_ref[rows, head * HD : (head + 1) * HD]
            k_main = kv_ref[rows, 2 * head * HD : (2 * head + 1) * HD]
            values = kv_ref[rows, (2 * head + 1) * HD : (2 * head + 2) * HD]
            probs = probabilities(q_main, q_rot, k_main, k_side, allowed)
            d_out = d_att[:, head * HD : (head + 1) * HD]
            d_prob = mat_trans(d_out, values)
            d_values = contract(low(probs), d_out)
            d_scores = low(probs * (d_prob - jnp.sum(probs * d_prob, axis=-1, keepdims=True)))
            d_main.append(matmul(d_scores, k_main) * SCALE)
            d_expanded += [contract(d_scores, q_main) * SCALE, d_values]
            dq_one = matmul(d_scores, k_side)
            dk_one = contract(d_scores, q_rot)
            dq_mix = dq_one if head == 0 else dq_mix + dq_one
            dk_mix = dk_one if head == 0 else dk_mix + pltpu.roll(dk_one, RD, 1)
        dq_mix = dq_mix * SCALE
        dk_mix = dk_mix * SCALE
        dq_mix = dq_mix * cosine - swap_halves(dq_mix) * sine
        dk_mix = dk_mix * cosine - swap_halves(dk_mix) * sine
        dk_mix = jnp.where(lax.broadcasted_iota(jnp.int32, dk_mix.shape, 1) < RD, dk_mix, 0.0)
        d_expanded = low(jnp.concatenate(d_expanded, axis=1))
        d_comp = mat_trans(d_expanded, w_exp)
        scaled = d_comp * lat_gain
        d_lat = lat_scale * (scaled - white_lat * jnp.mean(scaled * white_lat, axis=-1, keepdims=True))
        d_proj = low(jnp.concatenate(d_main + [dq_mix, d_lat, dk_mix], axis=1))
        d_normed = mat_trans(d_proj, wp_ref[...])
        part = low(d_normed)
        for k in range(2):
            piece = 2 * j + k
            place = lax.rem(z + 4 - piece % 4, 4) * 2 + (core ^ (piece // 4))
            dn_ref[pl.ds(pl.multiple_of(place * own, own), own), :] = part[k * own : (k + 1) * own, :]
        add(dg_ref, jnp.sum(d_normed * whitened, axis=0, keepdims=True), j == 0)
        add(dlg_ref, jnp.sum(d_comp * white_lat, axis=0, keepdims=True), j == 0)
        add(acc_q, contract(d_proj, normed), j == 0)
        add(acc_o, contract(att_ref[rows, :], grad), j == 0)
        add(acc_e, contract(low(white_lat * lat_gain), d_expanded), j == 0)
    dw_ref[:, :Q_COLS] = low(acc_q[:Q_COLS, :].T)
    dw_ref[:, Q_COLS:] = low(acc_o[...].T)
    dl_ref[...] = low(acc_q[Q_COLS:, :].T)
    de_ref[...] = low(acc_e[...])


def attention_backward(place, x_pieces, g_pieces, saved, gain, lat_gain, tables):
    own, width = x_pieces[0].shape
    q, kr, lat, kv, att, wp, wo, w_exp = saved
    args = list(x_pieces) + list(g_pieces) + [q, kr, lat, kv, att, wp, wo, w_exp, gain, lat_gain] + list(tables)
    outs = [
        shaped((8 * own, width), BF),
        shaped((width, Q_COLS + O_COLS), BF),
        shaped((width, PROJ - Q_COLS), BF),
        shaped((LAT, 4 * HD), BF),
        shaped((1, width), F32),
        shaped((1, LAT), F32),
    ]
    scratch = (
        pltpu.VMEM((PROJ, width), F32), pltpu.VMEM((O_COLS, width), F32), pltpu.VMEM((LAT, 4 * HD), F32)
    )
    flops = 2 * 8 * own * width * (2 * PROJ + 2 * O_COLS)
    kernel = functools.partial(backward_kernel, len(g_pieces))
    return whole_call(kernel, args, outs, scratch, flops=flops, scalars=place)


def enter_grad_kernel(slots, *refs):
    g_refs, (target_ref, gate_ref, rg0_ref, rg1_ref, rs_ref) = refs[:-5], refs[-5:]
    half = rg0_ref.shape[1]
    for j in range(8):
        grad = pair(g_refs, j)
        chosen = lax.broadcasted_iota(jnp.int32, (slots, CHUNK), 0) == target_ref[j]
        share = jnp.sum(jnp.where(chosen, gate_ref[j], 0.0), axis=1, keepdims=True)
        rs_ref[j * slots : (j + 1) * slots, :] = share
        value = low(matmul(low(chosen), grad) * share)
        rg0_ref[j * slots : (j + 1) * slots, :] = value[:, :half]
        rg1_ref[j * slots : (j + 1) * slots, :] = value[:, half:]


def dispatch_kernel(slots, *refs):
    t_refs, (target_ref, rx0_ref, rx1_ref) = refs[:-3], refs[-3:]
    half = rx0_ref.shape[1]
    for j in range(8):
        chosen = lax.broadcasted_iota(jnp.int32, (slots, CHUNK), 0) == target_ref[j]
        value = low(matmul(low(chosen), pair(t_refs, j)))
        rx0_ref[j * slots : (j + 1) * slots, :] = value[:, :half]
        rx1_ref[j * slots : (j + 1) * slots, :] = value[:, half:]


def hidden_shared_kernel(*refs):
    t_refs, (sgu_ref, da_ref, act_ref, pre_ref) = refs[:-4], refs[-4:]
    third = sgu_ref.shape[1] // 2
    for j in range(8):
        rows = slice(j * CHUNK, (j + 1) * CHUNK)
        both = matmul(pair(t_refs, j), sgu_ref[...])
        gate_pre, up = both[:, :third], both[:, third:]
        d_act = da_ref[rows, :]
        sigma = jax.nn.sigmoid(gate_pre)
        swish = gate_pre * sigma
        act_ref[rows, :] = low(swish * up)
        pre_ref[rows, :third] = low(d_act * up * (sigma * (1.0 + gate_pre * (1.0 - sigma))))
        pre_ref[rows, third:] = low(d_act * swish)


def enter_grad(g_pieces, target, gate, slots):
    own, width = g_pieces[0].shape
    args = list(g_pieces) + [target, gate]
    outs = [shaped((slots, width // 2), BF)] * 2 + [shaped((slots, 1), F32)]
    flops = 32 * own * width * (slots // 8)
    return whole_call(functools.partial(enter_grad_kernel, slots // 8), args, outs, flops=flops)


def dispatch(t_pieces, target, slots):
    own, width = t_pieces[0].shape
    args = list(t_pieces) + [target]
    outs = [shaped((slots, width // 2), BF)] * 2
    flops = 32 * own * width * (slots // 8)
    return whole_call(functools.partial(dispatch_kernel, slots // 8), args, outs, flops=flops)


def shared_grad_in_kernel(*refs):
    g_refs, (sd_ref, da_ref) = refs[:-2], refs[-2:]
    for j in range(8):
        da_ref[j * CHUNK : (j + 1) * CHUNK, :] = matmul(pair(g_refs, j), sd_ref[...])


def hidden_shared(t_pieces, g_pieces, s_both, s_down):
    own, width = t_pieces[0].shape
    third = s_down.shape[1]
    flops = 32 * own * width * third
    d_act = whole_call(
        shared_grad_in_kernel, list(g_pieces) + [s_down], [shaped((16 * own, third), F32)], flops=flops
    )[0]
    args = list(t_pieces) + [s_both, d_act]
    outs = [shaped((16 * own, third), BF), shaped((16 * own, 2 * third), BF)]
    return whole_call(hidden_shared_kernel, args, outs, flops=2 * flops)


def hidden_kernel(x0_ref, x1_ref, r0_ref, r1_ref, g0_ref, g1_ref, u0_ref, u1_ref, d0_ref, d1_ref, act_ref, dg_ref, du_ref):
    step = 256
    for j in range(x0_ref.shape[0] // step):
        rows = slice(j * step, (j + 1) * step)
        x0, x1 = x0_ref[rows, :], x1_ref[rows, :]
        gate = matmul(x0, g0_ref[...]) + matmul(x1, g1_ref[...])
        up = matmul(x0, u0_ref[...]) + matmul(x1, u1_ref[...])
        d_act = mat_trans(r0_ref[rows, :], d0_ref[...]) + mat_trans(r1_ref[rows, :], d1_ref[...])
        sigma = jax.nn.sigmoid(gate)
        swish = gate * sigma
        act_ref[rows, :] = low(swish * up)
        dg_ref[rows, :] = low(d_act * up * (sigma * (1.0 + gate * (1.0 - sigma))))
        du_ref[rows, :] = low(d_act * swish)


def tiled_call(kernel, steps, args, specs, outs, out_specs, scratch=(), flops=0, aliases=None):
    size = sum(a.size * a.dtype.itemsize for a in list(args) + list(outs))
    return pl.pallas_call(
        kernel,
        grid=(steps,),
        in_specs=specs,
        out_specs=out_specs,
        out_shape=outs,
        scratch_shapes=list(scratch),
        input_output_aliases=aliases or {},
        compiler_params=pltpu.CompilerParams(vmem_limit_bytes=VMEM_LIMIT),
        cost_estimate=pl.CostEstimate(flops=flops, bytes_accessed=size, transcendentals=0),
    )(*args)


def whole_spec(array):
    return pl.BlockSpec(array.shape, lambda i: (0,) * array.ndim)


def expert_hidden(rows_x, rows_g, own, other):
    slots, half = rows_x[0].shape
    hidden = own[0].shape[1]
    tile = HIDDEN_TILE
    by_column = pl.BlockSpec((half, tile), lambda i: (0, i))
    by_row = pl.BlockSpec((tile, half), lambda i: (i, 0))
    args = list(rows_x) + list(rows_g) + [own[0], other[0], own[1], other[1], own[2], other[2]]
    specs = [whole_spec(value) for value in args[:4]] + [by_column] * 4 + [by_row] * 2
    outs = [shaped((slots, hidden), BF)] * 3
    out_specs = [pl.BlockSpec((slots, tile), lambda i: (0, i))] * 3
    flops = 12 * slots * half * hidden
    return tiled_call(hidden_kernel, -(-hidden // tile), args, specs, outs, out_specs, flops=flops)


def back_kernel(per, dg_ref, du_ref, g0_ref, g1_ref, u0_ref, u1_ref, target_ref, left_ref, right_ref, near_ref, far_ref, rows_ref):
    steps = pl.num_programs(0) // 2
    own = pl.program_id(0) < steps

    @pl.when(own)
    def _():
        rows_ref[...] = low(mat_trans(dg_ref[...], g0_ref[...]) + mat_trans(du_ref[...], u0_ref[...]))

    @pl.when(jnp.logical_not(own))
    def _():
        rows_ref[...] = low(mat_trans(dg_ref[...], g1_ref[...]) + mat_trans(du_ref[...], u1_ref[...]))

    right = right_ref[...]
    for j in range(8):
        hot = low(lax.broadcasted_iota(jnp.int32, (CHUNK, per), 1) == target_ref[j * CHUNK : (j + 1) * CHUNK, :])
        out = matmul(hot, rows_ref[j * per : (j + 1) * per, :])
        put_half(near_ref, far_ref, j, 8, low(out + mat_trans(left_ref[j * CHUNK : (j + 1) * CHUNK, :], right)))


def expert_back(d_gate, d_up, own, other, target, left, right):
    slots, hidden = d_gate.shape
    rows, columns = left.shape
    width = right.shape[0]
    tile = 256
    steps = width // tile // 2
    near = pl.BlockSpec((tile, hidden), lambda i: (jnp.minimum(i, steps - 1), 0))
    far = pl.BlockSpec((tile, hidden), lambda i: (jnp.maximum(i - steps, 0), 0))
    args = [d_gate, d_up, own[0], other[0], own[1], other[1], target, left, right]
    specs = [whole_spec(d_gate), whole_spec(d_up)] + [near, far] * 2
    specs += [whole_spec(target), whole_spec(left), pl.BlockSpec((tile, columns), lambda i: (i, 0))]
    outs = [shaped((rows // 2, width), BF)] * 2
    out_specs = [pl.BlockSpec((rows // 2, tile), lambda i: (0, i))] * 2
    flops = 4 * slots * width * hidden + 2 * rows * width * (columns + slots // 8)
    return tiled_call(
        functools.partial(back_kernel, slots // 8), 2 * steps, args, specs, outs, out_specs,
        (pltpu.VMEM((slots, tile), BF),), flops=flops,
    )


def out_kernel(per, index_ref, act_ref, share_ref, d0_ref, d1_ref, target_ref, left_ref, right_ref, out_ref, rows_ref):
    steps = pl.num_programs(0) // 2
    own = pl.program_id(0) < steps

    @pl.when(own)
    def _():
        rows_ref[...] = low(matmul(act_ref[...], d0_ref[...]) * share_ref[...])

    @pl.when(jnp.logical_not(own))
    def _():
        rows_ref[...] = low(matmul(act_ref[...], d1_ref[...]) * share_ref[...])

    right = right_ref[...]
    piece = CHUNK // 2
    for j in range(8):
        hot = low(lax.broadcasted_iota(jnp.int32, (CHUNK, per), 1) == target_ref[j * CHUNK : (j + 1) * CHUNK, :])
        out = matmul(hot, rows_ref[j * per : (j + 1) * per, :])
        out = low(out + mat_trans(left_ref[j * CHUNK : (j + 1) * CHUNK, :], right))
        for k in range(2):
            row = pl.multiple_of(index_ref[2 * j + k] * piece, piece)
            out_ref[pl.ds(row, piece), :] = out[k * piece : (k + 1) * piece, :]


def expert_out(act, share, own, other, target, left, right, index):
    slots, hidden = act.shape
    rows, columns = left.shape
    width = right.shape[0]
    tile = 256
    steps = width // tile // 2
    args = [index, act, share, own[2], other[2], target, left, right]
    specs = [
        pl.BlockSpec(memory_space=pltpu.SMEM), whole_spec(act), whole_spec(share),
        pl.BlockSpec((hidden, tile), lambda i: (0, jnp.minimum(i, steps - 1))),
        pl.BlockSpec((hidden, tile), lambda i: (0, jnp.maximum(i - steps, 0))),
        whole_spec(target), whole_spec(left), pl.BlockSpec((tile, columns), lambda i: (i, 0)),
    ]
    outs = [shaped((rows, width), BF)]
    out_specs = [pl.BlockSpec((rows, tile), lambda i: (0, i))]
    flops = 2 * slots * width * hidden + 2 * rows * width * (columns + slots // 8)
    return tiled_call(
        functools.partial(out_kernel, slots // 8), 2 * steps, args, specs, outs, out_specs,
        (pltpu.VMEM((slots, tile), BF),), flops=flops,
    )[0]


def shared_kernel(part, count, *refs):
    t_refs, g_refs, (pre_ref, act_ref, out_ref, acc_t, acc_g) = refs[:count], refs[count:-5], refs[-5:]
    pad = act_ref.shape[1]
    for j in range(8):
        rows = slice(j * CHUNK, (j + 1) * CHUNK)
        by_tok = contract(pre_ref[rows, :], pair(t_refs, j))
        by_grad = contract(act_ref[rows, :], pair(g_refs, j))
        acc_t[...] = by_tok if j == 0 else acc_t[...] + by_tok
        acc_g[...] = by_grad if j == 0 else acc_g[...] + by_grad
    parts = [acc_t[:part, :], acc_t[pad : pad + part, :], acc_g[:part, :]]
    spare = -3 * part % 128
    if spare:
        parts.append(jnp.zeros((spare, acc_t.shape[1]), F32))
    out_ref[...] = low(jnp.concatenate(parts, axis=0).T[:, : 3 * part])


def shared_gradient(t_pieces, g_pieces, pre, act, part):
    own, width = t_pieces[0].shape
    args = list(t_pieces) + list(g_pieces) + [pre, act]
    outs = [shaped((width, 3 * part), BF)]
    scratch = (pltpu.VMEM((pre.shape[1], width), F32), pltpu.VMEM((act.shape[1], width), F32))
    flops = 32 * own * width * (pre.shape[1] + act.shape[1])
    return whole_call(functools.partial(shared_kernel, part, len(t_pieces)), args, outs, scratch, flops=flops)[0]


def local(
    tokens, lengths, routes, gates, norm_in, latent_gain, norm_mid, w_query, w_latent, w_expand, w_output,
    shared_gate, shared_up, shared_down, expert_gate, expert_up, expert_down, cotangent,
):
    micro = lengths.shape[0]
    own_rows, width = tokens.shape
    rows = own_rows // micro
    experts = lax.axis_size("expert")
    ndp = lax.axis_size("dp")
    two = ndp == 2
    cap = rows * TOP * 4 // (3 * experts)
    blocks = experts * micro
    all_rows = experts * own_rows
    devices = ndp * experts
    shard = width // devices
    lat_rows = w_expand.shape[0]
    lat_cols = w_latent.shape[1]
    ff_s = shared_gate.shape[1]
    ff_part = ff_s // experts
    ff_pad = -(-ff_part // 128) * 128
    half = width // 2
    me = lax.axis_index("expert")
    dp = lax.axis_index("dp")
    core, x, z = me % 2, (me // 2) % 2, me // 4
    scalars = jnp.stack([dp, z, x, core]).astype(jnp.int32)

    def turn(value):
        if not two:
            return value
        swapped = jnp.concatenate([value[..., half:], value[..., :half]], axis=-1)
        return jnp.where(dp == 1, swapped, value)

    def dp_swap(value):
        return lax.ppermute(value, "dp", [(0, 1), (1, 0)])

    clock = Clock(dp_swap)

    def lane(value):
        return [(dp_swap, value)] if two else []

    def dp_gather(value, axis):
        return lax.all_gather(value, "dp", axis=axis, tiled=True)

    def dp_scatter(value, axis=0):
        return lax.psum_scatter(value, "dp", scatter_dimension=axis, tiled=True)

    def cut(value, k):
        return value[k * own_rows : (k + 1) * own_rows]

    number = jnp.arange(experts, dtype=jnp.int32)
    near_z, near_x, near_c = number % 4, (number // 4) % 2, number // 8
    row_index = ((z + 4 - near_z) % 4) * 4 + (near_x ^ x) * 2 + (near_c ^ core)
    few_index = jnp.concatenate([row_index[:4], row_index[8:12]])
    n_z, n_x, n_c = number // 4, (number // 2) % 2, number % 2
    block_index = ((z + 4 - n_z) % 4) * 4 + (n_x ^ x) * 2 + (n_c ^ core)

    pairs = HEADS // 2
    groups = shard // lat_rows
    piece = w_query.reshape(shard, pairs, 2, HD + RD).transpose(1, 0, 2, 3)
    piece = jnp.concatenate(
        [
            piece[..., :HD].reshape(pairs, shard, 2 * HD),
            piece[..., HD:].reshape(pairs, shard, 2 * RD),
            w_output.reshape(pairs, O_COLS, shard).transpose(0, 2, 1),
            w_expand.reshape(lat_rows, pairs, groups, E_COLS).transpose(1, 2, 0, 3).reshape(pairs, shard, E_COLS),
        ],
        axis=2,
    )
    piece = piece.reshape(4, 2, shard, W_COLS)
    kept, away = at(piece, core, 1), at(piece, 1 - core, 1)

    by_expert = jnp.sum(jnp.where(routes.T[None] == number[:, None, None], gates.T[None], 0.0), axis=1)
    gate_high = low(by_expert)
    gate_low = low(by_expert - wide(gate_high))

    def as_row(value):
        return jnp.pad(value.reshape(1, -1), ((0, 0), (0, own_rows - value.size)))

    small = [as_row(norm_in), as_row(norm_mid), as_row(latent_gain), as_row(low(lengths)), gate_high, gate_low]
    small = jnp.concatenate(small, axis=0)
    small_rows = 48
    small = jnp.pad(small, ((0, small_rows - small.shape[0]), (0, 0)))

    s_piece = jnp.concatenate(
        [
            shared_gate.reshape(shard, experts, ff_part).transpose(1, 0, 2),
            shared_up.reshape(shard, experts, ff_part).transpose(1, 0, 2),
            shared_down.reshape(experts, ff_part, shard).transpose(0, 2, 1),
        ],
        axis=2,
    ).reshape(4, 2, 2, shard, 3 * ff_part)
    own_expert = (expert_gate[0], expert_up[0], expert_down[0])
    x0 = tokens
    g0 = low(turn(cotangent))

    if two:
        fetched = [clock.add(value) for value in (own_expert[2], own_expert[0], own_expert[1])]
        wide_lat = jnp.pad(w_latent, ((0, 0), (0, 640 - lat_cols)))
        low_rows = jnp.pad(small, ((0, shard - small_rows), (0, 0)))
        lat = jnp.concatenate([wide_lat[:, :384], jnp.concatenate([wide_lat[:, 384:], low_rows], axis=1)], axis=0)
    else:
        lat = small
    moved, _, _, _ = clock.slot((core_swap, away), (z_two, lat), (z_up, lat), (z_down, lat), (z_up, x0))
    x1 = moved[4]
    lats = jnp.stack([lat, moved[2], moved[1], moved[3]])
    facts = lats[:, shard : shard + small_rows, 256:] if two else lats
    w_own = jnp.where(
        core == 0, jnp.concatenate([kept, moved[0]], axis=1), jnp.concatenate([moved[0], kept], axis=1)
    )
    moved, _, _, _ = clock.slot(
        (z_two, at(w_own, (z + 2) % 4, 0)),
        (z_up, at(w_own, (z + 1) % 4, 0)),
        (z_down, at(w_own, (z + 3) % 4, 0)),
        (core_swap, facts),
        feed=0.75,
    )
    w_own = jnp.stack([at(w_own, z, 0), moved[1], moved[0], moved[2]])
    facts_few = jnp.concatenate([facts, moved[3]])
    if two:
        w_own = jnp.concatenate([w_own, lats], axis=2)
    s_kept, s_away = at(s_piece, core, 2), at(s_piece, 1 - core, 2)

    def tables_of(facts):
        lengths_few = facts[:, 3, : lengths.size].astype(jnp.int32).reshape(8 * micro, lengths.shape[1])
        position, doc = layout(lengths_few, rows)
        freq = jnp.power(10000.0, -2.0 * jnp.arange(RD // 2, dtype=F32) / RD)
        theta = position.reshape(-1, 1) * freq
        cosine, sine = jnp.cos(theta), jnp.sin(theta)
        cosine = jnp.concatenate([cosine] * 4, axis=1)
        sine = jnp.concatenate([-sine, sine, -sine, sine], axis=1)
        ids = doc + 4 * jnp.arange(8 * micro, dtype=jnp.int32)[:, None]
        return cosine, sine, ids.reshape(-1, 1), ids.reshape(-1, 1, CHUNK)

    moved, _, _, made = clock.slot(
        (x_swap, w_own), (z_up, x1), (z_up, g0), *lane(w_own), (core_swap, x0), work=[(tables_of, facts_few)]
    )
    tables = made[0]
    w_x, x2, g1 = moved[:3]
    cx0 = moved[-1]
    if two:
        w_y = moved[3]
        lat_near = jnp.concatenate([lats, w_x[..., W_COLS:], w_y[..., W_COLS:]])
        moved, _, _, _ = clock.slot(
            (x_swap, w_y[:2]), (dp_swap, w_x[2:]), (z_up, x2), (core_swap, x1), (core_swap, lat_near)
        )
        w_far, x3, cx1, lat_other = moved[:2], *moved[2:]
        lat_far = jnp.concatenate([w_far[0][..., W_COLS:], w_far[1][..., W_COLS:]])
        device = jnp.arange(devices, dtype=jnp.int32)
        place = (device // 2 % 2 ^ x) + 2 * (device // 16 ^ dp)
        place = (device % 2 ^ core) * 16 + place * 4 + (z + 4 - device // 4 % 4) % 4
        moved, _, _, _ = clock.slot((core_swap, lat_far), (core_swap, x3), (core_swap, x2), feed=0.35)
        cx3, cx2 = moved[1:]
        weights = [w_own, w_x, w_y] + w_far
        layout_of = ((0, 0, 0), (1, 0, 0), (0, 1, 0), (1, 1, 0), (1, 1, 2))
        w_lat = [lat_other, moved[0]]
        every = [lat_near, lat_far, lat_other, moved[0]]
        facts = reorder([jnp.concatenate([part[:, shard : shard + 16, 256:] for part in every])], place)[0]
        gain_in = wide(facts[:, 0, :shard]).reshape(1, width)
        gain_lat = wide(facts[:, 2, :lat_rows]).reshape(1, LAT)
        w_exp = gain_lat
    else:
        x3 = z_up(x2)
        cx1, cx2, cx3 = core_swap(x1), core_swap(x2), core_swap(x3)
        near, far = dp_gather(w_own[None], 0), dp_gather(w_x[None], 0)
        weights = [near[i] for i in range(ndp)] + [far[i] for i in range(ndp)]
        layout_of = tuple((side, j, 0) for side in range(2) for j in range(ndp))
        w_lat = lax.all_gather(w_latent, ("dp", "expert"), axis=0)
        w_lat = [w_lat[i][None] for i in range(devices)]
        facts = lax.all_gather(small, ("dp", "expert"), axis=0)
        w_exp = jnp.concatenate([value[..., Q_COLS + O_COLS :] for value in weights], axis=0)
        w_exp = w_exp.reshape(2, ndp, 4, 2 * shard, E_COLS).transpose(1, 2, 0, 3, 4)
        w_exp = w_exp.reshape(devices // 2, -1, E_COLS)
        chips = jnp.arange(devices // 2, dtype=jnp.int32)
        chip_index = chips // 8 * 8 + ((z + 4 - chips // 2 % 4) % 4) * 2 + (chips % 2 ^ x)
        w_exp = reorder([w_exp], chip_index)[0]
        w_exp = w_exp.reshape(devices, groups, lat_rows, E_COLS).transpose(0, 2, 1, 3).reshape(LAT, groups * E_COLS)
        gain_in = wide(facts[:, 0, :shard]).reshape(1, width)
        gain_lat = wide(facts[:, 2, :lat_rows]).reshape(1, LAT)
        every = None

    def facts_of(facts, every):
        if two:
            facts = reorder([jnp.concatenate([part[:, shard : shard + small_rows, 256:] for part in every])], place)[0]
        return facts, wide(facts[:, 1, :shard]).reshape(1, width)

    def routing_of(facts):
        group = wide(lax.dynamic_slice_in_dim(facts, dp * experts, experts, 0))
        gate_all = group[:, 4 : 4 + 2 * experts].reshape(experts, 2, experts, own_rows)
        gate_all = jnp.take(at(gate_all, me, 2).sum(axis=1), row_index, axis=0).reshape(blocks, rows)
        routed = (gate_all > 0.0).astype(jnp.int32)
        in_chunk = jnp.arange(blocks, dtype=jnp.int32)[:, None] % (CHUNK // rows)
        target = jnp.where(routed > 0, in_chunk * cap + jnp.cumsum(routed, axis=1) - 1, -1)
        return target.reshape(all_rows, 1), target.reshape(-1, 1, CHUNK), gate_all.reshape(-1, 1, CHUNK)

    def small_facts(facts, every):
        facts, gain_mid = facts_of(facts, every)
        return routing_of(facts) + (gain_mid,)

    x_pieces = [x0, x1, x2, x3, cx0, cx1, cx2, cx3]
    moved, _, _, made = clock.slot(
        (x_swap, g0), (z_up, g1), (core_swap, s_away),
        feed=0.9,
        work=[
            (
                lambda *a: attention_forward(*a[:3], layout_of, *a[3:], split=two),
                scalars, x_pieces, weights, w_lat, w_exp, gain_in, gain_lat, tables,
            )
        ],
    )
    gx0, g2 = moved[:2]
    s_piece = jnp.stack([s_kept, moved[2]], axis=2)
    (part_near, part_far), saved = made[0]

    s_kept, s_away = at(s_piece, x, 1), at(s_piece, 1 - x, 1)
    moved, _, _, _ = clock.slot((core_swap, part_far), (z_up, g2), (x_swap, g1), feed=0.6)
    g3, gx1 = moved[1:]
    g_near = jnp.concatenate([g0, g1, g2, g3])
    terms = [wide(cut(part_near, k)) + wide(cut(moved[0], k)) for k in range(4)]
    moved, _, _, made = clock.slot(
        (z_down, low(terms[3])), (x_swap, g2), work=[(small_facts, facts, every)], feed=0.67
    )
    gx2 = moved[1]
    target_col, target_row, gate_row, gain_mid = made[0]
    moved, _, _, _ = clock.slot(
        (z_down, low(terms[2] + wide(moved[0]))), (x_swap, g3), (core_swap, g_near), feed=0.67
    )
    gx3, cg_near = moved[1:]
    moved, _, _, _ = clock.slot((z_down, low(terms[1] + wide(moved[0]))), (x_swap, s_away), feed=0.67)
    s_piece = jnp.stack([s_kept, moved[1]], axis=1)
    xf = wide(tokens)
    mid = xf + terms[0] + wide(moved[0])
    scale_mid = rms_scale(mid)
    t0 = turn(low(mid * scale_mid * gain_mid))

    slots = blocks * cap
    g_far = jnp.concatenate([gx0, gx1, gx2, gx3])
    moved, _, _, _ = clock.slot((z_up, t0), (x_swap, t0), feed=0.67)
    t1, tx0 = moved
    moved, _, _, _ = clock.slot((z_up, t1), (x_swap, t1), (core_swap, g_far), feed=0.67)
    t2, tx1, cg_far = moved
    g_pieces = [g0, g1, g2, g3, gx0, gx1, gx2, gx3, cg_near, cg_far]
    moved, _, _, made = clock.slot(
        (z_up, t2), (x_swap, t2),
        feed=0.67,
        work=[(functools.partial(enter_grad, slots=slots), g_pieces, target_row, gate_row)],
    )
    t3, tx2 = moved
    *rows_g, share = made[0]
    t_near = jnp.concatenate([t0, t1, t2, t3])
    moved, s_begun, _, _ = clock.slot(
        (x_swap, t3), (core_swap, t_near), begin=[(z_two, at(s_piece, (z + 2) % 4, 0))], feed=0.67
    )
    tx3, ct_near = moved
    t_far = jnp.concatenate([tx0, tx1, tx2, tx3])
    moved, more, _, _ = clock.slot(
        (core_swap, t_far),
        begin=[(z_up, at(s_piece, (z + 1) % 4, 0)), (z_down, at(s_piece, (z + 3) % 4, 0))],
        feed=0.67,
    )
    t_pieces = [t0, t1, t2, t3, tx0, tx1, tx2, tx3, ct_near, moved[0]]

    _, _, ended, made = clock.slot(
        end=more + s_begun, work=[(functools.partial(dispatch, slots=slots), t_pieces, target_row)], feed=2.0
    )
    rows_x = made[0]
    s_piece = jnp.stack([at(s_piece, z, 0), ended[0], ended[2], ended[1]]).reshape(experts, shard, 3 * ff_part)
    if two:
        own, other = own_expert, [joined(fetched[i]) for i in (1, 2, 0)]
    else:
        full = [dp_gather(own_expert[0], 0), dp_gather(own_expert[1], 0), dp_gather(own_expert[2], 1)]
        own = [full[0][:half], full[1][:half], full[2][:, :half]]
        other = [full[0][half:], full[1][half:], full[2][:, half:]]
    s_got, _, _, made = clock.slot(*lane(s_piece), work=[(expert_hidden, rows_x, rows_g, own, other)])
    e_act, d_gate, d_up = made[0]
    s_pieces = [s_piece, s_got[0]] if two else jnp.split(dp_gather(s_piece[None], 0), ndp)
    s_pieces = [value.reshape(s_piece.shape) for value in s_pieces]
    _, _, _, made = clock.slot(work=[(contract, e_act, rows_g[1])])
    if two:
        sent = [clock.add(low(made[0]))]

    _, _, _, made = clock.slot(
        feed=0.2, work=[(lambda *a: shared_weights(a, block_index, ff_pad), *s_pieces)]
    )
    s_both, s_down = made[0]
    _, _, _, made = clock.slot(work=[(hidden_shared, t_pieces, g_pieces, s_both, s_down)], feed=0.8)
    s_act, d_s_pre = made[0]
    _, _, _, made = clock.slot(
        work=[(expert_back, d_gate, d_up, own, other, target_col, d_s_pre, s_both)], feed=1.3
    )
    near, far = made[0]
    quads = 4 * own_rows
    moved, _, _, made = clock.slot((core_swap, far[quads:]), work=[(contract, rows_x[1], d_gate)], feed=0.25)
    if two:
        sent.append(clock.add(low(made[0])))
    away = [low(wide(cut(near[quads:], k)) + wide(cut(moved[0], k))) for k in range(4)]
    moved, _, _, made = clock.slot(
        (x_swap, away[3]), (core_swap, far[:quads]), work=[(contract, rows_x[1], d_up)], feed=0.65
    )
    if two:
        sent.append(clock.add(low(made[0])))
    home = [wide(cut(near, k)) + wide(cut(moved[1], k)) for k in range(4)]
    moved, _, _, made = clock.slot(
        (x_swap, away[2]), (z_down, low(home[3] + wide(moved[0]))),
        feed=0.85,
        work=[(expert_out, e_act, share, own, other, target_col, s_act, s_down, row_index)],
    )
    out_part = made[0]
    moved, _, _, made = clock.slot(
        (x_swap, away[1]), (z_down, low(home[2] + wide(moved[0]) + wide(moved[1]))),
        work=[(contract, e_act, rows_g[0])], feed=0.65,
    )
    d_down_home = made[0]
    moved, _, _, made = clock.slot(
        (x_swap, away[0]), (z_down, low(home[1] + wide(moved[0]) + wide(moved[1]))),
        work=[(contract, rows_x[0], d_gate)], feed=0.65,
    )
    d_gate_home = made[0]
    out_sum = lax.psum_scatter(clock.tie(out_part), "expert", scatter_dimension=0, tiled=True)
    d_mid_normed = turn(home[0] + wide(moved[0]) + wide(moved[1]))
    d_mid_in, d_gain_mid = rms_back(d_mid_normed, mid, scale_mid, gain_mid)
    d_mid = cotangent + d_mid_in

    a0 = low(d_mid)
    moved, _, _, made = clock.slot(
        (z_up, a0),
        feed=0.7,
        work=[(functools.partial(shared_gradient, part=ff_part), t_pieces, g_pieces, d_s_pre, s_act)],
    )
    a1 = moved[0]
    d_shared = made[0].reshape(ndp, experts, shard, 3 * ff_part)
    part = experts // 2
    moved, _, _, made = clock.slot((z_up, a1), *lane(d_shared[1, :part]), work=[(contract, rows_x[0], d_up)])
    a2, s_got = moved[0], moved[1:]
    d_up_home = made[0]
    moved, _, _, _ = clock.slot((z_up, a2), *lane(d_shared[1, part:]))
    a3 = moved[0]
    if two:
        d_shared = low(wide(d_shared[0]) + wide(jnp.concatenate([s_got[0], moved[1]])))
    else:
        d_shared = dp_scatter(d_shared)[0]
    d_shared = d_shared.reshape(4, 2, 2, shard, 3 * ff_part)
    a_near = jnp.concatenate([a0, a1, a2, a3])
    moved, _, _, _ = clock.slot((core_swap, a_near), feed=0.25)
    a_pieces = [a0, a1, a2, a3, moved[0]]
    moved, _, _, made = clock.slot(
        (z_two, at(d_shared, (z + 2) % 4, 0)), (z_up, at(d_shared, (z + 1) % 4, 0)),
        (z_down, at(d_shared, (z + 3) % 4, 0)),
        feed=1.0,
        work=[(attention_backward, scalars, x_pieces, a_pieces, saved, gain_in, gain_lat, tables)],
    )
    d_shared = jnp.stack([at(d_shared, z, 0), moved[1], moved[0], moved[2]])
    d_norm, d_head, d_wl, d_we, d_gain_in, d_gain_lat = made[0]
    same_x = [[i for i in range(experts) if i // 2 % 2 == side] for side in range(2)]
    d_normed = lax.psum_scatter(d_norm, "expert", scatter_dimension=0, axis_index_groups=same_x, tiled=True)

    d_we = d_we.reshape(devices, lat_rows, groups, E_COLS).transpose(0, 2, 1, 3).reshape(width, E_COLS)
    d_head = jnp.concatenate([d_head, d_we], axis=1).reshape(ndp, 4, 2, 2 * shard, W_COLS)
    gains = [d_gain_in.reshape(width, 1), d_gain_mid.reshape(width, 1)]
    gains.append(jnp.pad(d_gain_lat.reshape(devices, lat_rows), ((0, 0), (0, shard - lat_rows))).reshape(width, 1))
    d_wl = jnp.concatenate([d_wl[:, :lat_cols]] + [low(value) for value in gains], axis=1)
    d_wl = jnp.pad(d_wl, ((0, 0), (0, -d_wl.shape[1] % 128))).reshape(ndp, 4, 2, 2, shard, -1)
    s_kept, s_away = at(d_shared, x, 1), at(d_shared, 1 - x, 1)
    if two:
        first, second = d_head[:, :2], d_head[:, 2:]
        moved, _, _, _ = clock.slot(
            (x_swap, at(first, 1 - x, 2)), (dp_swap, at(second, 1 - dp, 0)), (core_swap, at(d_wl, 1 - core, 3))
        )
        first = wide(at(first, x, 2)) + wide(moved[0])
        second = wide(at(second, dp, 0)) + wide(moved[1])
        d_wl = wide(at(d_wl, core, 3)) + wide(moved[2])
        moved, _, _, _ = clock.slot(
            (dp_swap, low(at(first, 1 - dp, 0))), (x_swap, low(at(second, 1 - x, 1))),
            (x_swap, low(at(d_wl, 1 - x, 2))), feed=0.6,
        )
        first = at(first, dp, 0) + wide(moved[0])
        second = at(second, x, 1) + wide(moved[1])
        d_wl = at(d_wl, x, 2) + wide(moved[2])
        d_head = low(jnp.concatenate([first, second]))
    else:
        d_head = wide(at(d_head, x, 2)) + wide(x_swap(at(d_head, 1 - x, 2)))
        d_head = dp_scatter(low(d_head))[0]
        d_wl = wide(at(d_wl, core, 3)) + wide(core_swap(at(d_wl, 1 - core, 3)))
        d_wl = at(d_wl, x, 2) + wide(x_swap(low(at(d_wl, 1 - x, 2))))
    moved, _, ended, _ = clock.slot(
        (z_two, at(d_head, (z + 2) % 4, 0)), (z_down, at(d_head, (z + 3) % 4, 0)),
        (z_up, at(d_head, (z + 1) % 4, 0)), (x_swap, s_away), *(lane(low(at(d_wl, 1 - dp, 0))) if two else []),
        end=[out_sum], feed=2.0,
    )
    d_head = jnp.stack([at(d_head, z, 0), moved[1], moved[0], moved[2]]).reshape(4, 2, shard, W_COLS)
    d_shared = jnp.stack([s_kept, moved[3]], axis=1)
    d_wl = at(d_wl, dp, 0) + wide(moved[4]) if two else wide(dp_scatter(low(d_wl))[0])
    out = low(mid + turn(wide(ended[0])))
    s_kept, s_away = at(d_shared, core, 2), at(d_shared, 1 - core, 2)
    moved, _, ended, _ = clock.slot(
        (core_swap, at(d_head, 1 - core, 1)), (z_two, low(at(d_wl, (z + 2) % 4, 0))),
        (z_down, low(at(d_wl, (z + 3) % 4, 0))), (z_up, low(at(d_wl, (z + 1) % 4, 0))), (core_swap, s_away),
        end=[d_normed],
    )
    d_head = jnp.stack([at(d_head, core, 1), moved[0]], axis=1).reshape(pairs, shard, W_COLS)
    d_wl = at(d_wl, z, 0) + wide(moved[1]) + wide(moved[2]) + wide(moved[3])
    d_shared = jnp.stack([s_kept, moved[4]], axis=2).reshape(experts, shard, 3 * ff_part)
    d_normed = wide(ended[0])

    if two:
        got = [wide(joined(entry)) for entry in sent]
        d_expert = [d_gate_home + got[1], d_up_home + got[2], d_down_home + got[0]]
    else:
        d_expert = [
            wide(dp_scatter(low(jnp.concatenate([contract(value, d) for value in rows_x]))))
            for d in (d_gate, d_up)
        ]
        d_expert.append(wide(dp_scatter(low(jnp.concatenate([contract(e_act, value) for value in rows_g], axis=1)), 1)))
    d_in, _ = rms_back(d_normed, xf, rms_scale(xf), gain_in)
    d_tokens = d_mid + d_in
    d_shared = wide(reorder([d_shared], block_index)[0])
    grad_sg, grad_su = (
        d_shared[:, :, i * ff_part : (i + 1) * ff_part].transpose(1, 0, 2).reshape(shard, ff_s) for i in range(2)
    )
    grad_sd = d_shared[:, :, 2 * ff_part :].transpose(0, 2, 1).reshape(ff_s, shard)
    pair_number = jnp.arange(pairs, dtype=jnp.int32)
    pair_index = ((pair_number // 2 + 4 - z) % 4) * 2 + (pair_number % 2 ^ core)
    d_head = wide(reorder([d_head], pair_index)[0])
    grad_wq = jnp.concatenate(
        [
            d_head[..., : 2 * HD].reshape(pairs, shard, 2, HD),
            d_head[..., 2 * HD : Q_COLS].reshape(pairs, shard, 2, RD),
        ],
        axis=3,
    )
    grad_wq = grad_wq.transpose(1, 0, 2, 3).reshape(shard, HEADS * (HD + RD))
    grad_wo = d_head[..., Q_COLS : Q_COLS + O_COLS].transpose(0, 2, 1).reshape(HEADS * VD, shard)
    grad_we = d_head[..., Q_COLS + O_COLS :].reshape(pairs, groups, lat_rows, E_COLS).transpose(2, 0, 1, 3)
    grad_we = grad_we.reshape(lat_rows, HEADS * (HD + VD))
    return (
        out,
        d_tokens,
        d_wl[:, lat_cols],
        d_wl[:lat_rows, lat_cols + 2],
        d_wl[:, lat_cols + 1],
        grad_wq,
        d_wl[:, :lat_cols],
        grad_we,
        grad_wo,
        grad_sg,
        grad_su,
        grad_sd,
        d_expert[0][None],
        d_expert[1][None],
        d_expert[2][None],
    )


def solution(mesh):
    rows = P(("dp", "expert"), None)
    vector = P(("dp", "expert"))
    columns = P(None, ("dp", "expert"))
    by_row = P("expert", "dp", None)
    by_column = P("expert", None, "dp")
    return jax.shard_map(
        local,
        mesh=mesh,
        in_specs=(
            rows, rows, rows, rows, vector, vector, vector, rows, rows, rows, columns, rows, rows, columns, by_row,
            by_row, by_column, rows,
        ),
        out_specs=(
            rows, rows, vector, vector, vector, rows, rows, rows, columns, rows, rows, columns, by_row, by_row,
            by_column,
        ),
        check_vma=False,
    )
```

```python
import functools

import jax
import jax.numpy as jnp
import ml_dtypes
import numpy as np
from jax import lax
from jax.experimental import pallas as pl
from jax.experimental.pallas import tpu as pltpu
from jax.sharding import PartitionSpec as P

HEADS = 16
HD = 128
RD = 64
VD = 128
LAT = 512
TOP = 6
EPS = 1e-06
CHUNK = 256
SCALE = (HD + RD) ** (-0.5)
BF = jnp.bfloat16
F32 = jnp.float32
VMEM_LIMIT = 60 * 1024 * 1024
Q_COLS = 2 * (HD + RD)
O_COLS = 2 * VD
E_COLS = 128
LAT_AT = Q_COLS
ROT_AT = Q_COLS + LAT
PROJ = ROT_AT + 128
W_COLS = Q_COLS + O_COLS + E_COLS
HIDDEN_TILE = 256


def matmul(left, right):
    return jnp.dot(left, right, preferred_element_type=F32)


def mat_trans(left, right):
    return lax.dot_general(left, right, (((1,), (1,)), ((), ())), preferred_element_type=F32)


def contract(left, right):
    return lax.dot_general(left, right, (((0,), (0,)), ((), ())), preferred_element_type=F32)


def rms_scale(values):
    return lax.rsqrt(jnp.mean(values * values, axis=-1, keepdims=True) + EPS)


def rms_back(incoming, values, scale, gain):
    scaled = incoming * gain
    inner = jnp.mean(scaled * values, axis=-1, keepdims=True)
    grad_in = scale * (scaled - values * scale * scale * inner)
    grad_gain = jnp.sum(incoming * values * scale, axis=0)
    return (grad_in, grad_gain)


def low(value):
    return value.astype(BF)


def wide(value):
    return value.astype(F32)


def move(value, to):
    return lax.ppermute(value, "expert", [(i, to(i)) for i in range(16)])


def z_up(value):
    return move(value, lambda i: (i + 4) % 16)


def z_down(value):
    return move(value, lambda i: (i + 12) % 16)


def z_two(value):
    return move(value, lambda i: (i + 8) % 16)


def x_swap(value):
    return move(value, lambda i: i ^ 2)


def core_swap(value):
    return move(value, lambda i: i ^ 1)


class Clock:
    def __init__(self, go):
        self.last = ()
        self.go = go
        self.queue = []

    def add(self, array):
        self.queue.append([array, 0, []])
        return self.queue[-1]

    def next_rows(self, size):
        moves, entries = [], []
        for entry in self.queue:
            array, start, _ = entry
            total = array.shape[0]
            line = array.size // total * array.dtype.itemsize
            count = round(size / line / 32) * 32
            if start == total or count < 64:
                continue
            stop = start + count
            stop = total if total - stop < 64 else stop
            entry[1] = stop
            moves.append((self.go, array[start:stop]))
            entries.append(entry)
            size -= (stop - start) * line
        return moves, entries

    def slot(self, *moves, begin=(), end=(), work=(), feed=0):
        fed, entries = self.next_rows(feed * 1e6)
        moves = fed + list(moves)
        count, late = len(moves), len(moves) + len(begin)
        args, tree = jax.tree.flatten([list(rest) for _, *rest in work])
        values = [value for _, value in moves + list(begin)]
        tied = lax.optimization_barrier(tuple(values + args) + self.last)
        moved = [go(value) for (go, _), value in zip(moves, tied)]
        begun = [go(value) for (go, _), value in zip(begin, tied[count:])]
        args = jax.tree.unflatten(tree, tied[late : late + len(args)])
        made = [job[0](*some) for job, some in zip(work, args)]
        flat, tree = jax.tree.flatten(made)
        self.last = lax.optimization_barrier(tuple(moved) + tuple(end) + tuple(flat))
        moved, ended = list(self.last[:count]), list(self.last[count : count + len(end)])
        for entry in entries:
            entry[2].append(moved.pop(0))
        return moved, begun, ended, jax.tree.unflatten(tree, self.last[count + len(end) :])


    def tie(self, value):
        return lax.optimization_barrier((value,) + self.last)[0]


def joined(entry):
    assert entry[1] == entry[0].shape[0]
    return jnp.concatenate(entry[2], axis=0)


def at(value, index, axis):
    return lax.dynamic_index_in_dim(value, index, axis, keepdims=False)


def whole_call(kernel, args, outs, scratch=(), flops=0, scalars=None):
    size = sum(a.size * a.dtype.itemsize for a in list(args) + list(outs))
    vmem = pl.BlockSpec(memory_space=pltpu.VMEM)
    specs = [vmem] * len(args)
    if scalars is not None:
        args = [scalars] + list(args)
        specs = [pl.BlockSpec(memory_space=pltpu.SMEM)] + specs
    return pl.pallas_call(
        kernel,
        in_specs=specs,
        out_specs=[vmem] * len(outs),
        out_shape=list(outs),
        scratch_shapes=list(scratch),
        compiler_params=pltpu.CompilerParams(vmem_limit_bytes=VMEM_LIMIT),
        cost_estimate=pl.CostEstimate(flops=flops, bytes_accessed=size, transcendentals=0),
    )(*args)


def shaped(shape, kind):
    return jax.ShapeDtypeStruct(shape, kind)


def reorder_kernel(count, parts, index_ref, *refs):
    for in_ref, out_ref in zip(refs[: len(refs) // 2], refs[len(refs) // 2 :]):
        pad = out_ref.shape[2] // parts
        width = in_ref.shape[2] // parts
        for i in range(count):
            value = in_ref[index_ref[i]]
            if pad == width:
                out_ref[i] = value
            else:
                spare = jnp.zeros((value.shape[0], pad - width), value.dtype)
                for part in range(parts):
                    cut = value[:, part * width : (part + 1) * width]
                    out_ref[i, :, part * pad : (part + 1) * pad] = jnp.concatenate([cut, spare], axis=1)


def shared_kernel_in(count, parts, index_ref, *refs):
    in_refs, (both_ref, down_ref) = refs[:-2], refs[-2:]
    pad = down_ref.shape[1]
    for k, in_ref in enumerate(in_refs):
        rows, columns = in_ref.shape[1], in_ref.shape[2] // parts
        spare = jnp.zeros((rows, pad - columns), in_ref.dtype)
        for i in range(count):
            value = in_ref[index_ref[i]]
            line = slice((k * count + i) * rows, (k * count + i + 1) * rows)
            for part in range(parts):
                cut = jnp.concatenate([value[:, part * columns : (part + 1) * columns], spare], axis=1)
                if part < parts - 1:
                    both_ref[line, part * pad : (part + 1) * pad] = cut
                else:
                    down_ref[line, :] = cut


def shared_weights(arrays, index, pad):
    rows = sum(a.shape[0] * a.shape[1] for a in arrays)
    outs = [shaped((rows, 2 * pad), BF), shaped((rows, pad), BF)]
    return whole_call(functools.partial(shared_kernel_in, index.shape[0], 3), arrays, outs, scalars=index)


def reorder(arrays, index, parts=1, pad=0):
    count = index.shape[0]
    outs = [shaped(a.shape[:2] + (a.shape[2] if not pad else parts * pad,), a.dtype) for a in arrays]
    return whole_call(functools.partial(reorder_kernel, count, parts), arrays, outs, scalars=index)


def swap_halves(values):
    lane = lax.broadcasted_iota(jnp.int32, values.shape, 1)
    return jnp.where(
        lane % RD < RD // 2, pltpu.roll(values, 2 * RD - RD // 2, 1), pltpu.roll(values, RD // 2, 1)
    )


def probabilities(q_main, q_rot, k_main, k_rot, allowed):
    scores = (mat_trans(q_main, k_main) + mat_trans(q_rot, k_rot)) * SCALE
    scores = jnp.where(allowed, scores, -1e30)
    expo = jnp.exp(scores - jnp.max(scores, axis=-1, keepdims=True))
    return expo / jnp.sum(expo, axis=-1, keepdims=True)


def allowed_pairs(id_col, id_row):
    shape = (id_col.shape[0], id_row.shape[1])
    key = lax.broadcasted_iota(jnp.int32, shape, 1)
    query = lax.broadcasted_iota(jnp.int32, shape, 0)
    return (id_col == id_row) & (key <= query)


def angle_table(rows):
    freq = np.power(np.float32(10000.0), np.float32(-2.0) * np.arange(RD // 2, dtype=np.float32) / np.float32(RD))
    theta = np.arange(rows, dtype=np.float32)[:, None] * freq.astype(np.float32)
    cosine, sine = np.cos(theta), np.sin(theta)
    terms = []
    for value in (np.concatenate([cosine] * 4, axis=1), np.concatenate([-sine, sine, -sine, sine], axis=1)):
        rest = value.astype(np.float32)
        for _ in range(3):
            term = rest.astype(ml_dtypes.bfloat16)
            terms.append(term)
            rest = rest - term.astype(np.float32)
    return np.concatenate(terms, axis=1)


def chunk_layout(facts_ref, j, rows, shape):
    count = CHUNK // rows
    number = lax.broadcasted_iota(jnp.int32, shape, 0 if shape[0] == CHUNK else 1)
    block, place = number // rows, number % rows
    doc, start, ends = 0, 0, [0] * count
    for k in range(3):
        lengths = [facts_ref[4 + (j * count + b) * 4 + k] for b in range(count)]
        ends = [end + length for end, length in zip(ends, lengths)]
        end, length = ends[-1], lengths[-1]
        for b in range(count - 2, -1, -1):
            end = jnp.where(block == b, ends[b], end)
            length = jnp.where(block == b, lengths[b], length)
        passed = place >= end
        doc = doc + passed.astype(jnp.int32)
        start = start + jnp.where(passed, length, 0)
    return place - start, doc + 4 * block


def chunk_tables(facts_ref, table_ref, j):
    rows = table_ref.shape[0]
    position, id_col = chunk_layout(facts_ref, j, rows, (CHUNK, 1))
    id_row = chunk_layout(facts_ref, j, rows, (1, CHUNK))[1]
    hot = low(lax.broadcasted_iota(jnp.int32, (CHUNK, rows), 1) == position)
    terms = matmul(hot, table_ref[...])
    cosine = terms[:, :128] + terms[:, 128:256] + terms[:, 256:384]
    sine = terms[:, 384:512] + terms[:, 512:640] + terms[:, 640:]
    return cosine, sine, allowed_pairs(id_col, id_row)


def pair(refs, j):
    pieces, start = [], 0
    for ref in refs:
        low_row, high_row = max(start, CHUNK * j), min(start + ref.shape[0], CHUNK * (j + 1))
        if low_row < high_row:
            pieces.append(ref[low_row - start : high_row - start, :])
        start += ref.shape[0]
    return pieces[0] if len(pieces) == 1 else jnp.concatenate(pieces, axis=0)


def forward_kernel(ndp, layout_of, pieces, count, split, place_ref, *refs):
    x_refs, refs = refs[:pieces], refs[pieces:]
    w_refs, refs = refs[: len(layout_of)], refs[len(layout_of) :]
    wl_refs, refs = refs[:count], refs[count:]
    we_ref, gains_ref, lg_ref, table_ref = refs[:4]
    near_ref, far_ref, q_ref, kr_ref, lat_ref, kv_ref, att_ref, wp_ref, wo_ref, exp_ref, gain_ref, mid_ref, lgo_ref = refs[4:]
    other_rows = [(ref, i) for ref in wl_refs for i in range(ref.shape[0])]
    dp, z, x, core = place_ref[0], place_ref[1], place_ref[2], place_ref[3]
    block = w_refs[0].shape[1]
    shard = block // 2
    lat_rows = jnp.zeros((4, 128), F32)
    spare = jnp.zeros((shard, 128 - RD), BF)
    turn = 0
    for w_ref, (far, j, first) in zip(w_refs, layout_of):
        y = j ^ dp if ndp == 2 else j
        for k in range(w_ref.shape[0]):
            row = ((y * 4 + lax.rem(z + 4 - first - k, 4)) * 2 + (x ^ far)) * block
            row = pl.multiple_of(row, block)
            wp_ref[pl.ds(row, block), :Q_COLS] = w_ref[k, :, :Q_COLS]
            wo_ref[pl.ds(row, block), :] = w_ref[k, :, Q_COLS : Q_COLS + O_COLS]
            if not split:
                continue
            here = pl.multiple_of(row + core * shard, shard)
            there = pl.multiple_of(row + (1 - core) * shard, shard)
            for at_row, lat in ((here, w_ref[k, :, W_COLS:]), (there, other_rows[turn][0][other_rows[turn][1]])):
                wp_ref[pl.ds(at_row, shard), LAT_AT : LAT_AT + 384] = lat[:shard, :]
                wp_ref[pl.ds(at_row, shard), LAT_AT + 384 :] = lat[shard:, :256]
            here_rows, there_rows = (
                wide(lat[shard : shard + 16, 256:]) for lat in (w_ref[k, :, W_COLS:], other_rows[turn][0][other_rows[turn][1]])
            )
            left = jnp.where(core == 0, here_rows[:1, :], there_rows[:1, :])
            right = jnp.where(core == 0, there_rows[:1, :], here_rows[:1, :])
            gain_ref[:, pl.ds(row, block)] = jnp.concatenate([left[:, :shard], right[:, :shard]], axis=1)
            mid_ref[:, pl.ds(row, block)] = jnp.concatenate([left[:, shard:], right[:, shard:]], axis=1)
            lat_rows = lat_rows + here_rows[1:5, :] + there_rows[1:5, :]
            turn += 1
            small = shard // 4
            for c in range(2):
                for g in range(4):
                    at_row = pl.multiple_of(row // 4 + c * small, small)
                    exp_ref[pl.ds(at_row, small), g * HD : (g + 1) * HD] = w_ref[
                        k, c * shard + g * small : c * shard + (g + 1) * small, Q_COLS + O_COLS : W_COLS
                    ]
    if not split:
        for i, (wl_ref, _) in enumerate(other_rows):
            wp_ref[i * shard : (i + 1) * shard, LAT_AT:] = jnp.concatenate([wl_ref[i, :shard, :], spare], axis=1)
        exp_ref[...] = we_ref[...]
        gain_ref[...] = gains_ref[:1, :]
        mid_ref[...] = gains_ref[1:2, :]
        lgo_ref[...] = lg_ref[...]
    else:
        lgo_ref[...] = jnp.concatenate([lat_rows[i : i + 1, :] for i in range(4)], axis=1)
    gain, lat_gain = gain_ref[...], lgo_ref[...]
    for j in range(4):
        rows = slice(CHUNK * j, CHUNK * (j + 1))
        xf = wide(pair(x_refs, j))
        normed = low(xf * rms_scale(xf) * gain)
        proj = matmul(normed, wp_ref[...])
        cosine, sine, allowed = chunk_tables(place_ref, table_ref, j)
        q_mix = proj[:, 2 * HD : Q_COLS]
        k_mix = proj[:, ROT_AT:]
        q_rot = low(q_mix * cosine + swap_halves(q_mix) * sine)
        k_rot = k_mix * cosine + swap_halves(k_mix) * sine
        k_turned = low(pltpu.roll(k_rot, RD, 1))
        k_rot = low(k_rot)
        q_main = low(proj[:, : 2 * HD])
        lat = proj[:, LAT_AT:ROT_AT]
        lat_ref[rows, :] = lat
        compressed = low(lat * rms_scale(lat) * lat_gain)
        expanded = low(matmul(compressed, exp_ref[...]))
        q_ref[rows, : 2 * HD] = q_main
        q_ref[rows, 2 * HD :] = q_rot
        kr_ref[rows, :] = k_rot
        kv_ref[rows, :] = expanded
        attended = []
        for head, k_side in ((0, k_rot), (1, k_turned)):
            k_main = expanded[:, 2 * head * HD : (2 * head + 1) * HD]
            values = expanded[:, (2 * head + 1) * HD : (2 * head + 2) * HD]
            probs = probabilities(q_main[:, head * HD : (head + 1) * HD], q_rot, k_main, k_side, allowed)
            attended.append(low(matmul(low(probs), values)))
        attended = jnp.concatenate(attended, axis=1)
        att_ref[rows, :] = attended
        put_half(near_ref, far_ref, j, 4, low(mat_trans(attended, wo_ref[...])))


def put_half(near_ref, far_ref, j, count, value):
    ref = near_ref if j < count // 2 else far_ref
    j = j % (count // 2)
    ref[j * CHUNK : (j + 1) * CHUNK, :] = value


def attention_forward(place, x_pieces, weights, layout_of, w_lat, w_exp, gains, lat_gain, table, split):
    own, width = x_pieces[0].shape
    rows = 8 * own
    args = list(x_pieces) + list(weights) + list(w_lat) + [w_exp, gains, lat_gain, table]
    outs = [shaped((rows // 2, width), BF)] * 2 + [
        shaped((rows, Q_COLS), BF),
        shaped((rows, 128), BF),
        shaped((rows, LAT), F32),
        shaped((rows, 4 * HD), BF),
        shaped((rows, O_COLS), BF),
        shaped((width, PROJ), BF),
        shaped((width, O_COLS), BF),
        shaped((LAT, 4 * HD), BF),
        shaped((1, width), F32),
        shaped((1, width), F32),
        shaped((1, LAT), F32),
    ]
    kernel = functools.partial(forward_kernel, lax.axis_size("dp"), layout_of, len(x_pieces), len(w_lat), split)
    flops = 2 * rows * width * (PROJ + O_COLS)
    out = whole_call(kernel, args, outs, flops=flops, scalars=place)
    return out[:2], out[2:]


def backward_kernel(pieces, count, lat_rows, place_ref, *refs):
    x_refs, g_refs, refs = refs[:pieces], refs[pieces : pieces + count], refs[pieces + count :]
    q_ref, kr_ref, lat_ref, kv_ref, att_ref, wp_ref, wo_ref, we_ref, gain_ref, mid_ref, lg_ref, dm_ref = refs[:12]
    table_ref, dn_ref, dw_ref, dl_ref, de_ref, acc_q, acc_o, acc_e, dg_ref, dlg_ref = refs[12:]
    split = len(dw_ref.shape) > 2
    dp, z, x, core = place_ref[0], place_ref[1], place_ref[2], place_ref[3]
    own = x_refs[0].shape[0]
    gain, w_exp, lat_gain = gain_ref[...], we_ref[...], lg_ref[...]

    def add(acc, value, first):
        acc[...] = value if first else acc[...] + value

    for j in range(4):
        rows = slice(CHUNK * j, CHUNK * (j + 1))
        xf = wide(pair(x_refs, j))
        whitened = xf * rms_scale(xf)
        normed = low(whitened * gain)
        lat = lat_ref[rows, :]
        lat_scale = rms_scale(lat)
        white_lat = lat * lat_scale
        grad = pair(g_refs, j)
        cosine, sine, allowed = chunk_tables(place_ref, table_ref, j)
        d_att = low(matmul(grad, wo_ref[...]))
        q_rot, k_rot = q_ref[rows, 2 * HD :], kr_ref[rows, :]
        k_turned = low(pltpu.roll(wide(k_rot), RD, 1))
        d_main, d_expanded = [], []
        dq_mix = None
        dk_mix = None
        for head, k_side in ((0, k_rot), (1, k_turned)):
            q_main = q_ref[rows, head * HD : (head + 1) * HD]
            k_main = kv_ref[rows, 2 * head * HD : (2 * head + 1) * HD]
            values = kv_ref[rows, (2 * head + 1) * HD : (2 * head + 2) * HD]
            probs = probabilities(q_main, q_rot, k_main, k_side, allowed)
            d_out = d_att[:, head * HD : (head + 1) * HD]
            d_prob = mat_trans(d_out, values)
            d_values = contract(low(probs), d_out)
            d_scores = low(probs * (d_prob - jnp.sum(probs * d_prob, axis=-1, keepdims=True)))
            d_main.append(matmul(d_scores, k_main) * SCALE)
            d_expanded += [contract(d_scores, q_main) * SCALE, d_values]
            dq_one = matmul(d_scores, k_side)
            dk_one = contract(d_scores, q_rot)
            dq_mix = dq_one if head == 0 else dq_mix + dq_one
            dk_mix = dk_one if head == 0 else dk_mix + pltpu.roll(dk_one, RD, 1)
        dq_mix = dq_mix * SCALE
        dk_mix = dk_mix * SCALE
        dq_mix = dq_mix * cosine - swap_halves(dq_mix) * sine
        dk_mix = dk_mix * cosine - swap_halves(dk_mix) * sine
        dk_mix = jnp.where(lax.broadcasted_iota(jnp.int32, dk_mix.shape, 1) < RD, dk_mix, 0.0)
        d_expanded = low(jnp.concatenate(d_expanded, axis=1))
        d_comp = mat_trans(d_expanded, w_exp)
        scaled = d_comp * lat_gain
        d_lat = lat_scale * (scaled - white_lat * jnp.mean(scaled * white_lat, axis=-1, keepdims=True))
        d_proj = low(jnp.concatenate(d_main + [dq_mix, d_lat, dk_mix], axis=1))
        d_normed = mat_trans(d_proj, wp_ref[...])
        part = low(d_normed)
        for k in range(2):
            piece = 2 * j + k
            place = lax.rem(z + 4 - piece % 4, 4) * 2 + (core ^ (piece // 4))
            dn_ref[pl.ds(pl.multiple_of(place * own, own), own), :] = part[k * own : (k + 1) * own, :]
        add(dg_ref, jnp.sum(d_normed * whitened, axis=0, keepdims=True), j == 0)
        add(dlg_ref, jnp.sum(d_comp * white_lat, axis=0, keepdims=True), j == 0)
        add(acc_q, contract(d_proj, normed), j == 0)
        add(acc_o, contract(att_ref[rows, :], grad), j == 0)
        add(acc_e, contract(low(white_lat * lat_gain), d_expanded), j == 0)
    shard = acc_q.shape[1] * lat_rows // LAT
    lane = lax.broadcasted_iota(jnp.int32, (LAT, acc_q.shape[1]), 1)
    line = lax.broadcasted_iota(jnp.int32, (LAT, acc_q.shape[1]), 0)
    spread = low((line // lat_rows == lane // shard) & (line % lat_rows == lane % shard))
    spread = matmul(low(jnp.broadcast_to(dlg_ref[...], (8, LAT))), spread)[:1, :]
    acc_q[ROT_AT + RD : ROT_AT + RD + 8, :] = jnp.concatenate(
        [dg_ref[...], dm_ref[...], spread, jnp.zeros((5, acc_q.shape[1]), F32)], axis=0
    )
    if not split:
        dw_ref[:, :Q_COLS] = low(acc_q[:Q_COLS, :].T)
        dw_ref[:, Q_COLS : Q_COLS + O_COLS] = low(acc_o[...].T)
        dl_ref[...] = low(acc_q[Q_COLS:, :].T)
        de_ref[...] = low(acc_e[...])
        return
    block = 2 * shard
    for number in range(acc_q.shape[1] // block):
        y, zz, xx = number // 8, number // 2 % 4, number % 2
        lanes = slice(number * block, (number + 1) * block)
        slot = (x ^ xx) * 4 + y * 2 + zz if zz < 2 else 8 + (dp ^ y) * 4 + (zz - 2) * 2 + xx
        dw_ref[slot, :, :Q_COLS] = low(acc_q[:Q_COLS, lanes].T)
        dw_ref[slot, :, Q_COLS : Q_COLS + O_COLS] = low(acc_o[:, lanes].T)
        for c in range(2):
            for g in range(4):
                row = c * shard + g * lat_rows
                i = number * 2 + c
                dw_ref[slot, row : row + lat_rows, Q_COLS + O_COLS :] = low(
                    acc_e[i * lat_rows : (i + 1) * lat_rows, g * HD : (g + 1) * HD]
                )
        both = low(acc_q[Q_COLS:, lanes].T)
        for c in range(2):
            dl_ref[core ^ c, number, :, :] = both[c * shard : (c + 1) * shard, :]


def attention_backward(place, x_pieces, g_pieces, saved, d_gain_mid, table, lat_rows):
    own, width = x_pieces[0].shape
    q, kr, lat, kv, att, wp, wo, w_exp, gain, mid, lat_gain = saved
    args = list(x_pieces) + list(g_pieces)
    args += [q, kr, lat, kv, att, wp, wo, w_exp, gain, mid, lat_gain, d_gain_mid, table]
    outs = [
        shaped((8 * own, width), BF),
        shaped((width, W_COLS), BF),
        shaped((width, PROJ - Q_COLS), BF),
        shaped((LAT, 4 * HD) if lat_rows % 16 else (16, 128), BF),
    ]
    shard = width * lat_rows // LAT
    if not lat_rows % 16:
        outs[1] = shaped((width // (2 * shard), 2 * shard, W_COLS), BF)
        outs[2] = shaped((2, width // (2 * shard), shard, PROJ - Q_COLS), BF)
    scratch = (
        pltpu.VMEM((PROJ, width), F32), pltpu.VMEM((O_COLS, width), F32), pltpu.VMEM((LAT, 4 * HD), F32),
        pltpu.VMEM((1, width), F32), pltpu.VMEM((1, LAT), F32),
    )
    flops = 2 * 8 * own * width * (2 * PROJ + 2 * O_COLS)
    kernel = functools.partial(backward_kernel, len(x_pieces), len(g_pieces), lat_rows)
    d_norm, d_head, d_wl, d_we = whole_call(kernel, args, outs, scratch, flops=flops, scalars=place)
    if lat_rows % 16:
        d_we = d_we.reshape(width // shard, lat_rows, 4, E_COLS).transpose(0, 2, 1, 3).reshape(width, E_COLS)
        d_head = jnp.concatenate([d_head[:, : Q_COLS + O_COLS], d_we], axis=1)
    return d_norm, d_head, d_wl


def routing_kernel(first, lanes, slots, me_ref, *refs):
    in_refs, (row_ref, gate_ref, col_ref) = refs[:4], refs[4:]
    mine = lax.broadcasted_iota(jnp.int32, (16, 128), 0) == me_ref[0]
    gates = []
    for ref, lane in zip(in_refs, lanes):
        for k in range(4):
            both = wide(ref[k, first : first + 32, lane : lane + 128])
            gates.append(jnp.sum(jnp.where(mine, both[:16, :] + both[16:, :], 0.0), axis=0, keepdims=True))
    gates = jnp.concatenate(gates, axis=0)
    routed = gates > 0.0
    line = lax.broadcasted_iota(jnp.int32, (128, 128), 0)
    column = lax.broadcasted_iota(jnp.int32, (128, 128), 1)
    before = low((line <= column) & (line // 64 == column // 64))
    count = matmul(low(routed), before)
    source = lax.broadcasted_iota(jnp.int32, (16, 128), 0)
    token = lax.broadcasted_iota(jnp.int32, (16, 128), 1)
    block = ((source % 2) * 2 + token // 64).astype(F32)
    target = jnp.where(routed, block * slots + count - 1.0, -1.0)
    turned = target.T
    for k in range(16):
        part = slice((k % 2) * 128, (k % 2 + 1) * 128)
        row_ref[k // 2, :, part] = target[k : k + 1, :].astype(jnp.int32)
        gate_ref[k // 2, :, part] = gates[k : k + 1, :]
        col_ref[k * 128 : (k + 1) * 128, :] = turned[:, k : k + 1].astype(jnp.int32)


def routing(me, arrays, first, lanes, slots):
    outs = [shaped((8, 1, CHUNK), jnp.int32), shaped((8, 1, CHUNK), F32), shaped((8 * CHUNK, 1), jnp.int32)]
    return whole_call(functools.partial(routing_kernel, first, lanes, slots), arrays, outs, scalars=me)


def enter_grad_kernel(slots, *refs):
    g_refs, (target_ref, gate_ref, rg0_ref, rg1_ref, rs_ref) = refs[:-5], refs[-5:]
    half = rg0_ref.shape[1]
    for j in range(8):
        grad = pair(g_refs, j)
        chosen = lax.broadcasted_iota(jnp.int32, (slots, CHUNK), 0) == target_ref[j]
        share = jnp.sum(jnp.where(chosen, gate_ref[j], 0.0), axis=1, keepdims=True)
        rs_ref[j * slots : (j + 1) * slots, :] = share
        value = low(matmul(low(chosen), grad) * share)
        rg0_ref[j * slots : (j + 1) * slots, :] = value[:, :half]
        rg1_ref[j * slots : (j + 1) * slots, :] = value[:, half:]


def dispatch_kernel(slots, *refs):
    t_refs, (target_ref, rx0_ref, rx1_ref) = refs[:-3], refs[-3:]
    half = rx0_ref.shape[1]
    for j in range(8):
        chosen = lax.broadcasted_iota(jnp.int32, (slots, CHUNK), 0) == target_ref[j]
        value = low(matmul(low(chosen), pair(t_refs, j)))
        rx0_ref[j * slots : (j + 1) * slots, :] = value[:, :half]
        rx1_ref[j * slots : (j + 1) * slots, :] = value[:, half:]


def hidden_shared_kernel(count, *refs):
    t_refs, g_refs, (sgu_ref, sd_ref, act_ref, pre_ref) = refs[:count], refs[count:-4], refs[-4:]
    third = sd_ref.shape[1]
    for j in range(8):
        rows = slice(j * CHUNK, (j + 1) * CHUNK)
        both = matmul(pair(t_refs, j), sgu_ref[...])
        gate_pre, up = both[:, :third], both[:, third:]
        d_act = matmul(pair(g_refs, j), sd_ref[...])
        sigma = jax.nn.sigmoid(gate_pre)
        swish = gate_pre * sigma
        act_ref[rows, :] = low(swish * up)
        pre_ref[rows, :third] = low(d_act * up * (sigma * (1.0 + gate_pre * (1.0 - sigma))))
        pre_ref[rows, third:] = low(d_act * swish)


def enter_grad(g_pieces, target, gate, slots):
    own, width = g_pieces[0].shape
    args = list(g_pieces) + [target, gate]
    outs = [shaped((slots, width // 2), BF)] * 2 + [shaped((slots, 1), F32)]
    flops = 32 * own * width * (slots // 8)
    return whole_call(functools.partial(enter_grad_kernel, slots // 8), args, outs, flops=flops)


def dispatch(t_pieces, target, slots):
    own, width = t_pieces[0].shape
    args = list(t_pieces) + [target]
    outs = [shaped((slots, width // 2), BF)] * 2
    flops = 32 * own * width * (slots // 8)
    return whole_call(functools.partial(dispatch_kernel, slots // 8), args, outs, flops=flops)


def hidden_shared(t_pieces, g_pieces, s_both, s_down):
    own, width = t_pieces[0].shape
    third = s_down.shape[1]
    args = list(t_pieces) + list(g_pieces) + [s_both, s_down]
    outs = [shaped((16 * own, third), BF), shaped((16 * own, 2 * third), BF)]
    return whole_call(functools.partial(hidden_shared_kernel, len(t_pieces)), args, outs, flops=96 * own * width * third)


def hidden_kernel(x0_ref, x1_ref, r0_ref, r1_ref, g0_ref, g1_ref, u0_ref, u1_ref, d0_ref, d1_ref, act_ref, dg_ref, du_ref, away_ref):
    step = 256
    for j in range(x0_ref.shape[0] // step):
        rows = slice(j * step, (j + 1) * step)
        x0, x1 = x0_ref[rows, :], x1_ref[rows, :]
        gate = matmul(x0, g0_ref[...]) + matmul(x1, g1_ref[...])
        up = matmul(x0, u0_ref[...]) + matmul(x1, u1_ref[...])
        d_act = mat_trans(r0_ref[rows, :], d0_ref[...]) + mat_trans(r1_ref[rows, :], d1_ref[...])
        sigma = jax.nn.sigmoid(gate)
        swish = gate * sigma
        act_ref[rows, :] = low(swish * up)
        dg_ref[rows, :] = low(d_act * up * (sigma * (1.0 + gate * (1.0 - sigma))))
        du_ref[rows, :] = low(d_act * swish)
    away_ref[...] = low(contract(act_ref[...], r1_ref[...]))


def tiled_call(kernel, steps, args, specs, outs, out_specs, scratch=(), flops=0, aliases=None):
    size = sum(a.size * a.dtype.itemsize for a in list(args) + list(outs))
    return pl.pallas_call(
        kernel,
        grid=(steps,),
        in_specs=specs,
        out_specs=out_specs,
        out_shape=outs,
        scratch_shapes=list(scratch),
        input_output_aliases=aliases or {},
        compiler_params=pltpu.CompilerParams(vmem_limit_bytes=VMEM_LIMIT),
        cost_estimate=pl.CostEstimate(flops=flops, bytes_accessed=size, transcendentals=0),
    )(*args)


def whole_spec(array):
    return pl.BlockSpec(array.shape, lambda i: (0,) * array.ndim)


def expert_hidden(rows_x, rows_g, own, other):
    slots, half = rows_x[0].shape
    hidden = own[0].shape[1]
    tile = HIDDEN_TILE
    by_column = pl.BlockSpec((half, tile), lambda i: (0, i))
    by_row = pl.BlockSpec((tile, half), lambda i: (i, 0))
    args = list(rows_x) + list(rows_g) + [own[0], other[0], own[1], other[1], own[2], other[2]]
    specs = [whole_spec(value) for value in args[:4]] + [by_column] * 4 + [by_row] * 2
    outs = [shaped((slots, hidden), BF)] * 3 + [shaped((hidden, half), BF)]
    out_specs = [pl.BlockSpec((slots, tile), lambda i: (0, i))] * 3 + [by_row]
    flops = 14 * slots * half * hidden
    return tiled_call(hidden_kernel, -(-hidden // tile), args, specs, outs, out_specs, flops=flops)


def back_kernel(per, dg_ref, du_ref, g0_ref, g1_ref, u0_ref, u1_ref, target_ref, left_ref, right_ref, *refs):
    out_refs, rows_ref = refs[:4], refs[4]
    steps = pl.num_programs(0) // 2
    own = pl.program_id(0) < steps

    @pl.when(own)
    def _():
        rows_ref[...] = low(mat_trans(dg_ref[...], g0_ref[...]) + mat_trans(du_ref[...], u0_ref[...]))

    @pl.when(jnp.logical_not(own))
    def _():
        rows_ref[...] = low(mat_trans(dg_ref[...], g1_ref[...]) + mat_trans(du_ref[...], u1_ref[...]))

    right = right_ref[...]
    for j in range(8):
        hot = low(lax.broadcasted_iota(jnp.int32, (CHUNK, per), 1) == target_ref[j * CHUNK : (j + 1) * CHUNK, :])
        out = matmul(hot, rows_ref[j * per : (j + 1) * per, :])
        out = low(out + mat_trans(left_ref[j * CHUNK : (j + 1) * CHUNK, :], right))
        out_refs[j // 2][(j % 2) * CHUNK : (j % 2 + 1) * CHUNK, :] = out


def expert_back(d_gate, d_up, own, other, target, left, right):
    slots, hidden = d_gate.shape
    rows, columns = left.shape
    width = right.shape[0]
    tile = 256
    steps = width // tile // 2
    near = pl.BlockSpec((tile, hidden), lambda i: (jnp.minimum(i, steps - 1), 0))
    far = pl.BlockSpec((tile, hidden), lambda i: (jnp.maximum(i - steps, 0), 0))
    args = [d_gate, d_up, own[0], other[0], own[1], other[1], target, left, right]
    specs = [whole_spec(d_gate), whole_spec(d_up)] + [near, far] * 2
    specs += [whole_spec(target), whole_spec(left), pl.BlockSpec((tile, columns), lambda i: (i, 0))]
    outs = [shaped((rows // 4, width), BF)] * 4
    out_specs = [pl.BlockSpec((rows // 4, tile), lambda i: (0, i))] * 4
    flops = 4 * slots * width * hidden + 2 * rows * width * (columns + slots // 8)
    return tiled_call(
        functools.partial(back_kernel, slots // 8), 2 * steps, args, specs, outs, out_specs,
        (pltpu.VMEM((slots, tile), BF),), flops=flops,
    )


def out_kernel(per, act_ref, share_ref, d0_ref, d1_ref, target_ref, left_ref, right_ref, *refs):
    out_refs, rows_ref = refs[:4], refs[4]
    steps = pl.num_programs(0) // 2
    own = pl.program_id(0) < steps

    @pl.when(own)
    def _():
        rows_ref[...] = low(matmul(act_ref[...], d0_ref[...]) * share_ref[...])

    @pl.when(jnp.logical_not(own))
    def _():
        rows_ref[...] = low(matmul(act_ref[...], d1_ref[...]) * share_ref[...])

    right = right_ref[...]
    for j in range(8):
        hot = low(lax.broadcasted_iota(jnp.int32, (CHUNK, per), 1) == target_ref[j * CHUNK : (j + 1) * CHUNK, :])
        out = matmul(hot, rows_ref[j * per : (j + 1) * per, :])
        out = low(out + mat_trans(left_ref[j * CHUNK : (j + 1) * CHUNK, :], right))
        out_refs[j // 2][(j % 2) * CHUNK : (j % 2 + 1) * CHUNK, :] = out


def expert_out(act, share, own, other, target, left, right):
    slots, hidden = act.shape
    rows, columns = left.shape
    width = right.shape[0]
    tile = 256
    steps = width // tile // 2
    args = [act, share, own[2], other[2], target, left, right]
    specs = [
        whole_spec(act), whole_spec(share),
        pl.BlockSpec((hidden, tile), lambda i: (0, jnp.minimum(i, steps - 1))),
        pl.BlockSpec((hidden, tile), lambda i: (0, jnp.maximum(i - steps, 0))),
        whole_spec(target), whole_spec(left), pl.BlockSpec((tile, columns), lambda i: (i, 0)),
    ]
    outs = [shaped((rows // 4, width), BF)] * 4
    out_specs = [pl.BlockSpec((rows // 4, tile), lambda i: (0, i))] * 4
    flops = 2 * slots * width * hidden + 2 * rows * width * (columns + slots // 8)
    return tiled_call(
        functools.partial(out_kernel, slots // 8), 2 * steps, args, specs, outs, out_specs,
        (pltpu.VMEM((slots, tile), BF),), flops=flops,
    )


def shared_kernel(part, count, *refs):
    t_refs, g_refs, (pre_ref, act_ref, out_ref, acc_t, acc_g) = refs[:count], refs[count:-5], refs[-5:]
    pad = act_ref.shape[1]
    for j in range(8):
        rows = slice(j * CHUNK, (j + 1) * CHUNK)
        by_tok = contract(pre_ref[rows, :], pair(t_refs, j))
        by_grad = contract(act_ref[rows, :], pair(g_refs, j))
        acc_t[...] = by_tok if j == 0 else acc_t[...] + by_tok
        acc_g[...] = by_grad if j == 0 else acc_g[...] + by_grad
    parts = [acc_t[:part, :], acc_t[pad : pad + part, :], acc_g[:part, :]]
    spare = -3 * part % 128
    if spare:
        parts.append(jnp.zeros((spare, acc_t.shape[1]), F32))
    out_ref[...] = low(jnp.concatenate(parts, axis=0).T[:, : 3 * part])


def shared_gradient(t_pieces, g_pieces, pre, act, part):
    own, width = t_pieces[0].shape
    args = list(t_pieces) + list(g_pieces) + [pre, act]
    outs = [shaped((width, 3 * part), BF)]
    scratch = (pltpu.VMEM((pre.shape[1], width), F32), pltpu.VMEM((act.shape[1], width), F32))
    flops = 32 * own * width * (pre.shape[1] + act.shape[1])
    return whole_call(functools.partial(shared_kernel, part, len(t_pieces)), args, outs, scratch, flops=flops)[0]


def local(
    tokens, lengths, routes, gates, norm_in, latent_gain, norm_mid, w_query, w_latent, w_expand, w_output,
    shared_gate, shared_up, shared_down, expert_gate, expert_up, expert_down, cotangent,
):
    micro = lengths.shape[0]
    own_rows, width = tokens.shape
    rows = own_rows // micro
    experts = lax.axis_size("expert")
    ndp = lax.axis_size("dp")
    two = ndp == 2
    cap = rows * TOP * 4 // (3 * experts)
    blocks = experts * micro
    all_rows = experts * own_rows
    devices = ndp * experts
    shard = width // devices
    lat_rows = w_expand.shape[0]
    lat_cols = w_latent.shape[1]
    ff_s = shared_gate.shape[1]
    ff_part = ff_s // experts
    ff_pad = -(-ff_part // 128) * 128
    half = width // 2
    me = lax.axis_index("expert")
    dp = lax.axis_index("dp")
    core, x, z = me % 2, (me // 2) % 2, me // 4

    def turn(value):
        if not two:
            return value
        swapped = jnp.concatenate([value[..., half:], value[..., :half]], axis=-1)
        return jnp.where(dp == 1, swapped, value)

    def dp_swap(value):
        return lax.ppermute(value, "dp", [(0, 1), (1, 0)])

    clock = Clock(dp_swap)

    def lane(value):
        return [(dp_swap, value)] if two else []

    def dp_gather(value, axis):
        return lax.all_gather(value, "dp", axis=axis, tiled=True)

    def dp_scatter(value, axis=0):
        return lax.psum_scatter(value, "dp", scatter_dimension=axis, tiled=True)

    def cut(value, k):
        return value[k * own_rows : (k + 1) * own_rows]

    number = jnp.arange(experts, dtype=jnp.int32)
    near_z, near_x, near_c = number % 4, (number // 4) % 2, number // 8
    row_index = ((z + 4 - near_z) % 4) * 4 + (near_x ^ x) * 2 + (near_c ^ core)
    few_index = jnp.concatenate([row_index[:4], row_index[8:12]])
    n_z, n_x, n_c = number // 4, (number // 2) % 2, number % 2
    block_index = ((z + 4 - n_z) % 4) * 4 + (n_x ^ x) * 2 + (n_c ^ core)

    pairs = HEADS // 2
    groups = shard // lat_rows
    piece = w_query.reshape(shard, pairs, 2, HD + RD).transpose(1, 0, 2, 3)
    piece = jnp.concatenate(
        [
            piece[..., :HD].reshape(pairs, shard, 2 * HD),
            piece[..., HD:].reshape(pairs, shard, 2 * RD),
            w_output.reshape(pairs, O_COLS, shard).transpose(0, 2, 1),
            w_expand.reshape(lat_rows, pairs, groups, E_COLS).transpose(1, 2, 0, 3).reshape(pairs, shard, E_COLS),
        ],
        axis=2,
    )
    piece = piece.reshape(4, 2, shard, W_COLS)
    kept, away = at(piece, core, 1), at(piece, 1 - core, 1)

    by_expert = jnp.sum(jnp.where(routes.T[None] == number[:, None, None], gates.T[None], 0.0), axis=1)
    gate_high = low(by_expert)
    gate_low = low(by_expert - wide(gate_high))

    def as_row(value):
        return jnp.pad(value.reshape(1, -1), ((0, 0), (0, own_rows - value.size)))

    small_rows = 48
    lat_gain_rows = lax.dynamic_update_slice(jnp.zeros((LAT,), BF), latent_gain, ((dp * experts + me) * lat_rows,))
    small = jnp.concatenate(
        [
            as_row(jnp.concatenate([norm_in, norm_mid])), lat_gain_rows.reshape(4, 128), as_row(low(lengths)),
            jnp.zeros((10, own_rows), BF), gate_high, gate_low,
        ],
        axis=0,
    )

    s_piece = jnp.concatenate(
        [
            shared_gate.reshape(shard, experts, ff_part).transpose(1, 0, 2),
            shared_up.reshape(shard, experts, ff_part).transpose(1, 0, 2),
            shared_down.reshape(experts, ff_part, shard).transpose(0, 2, 1),
        ],
        axis=2,
    ).reshape(4, 2, 2, shard, 3 * ff_part)
    own_expert = (expert_gate[0], expert_up[0], expert_down[0])
    x0 = tokens
    g0 = low(turn(cotangent))

    if two:
        fetched = [clock.add(value) for value in (own_expert[2], own_expert[0], own_expert[1])]
        wide_lat = jnp.pad(w_latent, ((0, 0), (0, 640 - lat_cols)))
        low_rows = jnp.pad(small, ((0, shard - small_rows), (0, 0)))
        lat = jnp.concatenate([wide_lat[:, :384], jnp.concatenate([wide_lat[:, 384:], low_rows], axis=1)], axis=0)
    else:
        lat = small
    s_kept, s_away = at(s_piece, core, 2), at(s_piece, 1 - core, 2)
    clock.slot(feed=0.6)
    moved, _, _, _ = clock.slot((core_swap, away), (core_swap, s_away), (z_up, x0), feed=0.55)
    x1 = moved[2]
    s_piece = jnp.stack([s_kept, moved[1]], axis=2)
    w_own = jnp.where(
        core == 0, jnp.concatenate([kept, moved[0]], axis=1), jnp.concatenate([moved[0], kept], axis=1)
    )
    if two:
        w_own = jnp.concatenate([w_own, jnp.broadcast_to(lat, (4,) + lat.shape)], axis=2)
    s_kept, s_away = at(s_piece, x, 1), at(s_piece, 1 - x, 1)
    moved, _, _, _ = clock.slot(
        (z_two, at(w_own, (z + 2) % 4, 0)),
        (z_up, at(w_own, (z + 1) % 4, 0)),
        (z_down, at(w_own, (z + 3) % 4, 0)),
        (x_swap, s_away),
        feed=1.1,
    )
    w_own = jnp.stack([at(w_own, z, 0), moved[1], moved[0], moved[2]])
    s_piece = jnp.stack([s_kept, moved[3]], axis=1)
    if two:
        lats = w_own[..., W_COLS:]
        facts = lats[:, shard : shard + small_rows, 256:]
    else:
        facts = jnp.stack([lat, z_up(lat), z_two(lat), z_down(lat)])

    moved, _, _, _ = clock.slot(
        (x_swap, w_own), *lane(w_own), (z_up, x1), (z_up, g0), (core_swap, lats if two else facts)
    )
    w_x, x2, g1, lat_other = moved[0], *moved[-3:]
    facts_few = jnp.concatenate([facts, lat_other[:, shard : shard + small_rows, 256:] if two else lat_other])
    lengths_few = facts_few[:, 5, : lengths.size].astype(jnp.int32).reshape(-1)
    scalars = jnp.concatenate([jnp.stack([dp, z, x, core]).astype(jnp.int32), lengths_few])
    table = jnp.asarray(angle_table(rows))
    s_two, s_up, s_down = (at(s_piece, (z + k) % 4, 0) for k in (2, 1, 3))
    if two:
        w_y = moved[1]
        moved, _, _, _ = clock.slot(
            (x_swap, w_y[:2]), (dp_swap, w_x[2:]), (z_up, x2),
            (core_swap, jnp.concatenate([w_x[..., W_COLS:], w_y[..., W_COLS:]])),
            (core_swap, jnp.concatenate([x0, x1])),
        )
        w_far, x3, lat_other_xy, cx01 = moved[:2], *moved[2:]
        lat_far = jnp.concatenate([w_far[0][..., W_COLS:], w_far[1][..., W_COLS:]])
        moved, _, _, _ = clock.slot(
            (core_swap, lat_far), (core_swap, jnp.concatenate([x2, x3])), (z_up, s_up), feed=0.35
        )
        cx23, s_up = moved[1:]
        weights = [w_own, w_x, w_y] + w_far
        layout_of = ((0, 0, 0), (1, 0, 0), (0, 1, 0), (1, 1, 0), (1, 1, 2))
        w_lat = [lat_other, lat_other_xy, moved[0]]
        w_exp = gains = gain_lat = jnp.zeros((8, 128), F32)
        route_from = [w_own, w_x, lat_other, lat_other_xy]
        route_lanes = (W_COLS + 256, W_COLS + 256, 256, 256)
    else:
        x3, s_up = z_up(x2), z_up(s_up)
        cx01, cx23 = core_swap(jnp.concatenate([x0, x1])), core_swap(jnp.concatenate([x2, x3]))
        near, far = dp_gather(w_own[None], 0), dp_gather(w_x[None], 0)
        weights = [near[i] for i in range(ndp)] + [far[i] for i in range(ndp)]
        layout_of = tuple((side, j, 0) for side in range(2) for j in range(ndp))
        w_lat = lax.all_gather(w_latent, ("dp", "expert"), axis=0)
        w_lat = [w_lat[i][None] for i in range(devices)]
        facts = lax.all_gather(small, ("dp", "expert"), axis=0)
        gains = wide(facts[:, 0, : 2 * shard]).reshape(devices, 2, shard).transpose(1, 0, 2).reshape(2, width)
        gain_lat = wide(facts[:, 1:5]).sum(axis=0).reshape(1, LAT)
        route_from = jnp.take(lax.dynamic_slice_in_dim(facts, dp * experts, experts, 0), row_index, axis=0)
        route_from = [route_from[4 * i : 4 * i + 4] for i in range(4)]
        route_lanes = (0, 0, 0, 0)
        w_exp = jnp.concatenate([value[..., Q_COLS + O_COLS :] for value in weights], axis=0)
        w_exp = w_exp.reshape(2, ndp, 4, 2 * shard, E_COLS).transpose(1, 2, 0, 3, 4)
        w_exp = w_exp.reshape(devices // 2, -1, E_COLS)
        chips = jnp.arange(devices // 2, dtype=jnp.int32)
        chip_index = chips // 8 * 8 + ((z + 4 - chips // 2 % 4) % 4) * 2 + (chips % 2 ^ x)
        w_exp = reorder([w_exp], chip_index)[0]
        w_exp = w_exp.reshape(devices, groups, lat_rows, E_COLS).transpose(0, 2, 1, 3).reshape(LAT, groups * E_COLS)
    slots = blocks * cap
    route = functools.partial(routing, first=(shard if two else 0) + 16, lanes=route_lanes, slots=cap)

    x_pieces = [x0, x1, x2, x3, cx01, cx23]
    moved, _, _, made = clock.slot(
        (x_swap, g0), (z_up, g1), (z_down, g0),
        feed=0.95,
        work=[
            (
                lambda *a: attention_forward(*a[:3], layout_of, *a[3:], split=two),
                scalars, x_pieces, weights, w_lat, w_exp, gains, gain_lat, table,
            )
        ],
    )
    gx0, g2, g3 = moved
    (part_near, part_far), saved = made[0]
    gain_in, gain_mid, gain_lat = saved[-3:]

    moved, _, _, _ = clock.slot((core_swap, part_far), (z_two, s_two), (z_down, s_down), feed=0.65)
    s_two, s_down = moved[1:]
    s_piece = jnp.stack([at(s_piece, z, 0), s_up, s_two, s_down]).reshape(experts, shard, 3 * ff_part)
    g_near = jnp.concatenate([g0, g1, g2, g3])
    terms = [wide(cut(part_near, k)) + wide(cut(moved[0], k)) for k in range(4)]
    moved, _, _, made = clock.slot(
        (z_down, low(terms[3])), (x_swap, g1), work=[(route, me.reshape(1), route_from)], feed=0.67
    )
    gx1 = moved[1]
    target_row, gate_row, target_col = made[0]
    moved, _, _, _ = clock.slot(
        (z_down, low(terms[2] + wide(moved[0]))), (x_swap, g2), (core_swap, g_near), feed=0.67
    )
    gx2, cg_near = moved[1:]
    moved, _, _, _ = clock.slot((z_down, low(terms[1] + wide(moved[0]))), (x_swap, g3), feed=0.67)
    gx3 = moved[1]
    xf = wide(tokens)
    mid = xf + terms[0] + wide(moved[0])
    scale_mid = rms_scale(mid)
    t0 = turn(low(mid * scale_mid * gain_mid))

    g_far = jnp.concatenate([gx0, gx1, gx2, gx3])
    join = lambda *pieces: jnp.concatenate(pieces, axis=0)
    moved, _, _, made = clock.slot(
        (z_up, t0), (x_swap, t0), work=[(join, *fetched[0][2])] if two else [], feed=0.67
    )
    t1, tx0 = moved
    down_got = made
    moved, _, _, _ = clock.slot((z_up, t1), (x_swap, t1), (core_swap, g_far), feed=0.67)
    t2, tx1, cg_far = moved
    g_pieces = [g0, g1, g2, g3, gx0, gx1, gx2, gx3, cg_near, cg_far]
    part = experts // 2
    moved, _, _, made = clock.slot(
        (z_up, t2), (x_swap, t2), *lane(s_piece[:part]), (core_swap, tx0),
        work=[(functools.partial(enter_grad, slots=slots), g_pieces, target_row, gate_row)],
    )
    t3, tx2 = moved[:2]
    s_got, ctx0 = moved[2:-1], moved[-1]
    *rows_g, share = made[0]
    t_near = jnp.concatenate([t0, t1, t2, t3])
    moved, _, _, made = clock.slot(
        (x_swap, t3), (core_swap, t_near), *lane(s_piece[part:]), (core_swap, tx1),
        work=[(join, *fetched[1][2])] if two else [],
    )
    tx3, ct_near = moved[:2]
    s_got, ctx1 = s_got + moved[2:-1], moved[-1]
    gate_got = made
    if two:
        s_pieces = [s_piece, jnp.concatenate(s_got)]
    else:
        s_pieces = jnp.split(dp_gather(s_piece[None], 0), ndp)
        s_pieces = [value.reshape(s_piece.shape) for value in s_pieces]
    moved, _, _, made = clock.slot(
        (core_swap, tx2), (core_swap, tx3), feed=0.4,
        work=[(lambda *a: shared_weights(a, block_index, ff_pad), *s_pieces)],
    )
    s_both, s_down_w = made[0]
    t_pieces = [t0, t1, t2, t3, tx0, tx1, tx2, tx3, ct_near, ctx0, ctx1, *moved]

    _, _, _, made = clock.slot(
        work=[
            (functools.partial(dispatch, slots=slots), t_pieces, target_row),
            (hidden_shared, t_pieces, g_pieces, s_both, s_down_w),
        ],
        feed=3.0,
    )
    rows_x, (s_act, d_s_pre) = made
    if two:
        assert all(entry[1] == entry[0].shape[0] for entry in fetched)
        own, other = own_expert, [gate_got[0], join(*fetched[2][2]), down_got[0]]
    else:
        full = [dp_gather(own_expert[0], 0), dp_gather(own_expert[1], 0), dp_gather(own_expert[2], 1)]
        own = [full[0][:half], full[1][:half], full[2][:, :half]]
        other = [full[0][half:], full[1][half:], full[2][:, half:]]
    _, _, _, made = clock.slot(work=[(expert_hidden, rows_x, rows_g, own, other)])
    e_act, d_gate, d_up, d_down_away = made[0]
    if two:
        sent = [clock.add(d_down_away)]

    _, _, _, made = clock.slot(
        work=[(expert_back, d_gate, d_up, own, other, target_col, d_s_pre, s_both)], feed=1.35
    )
    near, near_x, far, far_x = made[0]
    moved, _, _, made = clock.slot((core_swap, far_x), work=[(contract, rows_x[1], d_gate)], feed=0.3)
    if two:
        sent.append(clock.add(low(made[0])))
    away = [low(wide(cut(near_x, k)) + wide(cut(moved[0], k))) for k in range(4)]
    moved, _, _, made = clock.slot(
        (x_swap, away[3]), (core_swap, far),
        feed=0.72,
        work=[(functools.partial(shared_gradient, part=ff_part), t_pieces, g_pieces, d_s_pre, s_act)],
    )
    d_shared = made[0].reshape(ndp, experts, shard, 3 * ff_part)
    home = [wide(cut(near, k)) + wide(cut(moved[1], k)) for k in range(4)]
    moved, _, _, made = clock.slot(
        (x_swap, away[2]), (z_down, low(home[3] + wide(moved[0]))),
        feed=0.8,
        work=[(expert_out, e_act, share, own, other, target_col, s_act, s_down_w)],
    )
    o_near, o_near_x, o_far, o_far_x = made[0]
    s_away = d_shared[-1]
    moved, _, _, made = clock.slot(
        (x_swap, away[1]), (z_down, low(home[2] + wide(moved[0]) + wide(moved[1]))), (core_swap, o_far_x),
        *lane(s_away[:part]),
        work=[(contract, rows_x[1], d_up), (contract, e_act, rows_g[0])],
    )
    d_down_home = made[1]
    if two:
        sent.append(clock.add(low(made[0])))
    s_got = moved[3:]
    o_away = [low(wide(cut(o_near_x, k)) + wide(cut(moved[2], k))) for k in range(4)]
    moved, _, _, made = clock.slot(
        (x_swap, away[0]), (z_down, low(home[1] + wide(moved[0]) + wide(moved[1]))), (core_swap, o_far),
        *lane(s_away[part:]),
        work=[(contract, rows_x[0], d_gate)],
    )
    d_gate_home = made[0]
    s_got += moved[3:]
    o_home = [wide(cut(o_near, k)) + wide(cut(moved[2], k)) for k in range(4)]
    if two:
        d_shared = low(wide(d_shared[0]) + wide(jnp.concatenate(s_got)))
    else:
        d_shared = dp_scatter(d_shared)[0]
    d_shared = d_shared.reshape(4, 2, 2, shard, 3 * ff_part)
    d_mid_normed = turn(home[0] + wide(moved[0]) + wide(moved[1]))
    d_mid_in, d_gain_mid = rms_back(d_mid_normed, mid, scale_mid, gain_mid)
    d_mid = cotangent + d_mid_in

    a0 = low(d_mid)
    moved, _, _, made = clock.slot(
        (z_up, a0), (x_swap, o_away[3]), feed=0.7, work=[(contract, rows_x[0], d_up)]
    )
    a1, ox = moved
    d_up_home = made[0]
    s_kept, s_away = at(d_shared, x, 1), at(d_shared, 1 - x, 1)
    moved, _, _, _ = clock.slot(
        (z_up, a1), (x_swap, o_away[2]), (z_down, low(o_home[3] + wide(ox))), (x_swap, o_away[0]), feed=0.9
    )
    a2, ox, o_sum, ox0 = moved
    o_sum = low(o_home[2] + wide(ox) + wide(o_sum))
    moved, _, _, _ = clock.slot((z_up, a2), (x_swap, o_away[1]), (z_down, o_sum), (x_swap, s_away), feed=0.95)
    a3, ox, o_sum, s_got = moved
    o_sum = low(o_home[1] + wide(ox) + wide(o_sum))
    d_shared = jnp.stack([s_kept, s_got], axis=1)
    a_near = jnp.concatenate([a0, a1, a2, a3])
    moved, _, _, _ = clock.slot((core_swap, a_near), feed=0.35)
    a_pieces = [a0, a1, a2, a3, moved[0]]
    backward = functools.partial(attention_backward, lat_rows=lat_rows)
    moved, _, _, made = clock.slot(
        (z_two, at(d_shared, (z + 2) % 4, 0)), (z_up, at(d_shared, (z + 1) % 4, 0)),
        (z_down, at(d_shared, (z + 3) % 4, 0)), (z_down, o_sum),
        feed=1.4,
        work=[(backward, scalars, x_pieces, a_pieces, saved, d_gain_mid.reshape(1, width), table)],
    )
    d_shared = jnp.stack([at(d_shared, z, 0), moved[1], moved[0], moved[2]])
    o_last = o_home[0] + wide(ox0) + wide(moved[3])
    d_norm, d_head, d_wl = made[0]
    same_x = [[i for i in range(experts) if i // 2 % 2 == side] for side in range(2)]
    d_normed = lax.psum_scatter(d_norm, "expert", scatter_dimension=0, axis_index_groups=same_x, tiled=True)

    if not two:
        d_head = d_head.reshape(ndp, 4, 2, 2 * shard, W_COLS)
        d_wl = d_wl.reshape(ndp, 4, 2, 2, shard, -1)
    s_kept, s_away = at(d_shared, core, 2), at(d_shared, 1 - core, 2)

    def add_received(home, *pieces):
        return home + wide(jnp.concatenate(pieces))

    if two:
        moved, _, _, made = clock.slot(
            (x_swap, d_head[4:8]), (dp_swap, d_head[12:]), (core_swap, d_wl[1]), (core_swap, s_away),
            work=[(add_received, d_down_home, *sent[0][2])],
        )
        d_down = made[0]
        first = (wide(d_head[:4]) + wide(moved[0])).reshape(ndp, 2, 2 * shard, W_COLS)
        second = (wide(d_head[8:12]) + wide(moved[1])).reshape(2, 2, 2 * shard, W_COLS)
        d_wl = (wide(d_wl[0]) + wide(moved[2])).reshape(ndp, 4, 2, shard, -1)
        d_shared = jnp.stack([s_kept, moved[3]], axis=2)
        moved, _, _, made = clock.slot(
            (dp_swap, low(at(first, 1 - dp, 0))), (x_swap, low(at(second, 1 - x, 1))),
            (x_swap, low(at(d_wl, 1 - x, 2))), feed=0.65,
            work=[(add_received, d_gate_home, *sent[1][2])],
        )
        d_gate_all = made[0]
        first = at(first, dp, 0) + wide(moved[0])
        second = at(second, x, 1) + wide(moved[1])
        d_wl = at(d_wl, x, 2) + wide(moved[2])
        d_head = low(jnp.concatenate([first, second]))
    else:
        d_head = wide(at(d_head, x, 2)) + wide(x_swap(at(d_head, 1 - x, 2)))
        d_head = dp_scatter(low(d_head))[0]
        d_wl = wide(at(d_wl, core, 3)) + wide(core_swap(at(d_wl, 1 - core, 3)))
        d_wl = at(d_wl, x, 2) + wide(x_swap(low(at(d_wl, 1 - x, 2))))
        d_shared = jnp.stack([s_kept, core_swap(s_away)], axis=2)
        o_last = o_last + wide(z_down(o_sum))
    d_shared = d_shared.reshape(experts, shard, 3 * ff_part)
    moved, _, _, _ = clock.slot(
        (z_two, at(d_head, (z + 2) % 4, 0)), (z_down, at(d_head, (z + 3) % 4, 0)),
        (z_up, at(d_head, (z + 1) % 4, 0)),
        *(lane(low(at(d_wl, 1 - dp, 0))) if two else []), feed=3.0,
    )
    d_head = jnp.stack([at(d_head, z, 0), moved[1], moved[0], moved[2]]).reshape(4, 2, shard, W_COLS)
    d_wl = at(d_wl, dp, 0) + wide(moved[3]) if two else wide(dp_scatter(low(d_wl))[0])
    out = low(mid + turn(o_last))
    moved, _, ended, made = clock.slot(
        (core_swap, at(d_head, 1 - core, 1)), (z_two, low(at(d_wl, (z + 2) % 4, 0))),
        (z_down, low(at(d_wl, (z + 3) % 4, 0))), (z_up, low(at(d_wl, (z + 1) % 4, 0))),
        end=[d_normed], work=[(add_received, d_up_home, *sent[2][2])] if two else [],
    )
    d_up_all = made[0] if two else None
    d_head = jnp.stack([at(d_head, core, 1), moved[0]], axis=1).reshape(pairs, shard, W_COLS)
    d_wl = at(d_wl, z, 0) + wide(moved[1]) + wide(moved[2]) + wide(moved[3])
    d_normed = wide(ended[0])

    if two:
        assert all(entry[1] == entry[0].shape[0] for entry in sent)
        d_expert = [d_gate_all, d_up_all, d_down]
    else:
        d_expert = [
            wide(dp_scatter(low(jnp.concatenate([contract(value, d) for value in rows_x]))))
            for d in (d_gate, d_up)
        ]
        d_expert.append(wide(dp_scatter(low(jnp.concatenate([contract(e_act, value) for value in rows_g], axis=1)), 1)))
    d_in, _ = rms_back(d_normed, xf, rms_scale(xf), gain_in)
    d_tokens = d_mid + d_in
    d_shared = wide(reorder([d_shared], block_index)[0])
    grad_sg, grad_su = (
        d_shared[:, :, i * ff_part : (i + 1) * ff_part].transpose(1, 0, 2).reshape(shard, ff_s) for i in range(2)
    )
    grad_sd = d_shared[:, :, 2 * ff_part :].transpose(0, 2, 1).reshape(ff_s, shard)
    pair_number = jnp.arange(pairs, dtype=jnp.int32)
    pair_index = ((pair_number // 2 + 4 - z) % 4) * 2 + (pair_number % 2 ^ core)
    d_head = wide(reorder([d_head], pair_index)[0])
    grad_wq = jnp.concatenate(
        [
            d_head[..., : 2 * HD].reshape(pairs, shard, 2, HD),
            d_head[..., 2 * HD : Q_COLS].reshape(pairs, shard, 2, RD),
        ],
        axis=3,
    )
    grad_wq = grad_wq.transpose(1, 0, 2, 3).reshape(shard, HEADS * (HD + RD))
    grad_wo = d_head[..., Q_COLS : Q_COLS + O_COLS].transpose(0, 2, 1).reshape(HEADS * VD, shard)
    grad_we = d_head[..., Q_COLS + O_COLS :].reshape(pairs, groups, lat_rows, E_COLS).transpose(2, 0, 1, 3)
    grad_we = grad_we.reshape(lat_rows, HEADS * (HD + VD))
    return (
        out,
        d_tokens,
        d_wl[:, lat_cols],
        d_wl[:lat_rows, lat_cols + 2],
        d_wl[:, lat_cols + 1],
        grad_wq,
        d_wl[:, :lat_cols],
        grad_we,
        grad_wo,
        grad_sg,
        grad_su,
        grad_sd,
        d_expert[0][None],
        d_expert[1][None],
        d_expert[2][None],
    )


def solution(mesh):
    rows = P(("dp", "expert"), None)
    vector = P(("dp", "expert"))
    columns = P(None, ("dp", "expert"))
    by_row = P("expert", "dp", None)
    by_column = P("expert", None, "dp")
    return jax.shard_map(
        local,
        mesh=mesh,
        in_specs=(
            rows, rows, rows, rows, vector, vector, vector, rows, rows, rows, columns, rows, rows, columns, by_row,
            by_row, by_column, rows,
        ),
        out_specs=(
            rows, rows, vector, vector, vector, rows, rows, rows, columns, rows, rows, columns, by_row, by_row,
            by_column,
        ),
        check_vma=False,
    )
```

```python
import functools

import jax
import jax.numpy as jnp
import ml_dtypes
import numpy as np
from jax import lax
from jax.experimental import pallas as pl
from jax.experimental.pallas import tpu as pltpu
from jax.sharding import PartitionSpec as P

HEADS = 16
HD = 128
RD = 64
VD = 128
LAT = 512
TOP = 6
EPS = 1e-06
CHUNK = 256
SCALE = (HD + RD) ** (-0.5)
BF = jnp.bfloat16
F32 = jnp.float32
VMEM_LIMIT = 60 * 1024 * 1024
Q_COLS = 2 * (HD + RD)
O_COLS = 2 * VD
E_COLS = 128
LAT_AT = Q_COLS
ROT_AT = Q_COLS + LAT
PROJ = ROT_AT + 128
W_COLS = Q_COLS + O_COLS + E_COLS
HIDDEN_TILE = 256


def matmul(left, right):
    return jnp.dot(left, right, preferred_element_type=F32)


def mat_trans(left, right):
    return lax.dot_general(left, right, (((1,), (1,)), ((), ())), preferred_element_type=F32)


def contract(left, right):
    return lax.dot_general(left, right, (((0,), (0,)), ((), ())), preferred_element_type=F32)


def rms_scale(values):
    return lax.rsqrt(jnp.mean(values * values, axis=-1, keepdims=True) + EPS)


def rms_back(incoming, values, scale, gain):
    scaled = incoming * gain
    inner = jnp.mean(scaled * values, axis=-1, keepdims=True)
    grad_in = scale * (scaled - values * scale * scale * inner)
    grad_gain = jnp.sum(incoming * values * scale, axis=0)
    return (grad_in, grad_gain)


def low(value):
    return value.astype(BF)


def wide(value):
    return value.astype(F32)


def move(value, to):
    return lax.ppermute(value, "expert", [(i, to(i)) for i in range(16)])


def z_up(value):
    return move(value, lambda i: (i + 4) % 16)


def z_down(value):
    return move(value, lambda i: (i + 12) % 16)


def z_two(value):
    return move(value, lambda i: (i + 8) % 16)


def x_swap(value):
    return move(value, lambda i: i ^ 2)


def core_swap(value):
    return move(value, lambda i: i ^ 1)


class Clock:
    def __init__(self, go):
        self.last = ()
        self.go = go
        self.queue = []

    def add(self, array):
        self.queue.append([array, 0, []])
        return self.queue[-1]

    def next_rows(self, size):
        moves, entries = [], []
        for entry in self.queue:
            array, start, _ = entry
            total = array.shape[0]
            line = array.size // total * array.dtype.itemsize
            count = round(size / line / 32) * 32
            if start == total or count < 64:
                continue
            stop = start + count
            stop = total if total - stop < 64 else stop
            entry[1] = stop
            moves.append((self.go, array[start:stop]))
            entries.append(entry)
            size -= (stop - start) * line
        return moves, entries

    def slot(self, *moves, begin=(), end=(), work=(), feed=0, lasting=0, fed_before=()):
        later, later_entries = self.next_rows(lasting * 1e6)
        begin = list(begin) + later
        waited = [entry[2][place] for entry, place in fed_before]
        end = waited + list(end)
        fed, entries = self.next_rows(feed * 1e6)
        moves = fed + list(moves)
        count, late = len(moves), len(moves) + len(begin)
        args, tree = jax.tree.flatten([list(rest) for _, *rest in work])
        values = [value for _, value in moves + list(begin)]
        tied = lax.optimization_barrier(tuple(values + args) + self.last)
        moved = [go(value) for (go, _), value in zip(moves, tied)]
        begun = [go(value) for (go, _), value in zip(begin, tied[count:])]
        args = jax.tree.unflatten(tree, tied[late : late + len(args)])
        made = [job[0](*some) for job, some in zip(work, args)]
        flat, tree = jax.tree.flatten(made)
        self.last = lax.optimization_barrier(tuple(moved) + tuple(end) + tuple(flat))
        moved, ended = list(self.last[:count]), list(self.last[count : count + len(end)])
        for entry in entries:
            entry[2].append(moved.pop(0))
        for entry, place in fed_before:
            entry[2][place] = ended.pop(0)
        self.lasting = []
        for entry in later_entries:
            self.lasting.append((entry, len(entry[2])))
            entry[2].append(begun.pop(len(begun) - len(later_entries) + len(self.lasting) - 1))
        return moved, begun, ended, jax.tree.unflatten(tree, self.last[count + len(end) :])


    def tie(self, value):
        return lax.optimization_barrier((value,) + self.last)[0]


def joined(entry):
    assert entry[1] == entry[0].shape[0]
    return jnp.concatenate(entry[2], axis=0)


def at(value, index, axis):
    return lax.dynamic_index_in_dim(value, index, axis, keepdims=False)


def whole_call(kernel, args, outs, scratch=(), flops=0, scalars=None):
    size = sum(a.size * a.dtype.itemsize for a in list(args) + list(outs))
    vmem = pl.BlockSpec(memory_space=pltpu.VMEM)
    specs = [vmem] * len(args)
    if scalars is not None:
        args = [scalars] + list(args)
        specs = [pl.BlockSpec(memory_space=pltpu.SMEM)] + specs
    return pl.pallas_call(
        kernel,
        in_specs=specs,
        out_specs=[vmem] * len(outs),
        out_shape=list(outs),
        scratch_shapes=list(scratch),
        compiler_params=pltpu.CompilerParams(vmem_limit_bytes=VMEM_LIMIT),
        cost_estimate=pl.CostEstimate(flops=flops, bytes_accessed=size, transcendentals=0),
    )(*args)


def shaped(shape, kind):
    return jax.ShapeDtypeStruct(shape, kind)


def reorder_kernel(count, parts, index_ref, *refs):
    for in_ref, out_ref in zip(refs[: len(refs) // 2], refs[len(refs) // 2 :]):
        pad = out_ref.shape[2] // parts
        width = in_ref.shape[2] // parts
        for i in range(count):
            value = in_ref[index_ref[i]]
            if pad == width:
                out_ref[i] = value
            else:
                spare = jnp.zeros((value.shape[0], pad - width), value.dtype)
                for part in range(parts):
                    cut = value[:, part * width : (part + 1) * width]
                    out_ref[i, :, part * pad : (part + 1) * pad] = jnp.concatenate([cut, spare], axis=1)


def shared_kernel_in(count, parts, index_ref, *refs):
    in_refs, (both_ref, down_ref) = refs[:-2], refs[-2:]
    pad = down_ref.shape[1]
    for k, in_ref in enumerate(in_refs):
        rows, columns = in_ref.shape[1], in_ref.shape[2] // parts
        spare = jnp.zeros((rows, pad - columns), in_ref.dtype)
        for i in range(count):
            value = in_ref[index_ref[i]]
            line = slice((k * count + i) * rows, (k * count + i + 1) * rows)
            for part in range(parts):
                cut = jnp.concatenate([value[:, part * columns : (part + 1) * columns], spare], axis=1)
                if part < parts - 1:
                    both_ref[line, part * pad : (part + 1) * pad] = cut
                else:
                    down_ref[line, :] = cut


def shared_weights(arrays, index, pad):
    rows = sum(a.shape[0] * a.shape[1] for a in arrays)
    outs = [shaped((rows, 2 * pad), BF), shaped((rows, pad), BF)]
    return whole_call(functools.partial(shared_kernel_in, index.shape[0], 3), arrays, outs, scalars=index)


def reorder(arrays, index, parts=1, pad=0):
    count = index.shape[0]
    outs = [shaped(a.shape[:2] + (a.shape[2] if not pad else parts * pad,), a.dtype) for a in arrays]
    return whole_call(functools.partial(reorder_kernel, count, parts), arrays, outs, scalars=index)


def unpack_kernel(index_ref, in_ref, wq_ref, wo_ref, we_ref):
    rows = we_ref.shape[0]
    for a in range(in_ref.shape[0]):
        value = wide(in_ref[index_ref[a]])
        parts = [value[:, :HD], value[:, 2 * HD : 2 * HD + RD], value[:, HD : 2 * HD], value[:, 2 * HD + RD : Q_COLS]]
        wq_ref[:, a * Q_COLS : (a + 1) * Q_COLS] = jnp.concatenate(parts, axis=1)
        wo_ref[:, a * O_COLS : (a + 1) * O_COLS] = value[:, Q_COLS : Q_COLS + O_COLS]
        for g in range(4):
            we_ref[:, (4 * a + g) * E_COLS : (4 * a + g + 1) * E_COLS] = value[g * rows : (g + 1) * rows, Q_COLS + O_COLS :]


def unpack(blocks, index, rows):
    pairs, shard, _ = blocks.shape
    outs = [
        shaped((shard, pairs * Q_COLS), F32), shaped((shard, pairs * O_COLS), F32), shaped((rows, 4 * pairs * E_COLS), F32)
    ]
    return whole_call(unpack_kernel, [blocks], outs, scalars=index)


def swap_halves(values):
    lane = lax.broadcasted_iota(jnp.int32, values.shape, 1)
    return jnp.where(
        lane % RD < RD // 2, pltpu.roll(values, 2 * RD - RD // 2, 1), pltpu.roll(values, RD // 2, 1)
    )


def probabilities(q_main, q_rot, k_main, k_rot, allowed):
    scores = (mat_trans(q_main, k_main) + mat_trans(q_rot, k_rot)) * SCALE
    scores = jnp.where(allowed, scores, -1e30)
    expo = jnp.exp(scores - jnp.max(scores, axis=-1, keepdims=True))
    return expo / jnp.sum(expo, axis=-1, keepdims=True)


def allowed_pairs(id_col, id_row):
    shape = (id_col.shape[0], id_row.shape[1])
    key = lax.broadcasted_iota(jnp.int32, shape, 1)
    query = lax.broadcasted_iota(jnp.int32, shape, 0)
    return (id_col == id_row) & (key <= query)


def angle_table(rows):
    freq = np.power(np.float32(10000.0), np.float32(-2.0) * np.arange(RD // 2, dtype=np.float32) / np.float32(RD))
    theta = np.arange(rows, dtype=np.float32)[:, None] * freq.astype(np.float32)
    cosine, sine = np.cos(theta), np.sin(theta)
    terms = []
    for value in (np.concatenate([cosine] * 4, axis=1), np.concatenate([-sine, sine, -sine, sine], axis=1)):
        rest = value.astype(np.float32)
        for _ in range(3):
            term = rest.astype(ml_dtypes.bfloat16)
            terms.append(term)
            rest = rest - term.astype(np.float32)
    return np.concatenate(terms, axis=1)


def chunk_layout(facts_ref, j, rows, shape):
    count = CHUNK // rows
    number = lax.broadcasted_iota(jnp.int32, shape, 0 if shape[0] == CHUNK else 1)
    block, place = number // rows, number % rows
    doc, start, ends = 0, 0, [0] * count
    for k in range(3):
        lengths = [facts_ref[4 + (j * count + b) * 4 + k] for b in range(count)]
        ends = [end + length for end, length in zip(ends, lengths)]
        end, length = ends[-1], lengths[-1]
        for b in range(count - 2, -1, -1):
            end = jnp.where(block == b, ends[b], end)
            length = jnp.where(block == b, lengths[b], length)
        passed = place >= end
        doc = doc + passed.astype(jnp.int32)
        start = start + jnp.where(passed, length, 0)
    return place - start, doc + 4 * block


def chunk_tables(facts_ref, table_ref, j):
    rows = table_ref.shape[0]
    position, id_col = chunk_layout(facts_ref, j, rows, (CHUNK, 1))
    id_row = chunk_layout(facts_ref, j, rows, (1, CHUNK))[1]
    hot = low(lax.broadcasted_iota(jnp.int32, (CHUNK, rows), 1) == position)
    terms = matmul(hot, table_ref[...])
    cosine = terms[:, :128] + terms[:, 128:256] + terms[:, 256:384]
    sine = terms[:, 384:512] + terms[:, 512:640] + terms[:, 640:]
    return cosine, sine, allowed_pairs(id_col, id_row)


def pair(refs, j):
    pieces, start = [], 0
    for ref in refs:
        low_row, high_row = max(start, CHUNK * j), min(start + ref.shape[0], CHUNK * (j + 1))
        if low_row < high_row:
            pieces.append(ref[low_row - start : high_row - start, :])
        start += ref.shape[0]
    return pieces[0] if len(pieces) == 1 else jnp.concatenate(pieces, axis=0)


def forward_kernel(ndp, layout_of, pieces, count, split, place_ref, *refs):
    x_refs, refs = refs[:pieces], refs[pieces:]
    w_refs, refs = refs[: len(layout_of)], refs[len(layout_of) :]
    wl_refs, refs = refs[:count], refs[count:]
    we_ref, gains_ref, lg_ref, table_ref = refs[:4]
    near_ref, far_ref, q_ref, kr_ref, lat_ref, kv_ref, att_ref, wp_ref, wo_ref, exp_ref, gain_ref, mid_ref, lgo_ref = refs[4:]
    other_rows = [(ref, i) for ref in wl_refs for i in range(ref.shape[0])]
    dp, z, x, core = place_ref[0], place_ref[1], place_ref[2], place_ref[3]
    block = w_refs[0].shape[1]
    shard = block // 2
    lat_rows = jnp.zeros((4, 128), F32)
    spare = jnp.zeros((shard, 128 - RD), BF)
    turn = 0
    for w_ref, (far, j, first) in zip(w_refs, layout_of):
        y = j ^ dp if ndp == 2 else j
        for k in range(w_ref.shape[0]):
            row = ((y * 4 + lax.rem(z + 4 - first - k, 4)) * 2 + (x ^ far)) * block
            row = pl.multiple_of(row, block)
            wp_ref[pl.ds(row, block), :Q_COLS] = w_ref[k, :, :Q_COLS]
            wo_ref[pl.ds(row, block), :] = w_ref[k, :, Q_COLS : Q_COLS + O_COLS]
            if not split:
                continue
            here = pl.multiple_of(row + core * shard, shard)
            there = pl.multiple_of(row + (1 - core) * shard, shard)
            for at_row, lat in ((here, w_ref[k, :, W_COLS:]), (there, other_rows[turn][0][other_rows[turn][1]])):
                wp_ref[pl.ds(at_row, shard), LAT_AT : LAT_AT + 384] = lat[:shard, :]
                wp_ref[pl.ds(at_row, shard), LAT_AT + 384 :] = lat[shard:, :256]
            here_rows, there_rows = (
                wide(lat[shard : shard + 16, 256:]) for lat in (w_ref[k, :, W_COLS:], other_rows[turn][0][other_rows[turn][1]])
            )
            left = jnp.where(core == 0, here_rows[:1, :], there_rows[:1, :])
            right = jnp.where(core == 0, there_rows[:1, :], here_rows[:1, :])
            gain_ref[:, pl.ds(row, block)] = jnp.concatenate([left[:, :shard], right[:, :shard]], axis=1)
            mid_ref[:, pl.ds(row, block)] = jnp.concatenate([left[:, shard:], right[:, shard:]], axis=1)
            lat_rows = lat_rows + here_rows[1:5, :] + there_rows[1:5, :]
            turn += 1
            small = shard // 4
            for c in range(2):
                for g in range(4):
                    at_row = pl.multiple_of(row // 4 + c * small, small)
                    exp_ref[pl.ds(at_row, small), g * HD : (g + 1) * HD] = w_ref[
                        k, c * shard + g * small : c * shard + (g + 1) * small, Q_COLS + O_COLS : W_COLS
                    ]
    if not split:
        for i, (wl_ref, _) in enumerate(other_rows):
            wp_ref[i * shard : (i + 1) * shard, LAT_AT:] = jnp.concatenate([wl_ref[i, :shard, :], spare], axis=1)
        exp_ref[...] = we_ref[...]
        gain_ref[...] = gains_ref[:1, :]
        mid_ref[...] = gains_ref[1:2, :]
        lgo_ref[...] = lg_ref[...]
    else:
        lgo_ref[...] = jnp.concatenate([lat_rows[i : i + 1, :] for i in range(4)], axis=1)
    gain, lat_gain = gain_ref[...], lgo_ref[...]
    for j in range(4):
        rows = slice(CHUNK * j, CHUNK * (j + 1))
        xf = wide(pair(x_refs, j))
        normed = low(xf * rms_scale(xf) * gain)
        proj = matmul(normed, wp_ref[...])
        cosine, sine, allowed = chunk_tables(place_ref, table_ref, j)
        q_mix = proj[:, 2 * HD : Q_COLS]
        k_mix = proj[:, ROT_AT:]
        q_rot = low(q_mix * cosine + swap_halves(q_mix) * sine)
        k_rot = k_mix * cosine + swap_halves(k_mix) * sine
        k_turned = low(pltpu.roll(k_rot, RD, 1))
        k_rot = low(k_rot)
        q_main = low(proj[:, : 2 * HD])
        lat = proj[:, LAT_AT:ROT_AT]
        lat_ref[rows, :] = lat
        compressed = low(lat * rms_scale(lat) * lat_gain)
        expanded = low(matmul(compressed, exp_ref[...]))
        q_ref[rows, : 2 * HD] = q_main
        q_ref[rows, 2 * HD :] = q_rot
        kr_ref[rows, :] = k_rot
        kv_ref[rows, :] = expanded
        attended = []
        for head, k_side in ((0, k_rot), (1, k_turned)):
            k_main = expanded[:, 2 * head * HD : (2 * head + 1) * HD]
            values = expanded[:, (2 * head + 1) * HD : (2 * head + 2) * HD]
            probs = probabilities(q_main[:, head * HD : (head + 1) * HD], q_rot, k_main, k_side, allowed)
            attended.append(low(matmul(low(probs), values)))
        attended = jnp.concatenate(attended, axis=1)
        att_ref[rows, :] = attended
        put_half(near_ref, far_ref, j, 4, low(mat_trans(attended, wo_ref[...])))


def put_half(near_ref, far_ref, j, count, value):
    ref = near_ref if j < count // 2 else far_ref
    j = j % (count // 2)
    ref[j * CHUNK : (j + 1) * CHUNK, :] = value


def attention_forward(place, x_pieces, weights, layout_of, w_lat, w_exp, gains, lat_gain, table, split):
    own, width = x_pieces[0].shape
    rows = 8 * own
    args = list(x_pieces) + list(weights) + list(w_lat) + [w_exp, gains, lat_gain, table]
    outs = [shaped((rows // 2, width), BF)] * 2 + [
        shaped((rows, Q_COLS), BF),
        shaped((rows, 128), BF),
        shaped((rows, LAT), F32),
        shaped((rows, 4 * HD), BF),
        shaped((rows, O_COLS), BF),
        shaped((width, PROJ), BF),
        shaped((width, O_COLS), BF),
        shaped((LAT, 4 * HD), BF),
        shaped((1, width), F32),
        shaped((1, width), F32),
        shaped((1, LAT), F32),
    ]
    kernel = functools.partial(forward_kernel, lax.axis_size("dp"), layout_of, len(x_pieces), len(w_lat), split)
    flops = 2 * rows * width * (PROJ + O_COLS)
    out = whole_call(kernel, args, outs, flops=flops, scalars=place)
    return out[:2], out[2:]


def backward_kernel(pieces, count, lat_rows, place_ref, *refs):
    x_refs, g_refs, refs = refs[:pieces], refs[pieces : pieces + count], refs[pieces + count :]
    q_ref, kr_ref, lat_ref, kv_ref, att_ref, wp_ref, wo_ref, we_ref, gain_ref, mid_ref, lg_ref, dm_ref = refs[:12]
    table_ref, dn_ref, dw_ref, dl_ref, de_ref, acc_q, acc_o, acc_e, dg_ref, dlg_ref = refs[12:]
    split = len(dw_ref.shape) > 2
    dp, z, x, core = place_ref[0], place_ref[1], place_ref[2], place_ref[3]
    own = x_refs[0].shape[0]
    gain, w_exp, lat_gain = gain_ref[...], we_ref[...], lg_ref[...]

    def add(acc, value, first):
        acc[...] = value if first else acc[...] + value

    for j in range(4):
        rows = slice(CHUNK * j, CHUNK * (j + 1))
        xf = wide(pair(x_refs, j))
        whitened = xf * rms_scale(xf)
        normed = low(whitened * gain)
        lat = lat_ref[rows, :]
        lat_scale = rms_scale(lat)
        white_lat = lat * lat_scale
        grad = pair(g_refs, j)
        cosine, sine, allowed = chunk_tables(place_ref, table_ref, j)
        d_att = low(matmul(grad, wo_ref[...]))
        q_rot, k_rot = q_ref[rows, 2 * HD :], kr_ref[rows, :]
        k_turned = low(pltpu.roll(wide(k_rot), RD, 1))
        d_main, d_expanded = [], []
        dq_mix = None
        dk_mix = None
        for head, k_side in ((0, k_rot), (1, k_turned)):
            q_main = q_ref[rows, head * HD : (head + 1) * HD]
            k_main = kv_ref[rows, 2 * head * HD : (2 * head + 1) * HD]
            values = kv_ref[rows, (2 * head + 1) * HD : (2 * head + 2) * HD]
            probs = probabilities(q_main, q_rot, k_main, k_side, allowed)
            d_out = d_att[:, head * HD : (head + 1) * HD]
            d_prob = mat_trans(d_out, values)
            d_values = contract(low(probs), d_out)
            d_scores = low(probs * (d_prob - jnp.sum(probs * d_prob, axis=-1, keepdims=True)))
            d_main.append(matmul(d_scores, k_main) * SCALE)
            d_expanded += [contract(d_scores, q_main) * SCALE, d_values]
            dq_one = matmul(d_scores, k_side)
            dk_one = contract(d_scores, q_rot)
            dq_mix = dq_one if head == 0 else dq_mix + dq_one
            dk_mix = dk_one if head == 0 else dk_mix + pltpu.roll(dk_one, RD, 1)
        dq_mix = dq_mix * SCALE
        dk_mix = dk_mix * SCALE
        dq_mix = dq_mix * cosine - swap_halves(dq_mix) * sine
        dk_mix = dk_mix * cosine - swap_halves(dk_mix) * sine
        dk_mix = jnp.where(lax.broadcasted_iota(jnp.int32, dk_mix.shape, 1) < RD, dk_mix, 0.0)
        d_expanded = low(jnp.concatenate(d_expanded, axis=1))
        d_comp = mat_trans(d_expanded, w_exp)
        scaled = d_comp * lat_gain
        d_lat = lat_scale * (scaled - white_lat * jnp.mean(scaled * white_lat, axis=-1, keepdims=True))
        d_proj = low(jnp.concatenate(d_main + [dq_mix, d_lat, dk_mix], axis=1))
        d_normed = mat_trans(d_proj, wp_ref[...])
        part = low(d_normed)
        for k in range(2):
            piece = 2 * j + k
            place = lax.rem(z + 4 - piece % 4, 4) * 2 + (core ^ (piece // 4))
            dn_ref[pl.ds(pl.multiple_of(place * own, own), own), :] = part[k * own : (k + 1) * own, :]
        add(dg_ref, jnp.sum(d_normed * whitened, axis=0, keepdims=True), j == 0)
        add(dlg_ref, jnp.sum(d_comp * white_lat, axis=0, keepdims=True), j == 0)
        add(acc_q, contract(d_proj, normed), j == 0)
        add(acc_o, contract(att_ref[rows, :], grad), j == 0)
        add(acc_e, contract(low(white_lat * lat_gain), d_expanded), j == 0)
    shard = acc_q.shape[1] * lat_rows // LAT
    lane = lax.broadcasted_iota(jnp.int32, (LAT, acc_q.shape[1]), 1)
    line = lax.broadcasted_iota(jnp.int32, (LAT, acc_q.shape[1]), 0)
    spread = low((line // lat_rows == lane // shard) & (line % lat_rows == lane % shard))
    spread = matmul(low(jnp.broadcast_to(dlg_ref[...], (8, LAT))), spread)[:1, :]
    acc_q[ROT_AT + RD : ROT_AT + RD + 8, :] = jnp.concatenate(
        [dg_ref[...], dm_ref[...], spread, jnp.zeros((5, acc_q.shape[1]), F32)], axis=0
    )
    if not split:
        dw_ref[:, :Q_COLS] = low(acc_q[:Q_COLS, :].T)
        dw_ref[:, Q_COLS : Q_COLS + O_COLS] = low(acc_o[...].T)
        dl_ref[...] = low(acc_q[Q_COLS:, :].T)
        de_ref[...] = low(acc_e[...])
        return
    block = 2 * shard
    for number in range(acc_q.shape[1] // block):
        y, zz, xx = number // 8, number // 2 % 4, number % 2
        lanes = slice(number * block, (number + 1) * block)
        slot = (x ^ xx) * 4 + y * 2 + zz if zz < 2 else 8 + (dp ^ y) * 4 + (zz - 2) * 2 + xx
        dw_ref[slot, :, :Q_COLS] = low(acc_q[:Q_COLS, lanes].T)
        dw_ref[slot, :, Q_COLS : Q_COLS + O_COLS] = low(acc_o[:, lanes].T)
        for c in range(2):
            for g in range(4):
                row = c * shard + g * lat_rows
                i = number * 2 + c
                dw_ref[slot, row : row + lat_rows, Q_COLS + O_COLS :] = low(
                    acc_e[i * lat_rows : (i + 1) * lat_rows, g * HD : (g + 1) * HD]
                )
        both = low(acc_q[Q_COLS:, lanes].T)
        for c in range(2):
            dl_ref[core ^ c, number, :, :] = both[c * shard : (c + 1) * shard, :]


def attention_backward(place, x_pieces, g_pieces, saved, d_gain_mid, table, lat_rows):
    own, width = x_pieces[0].shape
    q, kr, lat, kv, att, wp, wo, w_exp, gain, mid, lat_gain = saved
    args = list(x_pieces) + list(g_pieces)
    args += [q, kr, lat, kv, att, wp, wo, w_exp, gain, mid, lat_gain, d_gain_mid, table]
    outs = [
        shaped((8 * own, width), BF),
        shaped((width, W_COLS), BF),
        shaped((width, PROJ - Q_COLS), BF),
        shaped((LAT, 4 * HD) if lat_rows % 16 else (16, 128), BF),
    ]
    shard = width * lat_rows // LAT
    if not lat_rows % 16:
        outs[1] = shaped((width // (2 * shard), 2 * shard, W_COLS), BF)
        outs[2] = shaped((2, width // (2 * shard), shard, PROJ - Q_COLS), BF)
    scratch = (
        pltpu.VMEM((PROJ, width), F32), pltpu.VMEM((O_COLS, width), F32), pltpu.VMEM((LAT, 4 * HD), F32),
        pltpu.VMEM((1, width), F32), pltpu.VMEM((1, LAT), F32),
    )
    flops = 2 * 8 * own * width * (2 * PROJ + 2 * O_COLS)
    kernel = functools.partial(backward_kernel, len(x_pieces), len(g_pieces), lat_rows)
    d_norm, d_head, d_wl, d_we = whole_call(kernel, args, outs, scratch, flops=flops, scalars=place)
    if lat_rows % 16:
        d_we = d_we.reshape(width // shard, lat_rows, 4, E_COLS).transpose(0, 2, 1, 3).reshape(width, E_COLS)
        d_head = jnp.concatenate([d_head[:, : Q_COLS + O_COLS], d_we], axis=1)
    return d_norm, d_head, d_wl


def routing_kernel(first, lanes, slots, me_ref, *refs):
    in_refs, (row_ref, gate_ref, col_ref) = refs[:4], refs[4:]
    mine = lax.broadcasted_iota(jnp.int32, (16, 128), 0) == me_ref[0]
    gates = []
    for ref, lane in zip(in_refs, lanes):
        for k in range(4):
            both = wide(ref[k, first : first + 32, lane : lane + 128])
            gates.append(jnp.sum(jnp.where(mine, both[:16, :] + both[16:, :], 0.0), axis=0, keepdims=True))
    gates = jnp.concatenate(gates, axis=0)
    routed = gates > 0.0
    line = lax.broadcasted_iota(jnp.int32, (128, 128), 0)
    column = lax.broadcasted_iota(jnp.int32, (128, 128), 1)
    before = low((line <= column) & (line // 64 == column // 64))
    count = matmul(low(routed), before)
    source = lax.broadcasted_iota(jnp.int32, (16, 128), 0)
    token = lax.broadcasted_iota(jnp.int32, (16, 128), 1)
    block = ((source % 2) * 2 + token // 64).astype(F32)
    target = jnp.where(routed, block * slots + count - 1.0, -1.0)
    turned = target.T
    for k in range(16):
        part = slice((k % 2) * 128, (k % 2 + 1) * 128)
        row_ref[k // 2, :, part] = target[k : k + 1, :].astype(jnp.int32)
        gate_ref[k // 2, :, part] = gates[k : k + 1, :]
        col_ref[k * 128 : (k + 1) * 128, :] = turned[:, k : k + 1].astype(jnp.int32)


def routing(me, arrays, first, lanes, slots):
    outs = [shaped((8, 1, CHUNK), jnp.int32), shaped((8, 1, CHUNK), F32), shaped((8 * CHUNK, 1), jnp.int32)]
    return whole_call(functools.partial(routing_kernel, first, lanes, slots), arrays, outs, scalars=me)


def enter_grad_kernel(slots, *refs):
    g_refs, (target_ref, gate_ref, rg0_ref, rg1_ref, rs_ref) = refs[:-5], refs[-5:]
    half = rg0_ref.shape[1]
    for j in range(8):
        grad = pair(g_refs, j)
        chosen = lax.broadcasted_iota(jnp.int32, (slots, CHUNK), 0) == target_ref[j]
        share = jnp.sum(jnp.where(chosen, gate_ref[j], 0.0), axis=1, keepdims=True)
        rs_ref[j * slots : (j + 1) * slots, :] = share
        value = low(matmul(low(chosen), grad) * share)
        rg0_ref[j * slots : (j + 1) * slots, :] = value[:, :half]
        rg1_ref[j * slots : (j + 1) * slots, :] = value[:, half:]


def dispatch_kernel(slots, *refs):
    t_refs, (target_ref, rx0_ref, rx1_ref) = refs[:-3], refs[-3:]
    half = rx0_ref.shape[1]
    for j in range(8):
        chosen = lax.broadcasted_iota(jnp.int32, (slots, CHUNK), 0) == target_ref[j]
        value = low(matmul(low(chosen), pair(t_refs, j)))
        rx0_ref[j * slots : (j + 1) * slots, :] = value[:, :half]
        rx1_ref[j * slots : (j + 1) * slots, :] = value[:, half:]


def hidden_shared_kernel(count, *refs):
    t_refs, g_refs, (sgu_ref, sd_ref, act_ref, pre_ref) = refs[:count], refs[count:-4], refs[-4:]
    third = sd_ref.shape[1]
    for j in range(8):
        rows = slice(j * CHUNK, (j + 1) * CHUNK)
        both = matmul(pair(t_refs, j), sgu_ref[...])
        gate_pre, up = both[:, :third], both[:, third:]
        d_act = matmul(pair(g_refs, j), sd_ref[...])
        sigma = jax.nn.sigmoid(gate_pre)
        swish = gate_pre * sigma
        act_ref[rows, :] = low(swish * up)
        pre_ref[rows, :third] = low(d_act * up * (sigma * (1.0 + gate_pre * (1.0 - sigma))))
        pre_ref[rows, third:] = low(d_act * swish)


def enter_grad(g_pieces, target, gate, slots):
    own, width = g_pieces[0].shape
    args = list(g_pieces) + [target, gate]
    outs = [shaped((slots, width // 2), BF)] * 2 + [shaped((slots, 1), F32)]
    flops = 32 * own * width * (slots // 8)
    return whole_call(functools.partial(enter_grad_kernel, slots // 8), args, outs, flops=flops)


def dispatch(t_pieces, target, slots):
    own, width = t_pieces[0].shape
    args = list(t_pieces) + [target]
    outs = [shaped((slots, width // 2), BF)] * 2
    flops = 32 * own * width * (slots // 8)
    return whole_call(functools.partial(dispatch_kernel, slots // 8), args, outs, flops=flops)


def hidden_shared(t_pieces, g_pieces, s_both, s_down):
    own, width = t_pieces[0].shape
    third = s_down.shape[1]
    args = list(t_pieces) + list(g_pieces) + [s_both, s_down]
    outs = [shaped((16 * own, third), BF), shaped((16 * own, 2 * third), BF)]
    return whole_call(functools.partial(hidden_shared_kernel, len(t_pieces)), args, outs, flops=96 * own * width * third)


def hidden_kernel(x0_ref, x1_ref, r0_ref, r1_ref, g0_ref, g1_ref, u0_ref, u1_ref, d0_ref, d1_ref, act_ref, dg_ref, du_ref, away_ref):
    step = 256
    for j in range(x0_ref.shape[0] // step):
        rows = slice(j * step, (j + 1) * step)
        x0, x1 = x0_ref[rows, :], x1_ref[rows, :]
        gate = matmul(x0, g0_ref[...]) + matmul(x1, g1_ref[...])
        up = matmul(x0, u0_ref[...]) + matmul(x1, u1_ref[...])
        d_act = mat_trans(r0_ref[rows, :], d0_ref[...]) + mat_trans(r1_ref[rows, :], d1_ref[...])
        sigma = jax.nn.sigmoid(gate)
        swish = gate * sigma
        act_ref[rows, :] = low(swish * up)
        dg_ref[rows, :] = low(d_act * up * (sigma * (1.0 + gate * (1.0 - sigma))))
        du_ref[rows, :] = low(d_act * swish)
    away_ref[...] = low(contract(act_ref[...], r1_ref[...]))


def tiled_call(kernel, steps, args, specs, outs, out_specs, scratch=(), flops=0, aliases=None):
    size = sum(a.size * a.dtype.itemsize for a in list(args) + list(outs))
    return pl.pallas_call(
        kernel,
        grid=(steps,),
        in_specs=specs,
        out_specs=out_specs,
        out_shape=outs,
        scratch_shapes=list(scratch),
        input_output_aliases=aliases or {},
        compiler_params=pltpu.CompilerParams(vmem_limit_bytes=VMEM_LIMIT),
        cost_estimate=pl.CostEstimate(flops=flops, bytes_accessed=size, transcendentals=0),
    )(*args)


def whole_spec(array):
    return pl.BlockSpec(array.shape, lambda i: (0,) * array.ndim)


def expert_hidden(rows_x, rows_g, own, other):
    slots, half = rows_x[0].shape
    hidden = own[0].shape[1]
    tile = HIDDEN_TILE
    by_column = pl.BlockSpec((half, tile), lambda i: (0, i))
    by_row = pl.BlockSpec((tile, half), lambda i: (i, 0))
    args = list(rows_x) + list(rows_g) + [own[0], other[0], own[1], other[1], own[2], other[2]]
    specs = [whole_spec(value) for value in args[:4]] + [by_column] * 4 + [by_row] * 2
    outs = [shaped((slots, hidden), BF)] * 3 + [shaped((hidden, half), BF)]
    out_specs = [pl.BlockSpec((slots, tile), lambda i: (0, i))] * 3 + [by_row]
    flops = 14 * slots * half * hidden
    return tiled_call(hidden_kernel, -(-hidden // tile), args, specs, outs, out_specs, flops=flops)


def back_kernel(per, dg_ref, du_ref, g0_ref, g1_ref, u0_ref, u1_ref, target_ref, left_ref, right_ref, *refs):
    out_refs, rows_ref = refs[:4], refs[4]
    steps = pl.num_programs(0) // 2
    own = pl.program_id(0) < steps

    @pl.when(own)
    def _():
        rows_ref[...] = low(mat_trans(dg_ref[...], g0_ref[...]) + mat_trans(du_ref[...], u0_ref[...]))

    @pl.when(jnp.logical_not(own))
    def _():
        rows_ref[...] = low(mat_trans(dg_ref[...], g1_ref[...]) + mat_trans(du_ref[...], u1_ref[...]))

    right = right_ref[...]
    for j in range(8):
        hot = low(lax.broadcasted_iota(jnp.int32, (CHUNK, per), 1) == target_ref[j * CHUNK : (j + 1) * CHUNK, :])
        out = matmul(hot, rows_ref[j * per : (j + 1) * per, :])
        out = low(out + mat_trans(left_ref[j * CHUNK : (j + 1) * CHUNK, :], right))
        out_refs[j // 2][(j % 2) * CHUNK : (j % 2 + 1) * CHUNK, :] = out


def expert_back(d_gate, d_up, own, other, target, left, right):
    slots, hidden = d_gate.shape
    rows, columns = left.shape
    width = right.shape[0]
    tile = 256
    steps = width // tile // 2
    near = pl.BlockSpec((tile, hidden), lambda i: (jnp.minimum(i, steps - 1), 0))
    far = pl.BlockSpec((tile, hidden), lambda i: (jnp.maximum(i - steps, 0), 0))
    args = [d_gate, d_up, own[0], other[0], own[1], other[1], target, left, right]
    specs = [whole_spec(d_gate), whole_spec(d_up)] + [near, far] * 2
    specs += [whole_spec(target), whole_spec(left), pl.BlockSpec((tile, columns), lambda i: (i, 0))]
    outs = [shaped((rows // 4, width), BF)] * 4
    out_specs = [pl.BlockSpec((rows // 4, tile), lambda i: (0, i))] * 4
    flops = 4 * slots * width * hidden + 2 * rows * width * (columns + slots // 8)
    return tiled_call(
        functools.partial(back_kernel, slots // 8), 2 * steps, args, specs, outs, out_specs,
        (pltpu.VMEM((slots, tile), BF),), flops=flops,
    )


def out_kernel(per, act_ref, share_ref, d0_ref, d1_ref, target_ref, left_ref, right_ref, *refs):
    out_refs, rows_ref = refs[:4], refs[4]
    steps = pl.num_programs(0) // 2
    own = pl.program_id(0) < steps

    @pl.when(own)
    def _():
        rows_ref[...] = low(matmul(act_ref[...], d0_ref[...]) * share_ref[...])

    @pl.when(jnp.logical_not(own))
    def _():
        rows_ref[...] = low(matmul(act_ref[...], d1_ref[...]) * share_ref[...])

    right = right_ref[...]
    for j in range(8):
        hot = low(lax.broadcasted_iota(jnp.int32, (CHUNK, per), 1) == target_ref[j * CHUNK : (j + 1) * CHUNK, :])
        out = matmul(hot, rows_ref[j * per : (j + 1) * per, :])
        out = low(out + mat_trans(left_ref[j * CHUNK : (j + 1) * CHUNK, :], right))
        out_refs[j // 2][(j % 2) * CHUNK : (j % 2 + 1) * CHUNK, :] = out


def expert_out(act, share, own, other, target, left, right):
    slots, hidden = act.shape
    rows, columns = left.shape
    width = right.shape[0]
    tile = 256
    steps = width // tile // 2
    args = [act, share, own[2], other[2], target, left, right]
    specs = [
        whole_spec(act), whole_spec(share),
        pl.BlockSpec((hidden, tile), lambda i: (0, jnp.minimum(i, steps - 1))),
        pl.BlockSpec((hidden, tile), lambda i: (0, jnp.maximum(i - steps, 0))),
        whole_spec(target), whole_spec(left), pl.BlockSpec((tile, columns), lambda i: (i, 0)),
    ]
    outs = [shaped((rows // 4, width), BF)] * 4
    out_specs = [pl.BlockSpec((rows // 4, tile), lambda i: (0, i))] * 4
    flops = 2 * slots * width * hidden + 2 * rows * width * (columns + slots // 8)
    return tiled_call(
        functools.partial(out_kernel, slots // 8), 2 * steps, args, specs, outs, out_specs,
        (pltpu.VMEM((slots, tile), BF),), flops=flops,
    )


def shared_kernel(part, count, *refs):
    t_refs, g_refs, (pre_ref, act_ref, out_ref, acc_t, acc_g) = refs[:count], refs[count:-5], refs[-5:]
    pad = act_ref.shape[1]
    for j in range(8):
        rows = slice(j * CHUNK, (j + 1) * CHUNK)
        by_tok = contract(pre_ref[rows, :], pair(t_refs, j))
        by_grad = contract(act_ref[rows, :], pair(g_refs, j))
        acc_t[...] = by_tok if j == 0 else acc_t[...] + by_tok
        acc_g[...] = by_grad if j == 0 else acc_g[...] + by_grad
    parts = [acc_t[:part, :], acc_t[pad : pad + part, :], acc_g[:part, :]]
    spare = -3 * part % 128
    if spare:
        parts.append(jnp.zeros((spare, acc_t.shape[1]), F32))
    out_ref[...] = low(jnp.concatenate(parts, axis=0).T[:, : 3 * part])


def shared_gradient(t_pieces, g_pieces, pre, act, part):
    own, width = t_pieces[0].shape
    args = list(t_pieces) + list(g_pieces) + [pre, act]
    outs = [shaped((width, 3 * part), BF)]
    scratch = (pltpu.VMEM((pre.shape[1], width), F32), pltpu.VMEM((act.shape[1], width), F32))
    flops = 32 * own * width * (pre.shape[1] + act.shape[1])
    return whole_call(functools.partial(shared_kernel, part, len(t_pieces)), args, outs, scratch, flops=flops)[0]


def local(
    tokens, lengths, routes, gates, norm_in, latent_gain, norm_mid, w_query, w_latent, w_expand, w_output,
    shared_gate, shared_up, shared_down, expert_gate, expert_up, expert_down, cotangent,
):
    micro = lengths.shape[0]
    own_rows, width = tokens.shape
    rows = own_rows // micro
    experts = lax.axis_size("expert")
    ndp = lax.axis_size("dp")
    two = ndp == 2
    cap = rows * TOP * 4 // (3 * experts)
    blocks = experts * micro
    all_rows = experts * own_rows
    devices = ndp * experts
    shard = width // devices
    lat_rows = w_expand.shape[0]
    lat_cols = w_latent.shape[1]
    ff_s = shared_gate.shape[1]
    ff_part = ff_s // experts
    ff_pad = -(-ff_part // 128) * 128
    half = width // 2
    me = lax.axis_index("expert")
    dp = lax.axis_index("dp")
    core, x, z = me % 2, (me // 2) % 2, me // 4

    def turn(value):
        if not two:
            return value
        swapped = jnp.concatenate([value[..., half:], value[..., :half]], axis=-1)
        return jnp.where(dp == 1, swapped, value)

    def dp_swap(value):
        return lax.ppermute(value, "dp", [(0, 1), (1, 0)])

    clock = Clock(dp_swap)

    def lane(value):
        return [(dp_swap, value)] if two else []

    def dp_gather(value, axis):
        return lax.all_gather(value, "dp", axis=axis, tiled=True)

    def dp_scatter(value, axis=0):
        return lax.psum_scatter(value, "dp", scatter_dimension=axis, tiled=True)

    def cut(value, k):
        return value[k * own_rows : (k + 1) * own_rows]

    number = jnp.arange(experts, dtype=jnp.int32)
    near_z, near_x, near_c = number % 4, (number // 4) % 2, number // 8
    row_index = ((z + 4 - near_z) % 4) * 4 + (near_x ^ x) * 2 + (near_c ^ core)
    few_index = jnp.concatenate([row_index[:4], row_index[8:12]])
    n_z, n_x, n_c = number // 4, (number // 2) % 2, number % 2
    block_index = ((z + 4 - n_z) % 4) * 4 + (n_x ^ x) * 2 + (n_c ^ core)

    pairs = HEADS // 2
    groups = shard // lat_rows
    piece = w_query.reshape(shard, pairs, 2, HD + RD).transpose(1, 0, 2, 3)
    piece = jnp.concatenate(
        [
            piece[..., :HD].reshape(pairs, shard, 2 * HD),
            piece[..., HD:].reshape(pairs, shard, 2 * RD),
            w_output.reshape(pairs, O_COLS, shard).transpose(0, 2, 1),
            w_expand.reshape(lat_rows, pairs, groups, E_COLS).transpose(1, 2, 0, 3).reshape(pairs, shard, E_COLS),
        ],
        axis=2,
    )
    piece = piece.reshape(4, 2, shard, W_COLS)
    kept, away = at(piece, core, 1), at(piece, 1 - core, 1)

    by_expert = jnp.sum(jnp.where(routes.T[None] == number[:, None, None], gates.T[None], 0.0), axis=1)
    gate_high = low(by_expert)
    gate_low = low(by_expert - wide(gate_high))

    def as_row(value):
        return jnp.pad(value.reshape(1, -1), ((0, 0), (0, own_rows - value.size)))

    small_rows = 48
    lat_gain_rows = lax.dynamic_update_slice(jnp.zeros((LAT,), BF), latent_gain, ((dp * experts + me) * lat_rows,))
    small = jnp.concatenate(
        [
            as_row(jnp.concatenate([norm_in, norm_mid])), lat_gain_rows.reshape(4, 128), as_row(low(lengths)),
            jnp.zeros((10, own_rows), BF), gate_high, gate_low,
        ],
        axis=0,
    )

    s_piece = jnp.concatenate(
        [
            shared_gate.reshape(shard, experts, ff_part).transpose(1, 0, 2),
            shared_up.reshape(shard, experts, ff_part).transpose(1, 0, 2),
            shared_down.reshape(experts, ff_part, shard).transpose(0, 2, 1),
        ],
        axis=2,
    ).reshape(4, 2, 2, shard, 3 * ff_part)
    own_expert = (expert_gate[0], expert_up[0], expert_down[0])
    x0 = tokens
    g0 = low(turn(cotangent))

    if two:
        fetched = [clock.add(value) for value in (own_expert[2], own_expert[0], own_expert[1])]
        wide_lat = jnp.pad(w_latent, ((0, 0), (0, 640 - lat_cols)))
        low_rows = jnp.pad(small, ((0, shard - small_rows), (0, 0)))
        lat = jnp.concatenate([wide_lat[:, :384], jnp.concatenate([wide_lat[:, 384:], low_rows], axis=1)], axis=0)
    else:
        lat = small
    s_kept, s_away = at(s_piece, core, 2), at(s_piece, 1 - core, 2)
    clock.slot(feed=0.65)
    moved, _, _, _ = clock.slot((core_swap, away), (core_swap, s_away), (z_up, x0), feed=0.59)
    x1 = moved[2]
    s_piece = jnp.stack([s_kept, moved[1]], axis=2)
    w_own = jnp.where(
        core == 0, jnp.concatenate([kept, moved[0]], axis=1), jnp.concatenate([moved[0], kept], axis=1)
    )
    if two:
        w_own = jnp.concatenate([w_own, jnp.broadcast_to(lat, (4,) + lat.shape)], axis=2)
    s_kept, s_away = at(s_piece, x, 1), at(s_piece, 1 - x, 1)
    moved, _, _, _ = clock.slot(
        (z_two, at(w_own, (z + 2) % 4, 0)),
        (z_up, at(w_own, (z + 1) % 4, 0)),
        (z_down, at(w_own, (z + 3) % 4, 0)),
        (x_swap, s_away),
        feed=1.17,
    )
    w_own = jnp.stack([at(w_own, z, 0), moved[1], moved[0], moved[2]])
    s_piece = jnp.stack([s_kept, moved[3]], axis=1)
    if two:
        lats = w_own[..., W_COLS:]
        facts = lats[:, shard : shard + small_rows, 256:]
    else:
        facts = jnp.stack([lat, z_up(lat), z_two(lat), z_down(lat)])

    moved, _, _, _ = clock.slot(
        (x_swap, w_own), *lane(w_own), (z_up, x1), (z_up, g0), (core_swap, lats if two else facts)
    )
    w_x, x2, g1, lat_other = moved[0], *moved[-3:]
    facts_few = jnp.concatenate([facts, lat_other[:, shard : shard + small_rows, 256:] if two else lat_other])
    lengths_few = facts_few[:, 5, : lengths.size].astype(jnp.int32).reshape(-1)
    scalars = jnp.concatenate([jnp.stack([dp, z, x, core]).astype(jnp.int32), lengths_few])
    table = jnp.asarray(angle_table(rows))
    s_two, s_up, s_down = (at(s_piece, (z + k) % 4, 0) for k in (2, 1, 3))
    if two:
        w_y = moved[1]
        moved, _, _, _ = clock.slot(
            (x_swap, w_y[:2]), (dp_swap, w_x[2:]), (z_up, x2),
            (core_swap, jnp.concatenate([w_x[..., W_COLS:], w_y[..., W_COLS:]])),
            (core_swap, jnp.concatenate([x0, x1])),
        )
        w_far, x3, lat_other_xy, cx01 = moved[:2], *moved[2:]
        lat_far = jnp.concatenate([w_far[0][..., W_COLS:], w_far[1][..., W_COLS:]])
        moved, _, _, _ = clock.slot(
            (core_swap, lat_far), (core_swap, jnp.concatenate([x2, x3])), (z_up, s_up), feed=0.5
        )
        cx23, s_up = moved[1:]
        weights = [w_own, w_x, w_y] + w_far
        layout_of = ((0, 0, 0), (1, 0, 0), (0, 1, 0), (1, 1, 0), (1, 1, 2))
        w_lat = [lat_other, lat_other_xy, moved[0]]
        w_exp = gains = gain_lat = jnp.zeros((8, 128), F32)
        route_from = [w_own, w_x, lat_other, lat_other_xy]
        route_lanes = (W_COLS + 256, W_COLS + 256, 256, 256)
    else:
        x3, s_up = z_up(x2), z_up(s_up)
        cx01, cx23 = core_swap(jnp.concatenate([x0, x1])), core_swap(jnp.concatenate([x2, x3]))
        near, far = dp_gather(w_own[None], 0), dp_gather(w_x[None], 0)
        weights = [near[i] for i in range(ndp)] + [far[i] for i in range(ndp)]
        layout_of = tuple((side, j, 0) for side in range(2) for j in range(ndp))
        w_lat = lax.all_gather(w_latent, ("dp", "expert"), axis=0)
        w_lat = [w_lat[i][None] for i in range(devices)]
        facts = lax.all_gather(small, ("dp", "expert"), axis=0)
        gains = wide(facts[:, 0, : 2 * shard]).reshape(devices, 2, shard).transpose(1, 0, 2).reshape(2, width)
        gain_lat = wide(facts[:, 1:5]).sum(axis=0).reshape(1, LAT)
        route_from = jnp.take(lax.dynamic_slice_in_dim(facts, dp * experts, experts, 0), row_index, axis=0)
        route_from = [route_from[4 * i : 4 * i + 4] for i in range(4)]
        route_lanes = (0, 0, 0, 0)
        w_exp = jnp.concatenate([value[..., Q_COLS + O_COLS :] for value in weights], axis=0)
        w_exp = w_exp.reshape(2, ndp, 4, 2 * shard, E_COLS).transpose(1, 2, 0, 3, 4)
        w_exp = w_exp.reshape(devices // 2, -1, E_COLS)
        chips = jnp.arange(devices // 2, dtype=jnp.int32)
        chip_index = chips // 8 * 8 + ((z + 4 - chips // 2 % 4) % 4) * 2 + (chips % 2 ^ x)
        w_exp = reorder([w_exp], chip_index)[0]
        w_exp = w_exp.reshape(devices, groups, lat_rows, E_COLS).transpose(0, 2, 1, 3).reshape(LAT, groups * E_COLS)
    slots = blocks * cap
    route = functools.partial(routing, first=(shard if two else 0) + 16, lanes=route_lanes, slots=cap)

    x_pieces = [x0, x1, x2, x3, cx01, cx23]
    moved, _, _, made = clock.slot(
        (x_swap, g0), (z_up, g1), (z_down, g0),
        feed=1.0,
        work=[
            (
                lambda *a: attention_forward(*a[:3], layout_of, *a[3:], split=two),
                scalars, x_pieces, weights, w_lat, w_exp, gains, gain_lat, table,
            )
        ],
    )
    gx0, g2, g3 = moved
    (part_near, part_far), saved = made[0]
    gain_in, gain_mid, gain_lat = saved[-3:]

    moved, _, _, _ = clock.slot((core_swap, part_far), (z_two, s_two), (z_down, s_down), feed=0.65)
    s_two, s_down = moved[1:]
    s_piece = jnp.stack([at(s_piece, z, 0), s_up, s_two, s_down]).reshape(experts, shard, 3 * ff_part)
    g_near = jnp.concatenate([g0, g1, g2, g3])
    terms = [wide(cut(part_near, k)) + wide(cut(moved[0], k)) for k in range(4)]
    moved, _, _, made = clock.slot(
        (z_down, low(terms[3])), (x_swap, g1), work=[(route, me.reshape(1), route_from)], feed=0.67
    )
    gx1 = moved[1]
    target_row, gate_row, target_col = made[0]
    moved, _, _, _ = clock.slot(
        (z_down, low(terms[2] + wide(moved[0]))), (x_swap, g2), (core_swap, g_near), feed=0.67
    )
    gx2, cg_near = moved[1:]
    moved, _, _, _ = clock.slot((z_down, low(terms[1] + wide(moved[0]))), (x_swap, g3), feed=0.67)
    gx3 = moved[1]
    xf = wide(tokens)
    mid = xf + terms[0] + wide(moved[0])
    scale_mid = rms_scale(mid)
    t0 = turn(low(mid * scale_mid * gain_mid))

    g_far = jnp.concatenate([gx0, gx1, gx2, gx3])
    join = lambda *pieces: jnp.concatenate(pieces, axis=0)
    moved, _, _, made = clock.slot(
        (z_up, t0), (x_swap, t0), work=[(join, *fetched[0][2])] if two else [], feed=0.67
    )
    t1, tx0 = moved
    down_got = made
    moved, _, _, _ = clock.slot((z_up, t1), (x_swap, t1), (core_swap, g_far), feed=0.67)
    t2, tx1, cg_far = moved
    g_pieces = [g0, g1, g2, g3, gx0, gx1, gx2, gx3, cg_near, cg_far]
    part = experts // 2
    moved, _, _, made = clock.slot(
        (z_up, t2), (x_swap, t2), *lane(s_piece[:part]), (core_swap, tx0),
        work=[(functools.partial(enter_grad, slots=slots), g_pieces, target_row, gate_row)],
    )
    t3, tx2 = moved[:2]
    s_got, ctx0 = moved[2:-1], moved[-1]
    *rows_g, share = made[0]
    t_near = jnp.concatenate([t0, t1, t2, t3])
    moved, _, _, made = clock.slot(
        (x_swap, t3), (core_swap, t_near), *lane(s_piece[part:]), (core_swap, tx1),
        work=[(join, *fetched[1][2])] if two else [],
    )
    tx3, ct_near = moved[:2]
    s_got, ctx1 = s_got + moved[2:-1], moved[-1]
    gate_got = made
    if two:
        s_pieces = [s_piece, jnp.concatenate(s_got)]
    else:
        s_pieces = jnp.split(dp_gather(s_piece[None], 0), ndp)
        s_pieces = [value.reshape(s_piece.shape) for value in s_pieces]
    moved, _, _, made = clock.slot(
        (core_swap, tx2), (core_swap, tx3), feed=0.4,
        work=[(lambda *a: shared_weights(a, block_index, ff_pad), *s_pieces)],
    )
    s_both, s_down_w = made[0]
    t_pieces = [t0, t1, t2, t3, tx0, tx1, tx2, tx3, ct_near, ctx0, ctx1, *moved]

    _, _, _, made = clock.slot(
        work=[
            (functools.partial(dispatch, slots=slots), t_pieces, target_row),
            (hidden_shared, t_pieces, g_pieces, s_both, s_down_w),
        ],
        feed=3.0,
    )
    rows_x, (s_act, d_s_pre) = made
    if two:
        assert all(entry[1] == entry[0].shape[0] for entry in fetched)
        own, other = own_expert, [gate_got[0], join(*fetched[2][2]), down_got[0]]
    else:
        full = [dp_gather(own_expert[0], 0), dp_gather(own_expert[1], 0), dp_gather(own_expert[2], 1)]
        own = [full[0][:half], full[1][:half], full[2][:, :half]]
        other = [full[0][half:], full[1][half:], full[2][:, half:]]
    _, _, _, made = clock.slot(work=[(expert_hidden, rows_x, rows_g, own, other)])
    e_act, d_gate, d_up, d_down_away = made[0]
    if two:
        sent = [clock.add(d_down_away)]

    _, _, _, made = clock.slot(
        work=[(expert_back, d_gate, d_up, own, other, target_col, d_s_pre, s_both)], feed=1.42
    )
    near, near_x, far, far_x = made[0]
    moved, _, _, made = clock.slot((core_swap, far_x), work=[(contract, rows_x[1], d_gate)], feed=0.35)
    if two:
        sent.append(clock.add(low(made[0])))
    away = [low(wide(cut(near_x, k)) + wide(cut(moved[0], k))) for k in range(4)]
    moved, _, _, made = clock.slot(
        (x_swap, away[3]), (core_swap, far),
        feed=0.75,
        work=[(functools.partial(shared_gradient, part=ff_part), t_pieces, g_pieces, d_s_pre, s_act)],
    )
    d_shared = made[0].reshape(ndp, experts, shard, 3 * ff_part)
    home = [wide(cut(near, k)) + wide(cut(moved[1], k)) for k in range(4)]
    moved, _, _, made = clock.slot(
        (x_swap, away[2]), (z_down, low(home[3] + wide(moved[0]))),
        feed=0.9,
        work=[(expert_out, e_act, share, own, other, target_col, s_act, s_down_w)],
    )
    o_near, o_near_x, o_far, o_far_x = made[0]
    s_away = d_shared[-1]
    moved, _, _, made = clock.slot(
        (x_swap, away[1]), (z_down, low(home[2] + wide(moved[0]) + wide(moved[1]))), (core_swap, o_far_x),
        *lane(s_away[:part]),
        work=[(contract, rows_x[1], d_up), (contract, e_act, rows_g[0])],
    )
    d_down_home = made[1]
    if two:
        sent.append(clock.add(low(made[0])))
    s_got = moved[3:]
    o_away = [low(wide(cut(o_near_x, k)) + wide(cut(moved[2], k))) for k in range(4)]
    moved, _, _, made = clock.slot(
        (x_swap, away[0]), (z_down, low(home[1] + wide(moved[0]) + wide(moved[1]))), (core_swap, o_far),
        *lane(s_away[part:]),
        work=[(contract, rows_x[0], d_gate)],
    )
    d_gate_home = made[0]
    s_got += moved[3:]
    o_home = [wide(cut(o_near, k)) + wide(cut(moved[2], k)) for k in range(4)]
    if two:
        d_shared = low(wide(d_shared[0]) + wide(jnp.concatenate(s_got)))
    else:
        d_shared = dp_scatter(d_shared)[0]
    d_shared = d_shared.reshape(4, 2, 2, shard, 3 * ff_part)
    d_mid_normed = turn(home[0] + wide(moved[0]) + wide(moved[1]))
    d_mid_in, d_gain_mid = rms_back(d_mid_normed, mid, scale_mid, gain_mid)
    d_mid = cotangent + d_mid_in

    a0 = low(d_mid)
    s_kept, s_away = at(d_shared, x, 1), at(d_shared, 1 - x, 1)
    moved, _, _, made = clock.slot(
        (z_up, a0), (x_swap, o_away[3]), lasting=1.65, work=[(contract, rows_x[0], d_up)]
    )
    a1, ox3 = moved
    d_up_home = made[0]
    moved, _, _, _ = clock.slot(
        (z_up, a1), (x_swap, o_away[2]), (z_down, low(o_home[3] + wide(ox3))), fed_before=clock.lasting
    )
    a2, ox2, o_sum = moved
    o_sum = low(o_home[2] + wide(ox2) + wide(o_sum))
    moved, _, _, _ = clock.slot((z_up, a2), (x_swap, o_away[1]), feed=0.67)
    a3, ox1 = moved
    moved, _, _, _ = clock.slot(
        (core_swap, jnp.concatenate([a0, a1, a2, a3])), (x_swap, s_away),
        (z_down, o_sum), feed=0.6,
    )
    a_pieces = [a0, a1, a2, a3, moved[0]]
    d_shared = jnp.stack([s_kept, moved[1]], axis=1)
    o_sum = low(o_home[1] + wide(ox1) + wide(moved[2]))
    backward = functools.partial(attention_backward, lat_rows=lat_rows)
    moved, _, _, made = clock.slot(
        (z_two, at(d_shared, (z + 2) % 4, 0)), (z_up, at(d_shared, (z + 1) % 4, 0)),
        (z_down, at(d_shared, (z + 3) % 4, 0)), (z_down, o_sum),
        feed=1.6,
        work=[(backward, scalars, x_pieces, a_pieces, saved, d_gain_mid.reshape(1, width), table)],
    )
    d_shared = jnp.stack([at(d_shared, z, 0), moved[1], moved[0], moved[2]])
    o_last = o_home[0] + wide(moved[3])
    d_norm, d_head, d_wl = made[0]
    same_x = [[i for i in range(experts) if i // 2 % 2 == side] for side in range(2)]
    d_normed = lax.psum_scatter(d_norm, "expert", scatter_dimension=0, axis_index_groups=same_x, tiled=True)

    if not two:
        d_head = d_head.reshape(ndp, 4, 2, 2 * shard, W_COLS)
        d_wl = d_wl.reshape(ndp, 4, 2, 2, shard, -1)
    s_kept, s_away = at(d_shared, core, 2), at(d_shared, 1 - core, 2)

    def add_received(home, *pieces):
        return home + wide(jnp.concatenate(pieces))

    if two:
        moved, _, _, made = clock.slot(
            (x_swap, d_head[4:8]), (dp_swap, d_head[12:]), (core_swap, d_wl[1]), (core_swap, s_away),
            work=[(add_received, d_down_home, *sent[0][2])],
        )
        d_down = made[0]
        first = (wide(d_head[:4]) + wide(moved[0])).reshape(ndp, 2, 2 * shard, W_COLS)
        second = (wide(d_head[8:12]) + wide(moved[1])).reshape(2, 2, 2 * shard, W_COLS)
        d_wl = (wide(d_wl[0]) + wide(moved[2])).reshape(ndp, 4, 2, shard, -1)
        d_shared = jnp.stack([s_kept, moved[3]], axis=2).reshape(experts, shard, 3 * ff_part)
        moved, _, _, made = clock.slot(
            (dp_swap, low(at(first, 1 - dp, 0))), (x_swap, low(at(second, 1 - x, 1))),
            (x_swap, low(at(d_wl, 1 - x, 2))), feed=0.45,
            work=[(add_received, d_gate_home, *sent[1][2]), (lambda a: reorder([a], block_index)[0], d_shared)],
        )
        d_gate_all, d_shared = made
        first = at(first, dp, 0) + wide(moved[0])
        second = at(second, x, 1) + wide(moved[1])
        d_wl = at(d_wl, x, 2) + wide(moved[2])
        d_head = low(jnp.concatenate([first, second]))
    else:
        d_head = wide(at(d_head, x, 2)) + wide(x_swap(at(d_head, 1 - x, 2)))
        d_head = dp_scatter(low(d_head))[0]
        d_wl = wide(at(d_wl, core, 3)) + wide(core_swap(at(d_wl, 1 - core, 3)))
        d_wl = at(d_wl, x, 2) + wide(x_swap(low(at(d_wl, 1 - x, 2))))
        d_shared = jnp.stack([s_kept, core_swap(s_away)], axis=2).reshape(experts, shard, 3 * ff_part)
        d_shared = reorder([d_shared], block_index)[0]
    moved, _, _, _ = clock.slot(
        (z_two, at(d_head, (z + 2) % 4, 0)), (z_down, at(d_head, (z + 3) % 4, 0)),
        (z_up, at(d_head, (z + 1) % 4, 0)),
        *(lane(low(at(d_wl, 1 - dp, 0))) if two else []), feed=3.0,
    )
    d_head = jnp.stack([at(d_head, z, 0), moved[1], moved[0], moved[2]]).reshape(4, 2, shard, W_COLS)
    d_wl = at(d_wl, dp, 0) + wide(moved[3]) if two else wide(dp_scatter(low(d_wl))[0])
    moved, _, ended, made = clock.slot(
        (core_swap, at(d_head, 1 - core, 1)), (z_two, low(at(d_wl, (z + 2) % 4, 0))),
        (z_down, low(at(d_wl, (z + 3) % 4, 0))), (z_up, low(at(d_wl, (z + 1) % 4, 0))), (x_swap, o_away[0]),
        end=[d_normed], work=[(add_received, d_up_home, *sent[2][2])] if two else [],
    )
    d_up_all = made[0] if two else None
    out = low(mid + turn(o_last + wide(moved[4])))
    d_head = jnp.stack([at(d_head, core, 1), moved[0]], axis=1).reshape(pairs, shard, W_COLS)
    d_wl = at(d_wl, z, 0) + wide(moved[1]) + wide(moved[2]) + wide(moved[3])
    d_normed = wide(ended[0])

    if two:
        assert all(entry[1] == entry[0].shape[0] for entry in sent)
        d_expert = [d_gate_all, d_up_all, d_down]
    else:
        d_expert = [
            wide(dp_scatter(low(jnp.concatenate([contract(value, d) for value in rows_x]))))
            for d in (d_gate, d_up)
        ]
        d_expert.append(wide(dp_scatter(low(jnp.concatenate([contract(e_act, value) for value in rows_g], axis=1)), 1)))
    d_in, _ = rms_back(d_normed, xf, rms_scale(xf), gain_in)
    d_tokens = d_mid + d_in
    d_shared = wide(d_shared)
    grad_sg, grad_su = (
        d_shared[:, :, i * ff_part : (i + 1) * ff_part].transpose(1, 0, 2).reshape(shard, ff_s) for i in range(2)
    )
    grad_sd = d_shared[:, :, 2 * ff_part :].transpose(0, 2, 1).reshape(ff_s, shard)
    pair_number = jnp.arange(pairs, dtype=jnp.int32)
    pair_index = ((pair_number // 2 + 4 - z) % 4) * 2 + (pair_number % 2 ^ core)
    if two:
        grad_wq, grad_wo, grad_we = unpack(d_head, pair_index, lat_rows)
        grad_wo = grad_wo.T
    else:
        d_head = wide(reorder([d_head], pair_index)[0])
        grad_wq = jnp.concatenate(
            [
                d_head[..., : 2 * HD].reshape(pairs, shard, 2, HD),
                d_head[..., 2 * HD : Q_COLS].reshape(pairs, shard, 2, RD),
            ],
            axis=3,
        )
        grad_wq = grad_wq.transpose(1, 0, 2, 3).reshape(shard, HEADS * (HD + RD))
        grad_wo = d_head[..., Q_COLS : Q_COLS + O_COLS].transpose(0, 2, 1).reshape(HEADS * VD, shard)
        grad_we = d_head[..., Q_COLS + O_COLS :].reshape(pairs, groups, lat_rows, E_COLS).transpose(2, 0, 1, 3)
        grad_we = grad_we.reshape(lat_rows, HEADS * (HD + VD))
    return (
        out,
        d_tokens,
        d_wl[:, lat_cols],
        d_wl[:lat_rows, lat_cols + 2],
        d_wl[:, lat_cols + 1],
        grad_wq,
        d_wl[:, :lat_cols],
        grad_we,
        grad_wo,
        grad_sg,
        grad_su,
        grad_sd,
        d_expert[0][None],
        d_expert[1][None],
        d_expert[2][None],
    )


def solution(mesh):
    rows = P(("dp", "expert"), None)
    vector = P(("dp", "expert"))
    columns = P(None, ("dp", "expert"))
    by_row = P("expert", "dp", None)
    by_column = P("expert", None, "dp")
    return jax.shard_map(
        local,
        mesh=mesh,
        in_specs=(
            rows, rows, rows, rows, vector, vector, vector, rows, rows, rows, columns, rows, rows, columns, by_row,
            by_row, by_column, rows,
        ),
        out_specs=(
            rows, rows, vector, vector, vector, rows, rows, rows, columns, rows, rows, columns, by_row, by_row,
            by_column,
        ),
        check_vma=False,
    )
```

```python
import functools

import jax
import jax.numpy as jnp
import ml_dtypes
import numpy as np
from jax import lax
from jax.experimental import pallas as pl
from jax.experimental.pallas import tpu as pltpu
from jax.sharding import PartitionSpec as P

HEADS = 16
HD = 128
RD = 64
VD = 128
LAT = 512
TOP = 6
EPS = 1e-06
CHUNK = 256
SCALE = (HD + RD) ** (-0.5)
BF = jnp.bfloat16
F32 = jnp.float32
VMEM_LIMIT = 60 * 1024 * 1024
Q_COLS = 2 * (HD + RD)
O_COLS = 2 * VD
E_COLS = 128
LAT_AT = Q_COLS
ROT_AT = Q_COLS + LAT
PROJ = ROT_AT + 128
W_COLS = Q_COLS + O_COLS + E_COLS
HIDDEN_TILE = 256


def matmul(left, right):
    return jnp.dot(left, right, preferred_element_type=F32)


def mat_trans(left, right):
    return lax.dot_general(left, right, (((1,), (1,)), ((), ())), preferred_element_type=F32)


def contract(left, right):
    return lax.dot_general(left, right, (((0,), (0,)), ((), ())), preferred_element_type=F32)


def rms_scale(values):
    return lax.rsqrt(jnp.mean(values * values, axis=-1, keepdims=True) + EPS)


def rms_back(incoming, values, scale, gain):
    scaled = incoming * gain
    inner = jnp.mean(scaled * values, axis=-1, keepdims=True)
    grad_in = scale * (scaled - values * scale * scale * inner)
    grad_gain = jnp.sum(incoming * values * scale, axis=0)
    return (grad_in, grad_gain)


def low(value):
    return value.astype(BF)


def wide(value):
    return value.astype(F32)


def move(value, to):
    return lax.ppermute(value, "expert", [(i, to(i)) for i in range(16)])


def z_up(value):
    return move(value, lambda i: (i + 4) % 16)


def z_down(value):
    return move(value, lambda i: (i + 12) % 16)


def z_two(value):
    return move(value, lambda i: (i + 8) % 16)


def x_swap(value):
    return move(value, lambda i: i ^ 2)


def core_swap(value):
    return move(value, lambda i: i ^ 1)


class Clock:
    def __init__(self, go):
        self.last = ()
        self.go = go
        self.queue = []

    def add(self, array):
        self.queue.append([array, 0, []])
        return self.queue[-1]

    def next_rows(self, size):
        moves, entries = [], []
        for entry in self.queue:
            array, start, _ = entry
            total = array.shape[0]
            line = array.size // total * array.dtype.itemsize
            count = round(size / line / 32) * 32
            if start == total or count < 64:
                continue
            stop = start + count
            stop = total if total - stop < 64 else stop
            entry[1] = stop
            moves.append((self.go, array[start:stop]))
            entries.append(entry)
            size -= (stop - start) * line
        return moves, entries

    def slot(self, *moves, begin=(), end=(), work=(), feed=0, lasting=0, fed_before=()):
        later, later_entries = self.next_rows(lasting * 1e6)
        begin = list(begin) + later
        waited = [entry[2][place] for entry, place in fed_before]
        end = waited + list(end)
        fed, entries = self.next_rows(feed * 1e6)
        moves = fed + list(moves)
        count, late = len(moves), len(moves) + len(begin)
        args, tree = jax.tree.flatten([list(rest) for _, *rest in work])
        values = [value for _, value in moves + list(begin)]
        tied = lax.optimization_barrier(tuple(values + args) + self.last)
        moved = [go(value) for (go, _), value in zip(moves, tied)]
        begun = [go(value) for (go, _), value in zip(begin, tied[count:])]
        args = jax.tree.unflatten(tree, tied[late : late + len(args)])
        made = [job[0](*some) for job, some in zip(work, args)]
        flat, tree = jax.tree.flatten(made)
        self.last = lax.optimization_barrier(tuple(moved) + tuple(end) + tuple(flat))
        moved, ended = list(self.last[:count]), list(self.last[count : count + len(end)])
        for entry in entries:
            entry[2].append(moved.pop(0))
        for entry, place in fed_before:
            entry[2][place] = ended.pop(0)
        self.lasting = []
        for entry in later_entries:
            self.lasting.append((entry, len(entry[2])))
            entry[2].append(begun.pop(len(begun) - len(later_entries) + len(self.lasting) - 1))
        return moved, begun, ended, jax.tree.unflatten(tree, self.last[count + len(end) :])


    def tie(self, value):
        return lax.optimization_barrier((value,) + self.last)[0]


def joined(entry):
    assert entry[1] == entry[0].shape[0]
    return jnp.concatenate(entry[2], axis=0)


def at(value, index, axis):
    return lax.dynamic_index_in_dim(value, index, axis, keepdims=False)


def whole_call(kernel, args, outs, scratch=(), flops=0, scalars=None):
    size = sum(a.size * a.dtype.itemsize for a in list(args) + list(outs))
    vmem = pl.BlockSpec(memory_space=pltpu.VMEM)
    specs = [vmem] * len(args)
    if scalars is not None:
        args = [scalars] + list(args)
        specs = [pl.BlockSpec(memory_space=pltpu.SMEM)] + specs
    return pl.pallas_call(
        kernel,
        in_specs=specs,
        out_specs=[vmem] * len(outs),
        out_shape=list(outs),
        scratch_shapes=list(scratch),
        compiler_params=pltpu.CompilerParams(vmem_limit_bytes=VMEM_LIMIT),
        cost_estimate=pl.CostEstimate(flops=flops, bytes_accessed=size, transcendentals=0),
    )(*args)


def shaped(shape, kind):
    return jax.ShapeDtypeStruct(shape, kind)


def reorder_kernel(count, parts, index_ref, *refs):
    for in_ref, out_ref in zip(refs[: len(refs) // 2], refs[len(refs) // 2 :]):
        pad = out_ref.shape[2] // parts
        width = in_ref.shape[2] // parts
        for i in range(count):
            value = in_ref[index_ref[i]]
            if pad == width:
                out_ref[i] = value
            else:
                spare = jnp.zeros((value.shape[0], pad - width), value.dtype)
                for part in range(parts):
                    cut = value[:, part * width : (part + 1) * width]
                    out_ref[i, :, part * pad : (part + 1) * pad] = jnp.concatenate([cut, spare], axis=1)


def shared_kernel_in(count, parts, index_ref, *refs):
    in_refs, (both_ref, down_ref) = refs[:-2], refs[-2:]
    pad = down_ref.shape[1]
    for k, in_ref in enumerate(in_refs):
        rows, columns = in_ref.shape[1], in_ref.shape[2] // parts
        spare = jnp.zeros((rows, pad - columns), in_ref.dtype)
        for i in range(count):
            value = in_ref[index_ref[i]]
            line = slice((k * count + i) * rows, (k * count + i + 1) * rows)
            for part in range(parts):
                cut = jnp.concatenate([value[:, part * columns : (part + 1) * columns], spare], axis=1)
                if part < parts - 1:
                    both_ref[line, part * pad : (part + 1) * pad] = cut
                else:
                    down_ref[line, :] = cut


def shared_weights(arrays, index, pad):
    rows = sum(a.shape[0] * a.shape[1] for a in arrays)
    outs = [shaped((rows, 2 * pad), BF), shaped((rows, pad), BF)]
    return whole_call(functools.partial(shared_kernel_in, index.shape[0], 3), arrays, outs, scalars=index)


def reorder(arrays, index, parts=1, pad=0):
    count = index.shape[0]
    outs = [shaped(a.shape[:2] + (a.shape[2] if not pad else parts * pad,), a.dtype) for a in arrays]
    return whole_call(functools.partial(reorder_kernel, count, parts), arrays, outs, scalars=index)


def unpack_kernel(index_ref, in_ref, wq_ref, wo_ref, we_ref):
    rows = we_ref.shape[0]
    for a in range(in_ref.shape[0]):
        value = wide(in_ref[index_ref[a]])
        parts = [value[:, :HD], value[:, 2 * HD : 2 * HD + RD], value[:, HD : 2 * HD], value[:, 2 * HD + RD : Q_COLS]]
        wq_ref[:, a * Q_COLS : (a + 1) * Q_COLS] = jnp.concatenate(parts, axis=1)
        wo_ref[:, a * O_COLS : (a + 1) * O_COLS] = value[:, Q_COLS : Q_COLS + O_COLS]
        for g in range(4):
            we_ref[:, (4 * a + g) * E_COLS : (4 * a + g + 1) * E_COLS] = value[g * rows : (g + 1) * rows, Q_COLS + O_COLS :]


def unpack(blocks, index, rows):
    pairs, shard, _ = blocks.shape
    outs = [
        shaped((shard, pairs * Q_COLS), F32), shaped((shard, pairs * O_COLS), F32), shaped((rows, 4 * pairs * E_COLS), F32)
    ]
    return whole_call(unpack_kernel, [blocks], outs, scalars=index)


def swap_halves(values):
    lane = lax.broadcasted_iota(jnp.int32, values.shape, 1)
    return jnp.where(
        lane % RD < RD // 2, pltpu.roll(values, 2 * RD - RD // 2, 1), pltpu.roll(values, RD // 2, 1)
    )


def probabilities(q_main, q_rot, k_main, k_rot, allowed):
    scores = (mat_trans(q_main, k_main) + mat_trans(q_rot, k_rot)) * SCALE
    scores = jnp.where(allowed, scores, -1e30)
    expo = jnp.exp(scores - jnp.max(scores, axis=-1, keepdims=True))
    return expo / jnp.sum(expo, axis=-1, keepdims=True)


def allowed_pairs(id_col, id_row):
    shape = (id_col.shape[0], id_row.shape[1])
    key = lax.broadcasted_iota(jnp.int32, shape, 1)
    query = lax.broadcasted_iota(jnp.int32, shape, 0)
    return (id_col == id_row) & (key <= query)


def angle_table(rows):
    freq = np.power(np.float32(10000.0), np.float32(-2.0) * np.arange(RD // 2, dtype=np.float32) / np.float32(RD))
    theta = np.arange(rows, dtype=np.float32)[:, None] * freq.astype(np.float32)
    cosine, sine = np.cos(theta), np.sin(theta)
    terms = []
    for value in (np.concatenate([cosine] * 4, axis=1), np.concatenate([-sine, sine, -sine, sine], axis=1)):
        rest = value.astype(np.float32)
        for _ in range(3):
            term = rest.astype(ml_dtypes.bfloat16)
            terms.append(term)
            rest = rest - term.astype(np.float32)
    return np.concatenate(terms, axis=1)


def chunk_layout(facts_ref, j, rows, shape):
    count = CHUNK // rows
    number = lax.broadcasted_iota(jnp.int32, shape, 0 if shape[0] == CHUNK else 1)
    block, place = number // rows, number % rows
    doc, start, ends = 0, 0, [0] * count
    for k in range(3):
        lengths = [facts_ref[4 + (j * count + b) * 4 + k] for b in range(count)]
        ends = [end + length for end, length in zip(ends, lengths)]
        end, length = ends[-1], lengths[-1]
        for b in range(count - 2, -1, -1):
            end = jnp.where(block == b, ends[b], end)
            length = jnp.where(block == b, lengths[b], length)
        passed = place >= end
        doc = doc + passed.astype(jnp.int32)
        start = start + jnp.where(passed, length, 0)
    return place - start, doc + 4 * block


def chunk_tables(facts_ref, table_ref, j):
    rows = table_ref.shape[0]
    position, id_col = chunk_layout(facts_ref, j, rows, (CHUNK, 1))
    id_row = chunk_layout(facts_ref, j, rows, (1, CHUNK))[1]
    hot = low(lax.broadcasted_iota(jnp.int32, (CHUNK, rows), 1) == position)
    terms = matmul(hot, table_ref[...])
    cosine = terms[:, :128] + terms[:, 128:256] + terms[:, 256:384]
    sine = terms[:, 384:512] + terms[:, 512:640] + terms[:, 640:]
    return cosine, sine, allowed_pairs(id_col, id_row)


def pair(refs, j):
    pieces, start = [], 0
    for ref in refs:
        low_row, high_row = max(start, CHUNK * j), min(start + ref.shape[0], CHUNK * (j + 1))
        if low_row < high_row:
            pieces.append(ref[low_row - start : high_row - start, :])
        start += ref.shape[0]
    return pieces[0] if len(pieces) == 1 else jnp.concatenate(pieces, axis=0)


def forward_kernel(ndp, layout_of, pieces, count, split, place_ref, *refs):
    x_refs, refs = refs[:pieces], refs[pieces:]
    w_refs, refs = refs[: len(layout_of)], refs[len(layout_of) :]
    wl_refs, refs = refs[:count], refs[count:]
    we_ref, gains_ref, lg_ref, table_ref = refs[:4]
    near_ref, far_ref, q_ref, kr_ref, lat_ref, kv_ref, att_ref, wp_ref, wo_ref, exp_ref, gain_ref, mid_ref, lgo_ref = refs[4:]
    other_rows = [(ref, i) for ref in wl_refs for i in range(ref.shape[0])]
    dp, z, x, core = place_ref[0], place_ref[1], place_ref[2], place_ref[3]
    block = w_refs[0].shape[1]
    shard = block // 2
    lat_rows = jnp.zeros((4, 128), F32)
    spare = jnp.zeros((shard, 128 - RD), BF)
    turn = 0
    for w_ref, (far, j, first) in zip(w_refs, layout_of):
        y = j ^ dp if ndp == 2 else j
        for k in range(w_ref.shape[0]):
            row = ((y * 4 + lax.rem(z + 4 - first - k, 4)) * 2 + (x ^ far)) * block
            row = pl.multiple_of(row, block)
            wp_ref[pl.ds(row, block), :Q_COLS] = w_ref[k, :, :Q_COLS]
            wo_ref[pl.ds(row, block), :] = w_ref[k, :, Q_COLS : Q_COLS + O_COLS]
            if not split:
                continue
            here = pl.multiple_of(row + core * shard, shard)
            there = pl.multiple_of(row + (1 - core) * shard, shard)
            for at_row, lat in ((here, w_ref[k, :, W_COLS:]), (there, other_rows[turn][0][other_rows[turn][1]])):
                wp_ref[pl.ds(at_row, shard), LAT_AT : LAT_AT + 384] = lat[:shard, :]
                wp_ref[pl.ds(at_row, shard), LAT_AT + 384 :] = lat[shard:, :256]
            here_rows, there_rows = (
                wide(lat[shard : shard + 16, 256:]) for lat in (w_ref[k, :, W_COLS:], other_rows[turn][0][other_rows[turn][1]])
            )
            left = jnp.where(core == 0, here_rows[:1, :], there_rows[:1, :])
            right = jnp.where(core == 0, there_rows[:1, :], here_rows[:1, :])
            gain_ref[:, pl.ds(row, block)] = jnp.concatenate([left[:, :shard], right[:, :shard]], axis=1)
            mid_ref[:, pl.ds(row, block)] = jnp.concatenate([left[:, shard:], right[:, shard:]], axis=1)
            lat_rows = lat_rows + here_rows[1:5, :] + there_rows[1:5, :]
            turn += 1
            small = shard // 4
            for c in range(2):
                for g in range(4):
                    at_row = pl.multiple_of(row // 4 + c * small, small)
                    exp_ref[pl.ds(at_row, small), g * HD : (g + 1) * HD] = w_ref[
                        k, c * shard + g * small : c * shard + (g + 1) * small, Q_COLS + O_COLS : W_COLS
                    ]
    if not split:
        for i, (wl_ref, _) in enumerate(other_rows):
            wp_ref[i * shard : (i + 1) * shard, LAT_AT:] = jnp.concatenate([wl_ref[i, :shard, :], spare], axis=1)
        exp_ref[...] = we_ref[...]
        gain_ref[...] = gains_ref[:1, :]
        mid_ref[...] = gains_ref[1:2, :]
        lgo_ref[...] = lg_ref[...]
    else:
        lgo_ref[...] = jnp.concatenate([lat_rows[i : i + 1, :] for i in range(4)], axis=1)
    gain, lat_gain = gain_ref[...], lgo_ref[...]
    for j in range(4):
        rows = slice(CHUNK * j, CHUNK * (j + 1))
        xf = wide(pair(x_refs, j))
        normed = low(xf * rms_scale(xf) * gain)
        proj = matmul(normed, wp_ref[...])
        cosine, sine, allowed = chunk_tables(place_ref, table_ref, j)
        q_mix = proj[:, 2 * HD : Q_COLS]
        k_mix = proj[:, ROT_AT:]
        q_rot = low(q_mix * cosine + swap_halves(q_mix) * sine)
        k_rot = k_mix * cosine + swap_halves(k_mix) * sine
        k_turned = low(pltpu.roll(k_rot, RD, 1))
        k_rot = low(k_rot)
        q_main = low(proj[:, : 2 * HD])
        lat = proj[:, LAT_AT:ROT_AT]
        lat_ref[rows, :] = lat
        compressed = low(lat * rms_scale(lat) * lat_gain)
        expanded = low(matmul(compressed, exp_ref[...]))
        q_ref[rows, : 2 * HD] = q_main
        q_ref[rows, 2 * HD :] = q_rot
        kr_ref[rows, :] = k_rot
        kv_ref[rows, :] = expanded
        attended = []
        for head, k_side in ((0, k_rot), (1, k_turned)):
            k_main = expanded[:, 2 * head * HD : (2 * head + 1) * HD]
            values = expanded[:, (2 * head + 1) * HD : (2 * head + 2) * HD]
            probs = probabilities(q_main[:, head * HD : (head + 1) * HD], q_rot, k_main, k_side, allowed)
            attended.append(low(matmul(low(probs), values)))
        attended = jnp.concatenate(attended, axis=1)
        att_ref[rows, :] = attended
        put_half(near_ref, far_ref, j, 4, low(mat_trans(attended, wo_ref[...])))


def put_half(near_ref, far_ref, j, count, value):
    ref = near_ref if j < count // 2 else far_ref
    j = j % (count // 2)
    ref[j * CHUNK : (j + 1) * CHUNK, :] = value


def attention_forward(place, x_pieces, weights, layout_of, w_lat, w_exp, gains, lat_gain, table, split):
    own, width = x_pieces[0].shape
    rows = 8 * own
    args = list(x_pieces) + list(weights) + list(w_lat) + [w_exp, gains, lat_gain, table]
    outs = [shaped((rows // 2, width), BF)] * 2 + [
        shaped((rows, Q_COLS), BF),
        shaped((rows, 128), BF),
        shaped((rows, LAT), F32),
        shaped((rows, 4 * HD), BF),
        shaped((rows, O_COLS), BF),
        shaped((width, PROJ), BF),
        shaped((width, O_COLS), BF),
        shaped((LAT, 4 * HD), BF),
        shaped((1, width), F32),
        shaped((1, width), F32),
        shaped((1, LAT), F32),
    ]
    kernel = functools.partial(forward_kernel, lax.axis_size("dp"), layout_of, len(x_pieces), len(w_lat), split)
    flops = 2 * rows * width * (PROJ + O_COLS)
    out = whole_call(kernel, args, outs, flops=flops, scalars=place)
    return out[:2], out[2:]


def backward_kernel(pieces, count, lat_rows, place_ref, *refs):
    x_refs, g_refs, refs = refs[:pieces], refs[pieces : pieces + count], refs[pieces + count :]
    q_ref, kr_ref, lat_ref, kv_ref, att_ref, wp_ref, wo_ref, we_ref, gain_ref, mid_ref, lg_ref, dm_ref = refs[:12]
    table_ref, dn_ref, dw_ref, dl_ref, de_ref, acc_q, acc_o, acc_e, dg_ref, dlg_ref = refs[12:]
    split = len(dw_ref.shape) > 2
    dp, z, x, core = place_ref[0], place_ref[1], place_ref[2], place_ref[3]
    own = x_refs[0].shape[0]
    gain, w_exp, lat_gain = gain_ref[...], we_ref[...], lg_ref[...]

    def add(acc, value, first):
        acc[...] = value if first else acc[...] + value

    for j in range(4):
        rows = slice(CHUNK * j, CHUNK * (j + 1))
        xf = wide(pair(x_refs, j))
        whitened = xf * rms_scale(xf)
        normed = low(whitened * gain)
        lat = lat_ref[rows, :]
        lat_scale = rms_scale(lat)
        white_lat = lat * lat_scale
        grad = pair(g_refs, j)
        cosine, sine, allowed = chunk_tables(place_ref, table_ref, j)
        d_att = low(matmul(grad, wo_ref[...]))
        q_rot, k_rot = q_ref[rows, 2 * HD :], kr_ref[rows, :]
        k_turned = low(pltpu.roll(wide(k_rot), RD, 1))
        d_main, d_expanded = [], []
        dq_mix = None
        dk_mix = None
        for head, k_side in ((0, k_rot), (1, k_turned)):
            q_main = q_ref[rows, head * HD : (head + 1) * HD]
            k_main = kv_ref[rows, 2 * head * HD : (2 * head + 1) * HD]
            values = kv_ref[rows, (2 * head + 1) * HD : (2 * head + 2) * HD]
            probs = probabilities(q_main, q_rot, k_main, k_side, allowed)
            d_out = d_att[:, head * HD : (head + 1) * HD]
            d_prob = mat_trans(d_out, values)
            d_values = contract(low(probs), d_out)
            d_scores = low(probs * (d_prob - jnp.sum(probs * d_prob, axis=-1, keepdims=True)))
            d_main.append(matmul(d_scores, k_main) * SCALE)
            d_expanded += [contract(d_scores, q_main) * SCALE, d_values]
            dq_one = matmul(d_scores, k_side)
            dk_one = contract(d_scores, q_rot)
            dq_mix = dq_one if head == 0 else dq_mix + dq_one
            dk_mix = dk_one if head == 0 else dk_mix + pltpu.roll(dk_one, RD, 1)
        dq_mix = dq_mix * SCALE
        dk_mix = dk_mix * SCALE
        dq_mix = dq_mix * cosine - swap_halves(dq_mix) * sine
        dk_mix = dk_mix * cosine - swap_halves(dk_mix) * sine
        dk_mix = jnp.where(lax.broadcasted_iota(jnp.int32, dk_mix.shape, 1) < RD, dk_mix, 0.0)
        d_expanded = low(jnp.concatenate(d_expanded, axis=1))
        d_comp = mat_trans(d_expanded, w_exp)
        scaled = d_comp * lat_gain
        d_lat = lat_scale * (scaled - white_lat * jnp.mean(scaled * white_lat, axis=-1, keepdims=True))
        d_proj = low(jnp.concatenate(d_main + [dq_mix, d_lat, dk_mix], axis=1))
        d_normed = mat_trans(d_proj, wp_ref[...])
        part = low(d_normed)
        for k in range(2):
            piece = 2 * j + k
            place = lax.rem(z + 4 - piece % 4, 4) * 2 + (core ^ (piece // 4))
            dn_ref[pl.ds(pl.multiple_of(place * own, own), own), :] = part[k * own : (k + 1) * own, :]
        add(dg_ref, jnp.sum(d_normed * whitened, axis=0, keepdims=True), j == 0)
        add(dlg_ref, jnp.sum(d_comp * white_lat, axis=0, keepdims=True), j == 0)
        add(acc_q, contract(d_proj, normed), j == 0)
        add(acc_o, contract(att_ref[rows, :], grad), j == 0)
        add(acc_e, contract(low(white_lat * lat_gain), d_expanded), j == 0)
    shard = acc_q.shape[1] * lat_rows // LAT
    lane = lax.broadcasted_iota(jnp.int32, (LAT, acc_q.shape[1]), 1)
    line = lax.broadcasted_iota(jnp.int32, (LAT, acc_q.shape[1]), 0)
    spread = low((line // lat_rows == lane // shard) & (line % lat_rows == lane % shard))
    spread = matmul(low(jnp.broadcast_to(dlg_ref[...], (8, LAT))), spread)[:1, :]
    acc_q[ROT_AT + RD : ROT_AT + RD + 8, :] = jnp.concatenate(
        [dg_ref[...], dm_ref[...], spread, jnp.zeros((5, acc_q.shape[1]), F32)], axis=0
    )
    if not split:
        dw_ref[:, :Q_COLS] = low(acc_q[:Q_COLS, :].T)
        dw_ref[:, Q_COLS : Q_COLS + O_COLS] = low(acc_o[...].T)
        dl_ref[...] = low(acc_q[Q_COLS:, :].T)
        de_ref[...] = low(acc_e[...])
        return
    block = 2 * shard
    for number in range(acc_q.shape[1] // block):
        y, zz, xx = number // 8, number // 2 % 4, number % 2
        lanes = slice(number * block, (number + 1) * block)
        slot = (x ^ xx) * 4 + y * 2 + zz if zz < 2 else 8 + (dp ^ y) * 4 + (zz - 2) * 2 + xx
        dw_ref[slot, :, :Q_COLS] = low(acc_q[:Q_COLS, lanes].T)
        dw_ref[slot, :, Q_COLS : Q_COLS + O_COLS] = low(acc_o[:, lanes].T)
        for c in range(2):
            for g in range(4):
                row = c * shard + g * lat_rows
                i = number * 2 + c
                dw_ref[slot, row : row + lat_rows, Q_COLS + O_COLS :] = low(
                    acc_e[i * lat_rows : (i + 1) * lat_rows, g * HD : (g + 1) * HD]
                )
        both = low(acc_q[Q_COLS:, lanes].T)
        for c in range(2):
            dl_ref[core ^ c, number, :, :] = both[c * shard : (c + 1) * shard, :]


def attention_backward(place, x_pieces, g_pieces, saved, d_gain_mid, table, lat_rows):
    own, width = x_pieces[0].shape
    q, kr, lat, kv, att, wp, wo, w_exp, gain, mid, lat_gain = saved
    args = list(x_pieces) + list(g_pieces)
    args += [q, kr, lat, kv, att, wp, wo, w_exp, gain, mid, lat_gain, d_gain_mid, table]
    outs = [
        shaped((8 * own, width), BF),
        shaped((width, W_COLS), BF),
        shaped((width, PROJ - Q_COLS), BF),
        shaped((LAT, 4 * HD) if lat_rows % 16 else (16, 128), BF),
    ]
    shard = width * lat_rows // LAT
    if not lat_rows % 16:
        outs[1] = shaped((width // (2 * shard), 2 * shard, W_COLS), BF)
        outs[2] = shaped((2, width // (2 * shard), shard, PROJ - Q_COLS), BF)
    scratch = (
        pltpu.VMEM((PROJ, width), F32), pltpu.VMEM((O_COLS, width), F32), pltpu.VMEM((LAT, 4 * HD), F32),
        pltpu.VMEM((1, width), F32), pltpu.VMEM((1, LAT), F32),
    )
    flops = 2 * 8 * own * width * (2 * PROJ + 2 * O_COLS)
    kernel = functools.partial(backward_kernel, len(x_pieces), len(g_pieces), lat_rows)
    d_norm, d_head, d_wl, d_we = whole_call(kernel, args, outs, scratch, flops=flops, scalars=place)
    if lat_rows % 16:
        d_we = d_we.reshape(width // shard, lat_rows, 4, E_COLS).transpose(0, 2, 1, 3).reshape(width, E_COLS)
        d_head = jnp.concatenate([d_head[:, : Q_COLS + O_COLS], d_we], axis=1)
    return d_norm, d_head, d_wl


def routing_kernel(first, lanes, slots, me_ref, *refs):
    in_refs, (row_ref, gate_ref, col_ref) = refs[:4], refs[4:]
    mine = lax.broadcasted_iota(jnp.int32, (16, 128), 0) == me_ref[0]
    gates = []
    for ref, lane in zip(in_refs, lanes):
        for k in range(4):
            both = wide(ref[k, first : first + 32, lane : lane + 128])
            gates.append(jnp.sum(jnp.where(mine, both[:16, :] + both[16:, :], 0.0), axis=0, keepdims=True))
    gates = jnp.concatenate(gates, axis=0)
    routed = gates > 0.0
    line = lax.broadcasted_iota(jnp.int32, (128, 128), 0)
    column = lax.broadcasted_iota(jnp.int32, (128, 128), 1)
    before = low((line <= column) & (line // 64 == column // 64))
    count = matmul(low(routed), before)
    source = lax.broadcasted_iota(jnp.int32, (16, 128), 0)
    token = lax.broadcasted_iota(jnp.int32, (16, 128), 1)
    block = ((source % 2) * 2 + token // 64).astype(F32)
    target = jnp.where(routed, block * slots + count - 1.0, -1.0)
    turned = target.T
    for k in range(16):
        part = slice((k % 2) * 128, (k % 2 + 1) * 128)
        row_ref[k // 2, :, part] = target[k : k + 1, :].astype(jnp.int32)
        gate_ref[k // 2, :, part] = gates[k : k + 1, :]
        col_ref[k * 128 : (k + 1) * 128, :] = turned[:, k : k + 1].astype(jnp.int32)


def routing(me, arrays, first, lanes, slots):
    outs = [shaped((8, 1, CHUNK), jnp.int32), shaped((8, 1, CHUNK), F32), shaped((8 * CHUNK, 1), jnp.int32)]
    return whole_call(functools.partial(routing_kernel, first, lanes, slots), arrays, outs, scalars=me)


def enter_grad_kernel(slots, *refs):
    g_refs, (target_ref, gate_ref, rg0_ref, rg1_ref, rs_ref) = refs[:-5], refs[-5:]
    half = rg0_ref.shape[1]
    for j in range(8):
        grad = pair(g_refs, j)
        chosen = lax.broadcasted_iota(jnp.int32, (slots, CHUNK), 0) == target_ref[j]
        share = jnp.sum(jnp.where(chosen, gate_ref[j], 0.0), axis=1, keepdims=True)
        rs_ref[j * slots : (j + 1) * slots, :] = share
        value = low(matmul(low(chosen), grad) * share)
        rg0_ref[j * slots : (j + 1) * slots, :] = value[:, :half]
        rg1_ref[j * slots : (j + 1) * slots, :] = value[:, half:]


def dispatch_kernel(slots, *refs):
    t_refs, (target_ref, rx0_ref, rx1_ref) = refs[:-3], refs[-3:]
    half = rx0_ref.shape[1]
    for j in range(8):
        chosen = lax.broadcasted_iota(jnp.int32, (slots, CHUNK), 0) == target_ref[j]
        value = low(matmul(low(chosen), pair(t_refs, j)))
        rx0_ref[j * slots : (j + 1) * slots, :] = value[:, :half]
        rx1_ref[j * slots : (j + 1) * slots, :] = value[:, half:]


def hidden_shared_kernel(count, *refs):
    t_refs, g_refs, (sgu_ref, sd_ref, act_ref, pre_ref) = refs[:count], refs[count:-4], refs[-4:]
    third = sd_ref.shape[1]
    for j in range(8):
        rows = slice(j * CHUNK, (j + 1) * CHUNK)
        both = matmul(pair(t_refs, j), sgu_ref[...])
        gate_pre, up = both[:, :third], both[:, third:]
        d_act = matmul(pair(g_refs, j), sd_ref[...])
        sigma = jax.nn.sigmoid(gate_pre)
        swish = gate_pre * sigma
        act_ref[rows, :] = low(swish * up)
        pre_ref[rows, :third] = low(d_act * up * (sigma * (1.0 + gate_pre * (1.0 - sigma))))
        pre_ref[rows, third:] = low(d_act * swish)


def enter_grad(g_pieces, target, gate, slots):
    own, width = g_pieces[0].shape
    args = list(g_pieces) + [target, gate]
    outs = [shaped((slots, width // 2), BF)] * 2 + [shaped((slots, 1), F32)]
    flops = 32 * own * width * (slots // 8)
    return whole_call(functools.partial(enter_grad_kernel, slots // 8), args, outs, flops=flops)


def dispatch(t_pieces, target, slots):
    own, width = t_pieces[0].shape
    args = list(t_pieces) + [target]
    outs = [shaped((slots, width // 2), BF)] * 2
    flops = 32 * own * width * (slots // 8)
    return whole_call(functools.partial(dispatch_kernel, slots // 8), args, outs, flops=flops)


def hidden_shared(t_pieces, g_pieces, s_both, s_down):
    own, width = t_pieces[0].shape
    third = s_down.shape[1]
    args = list(t_pieces) + list(g_pieces) + [s_both, s_down]
    outs = [shaped((16 * own, third), BF), shaped((16 * own, 2 * third), BF)]
    return whole_call(functools.partial(hidden_shared_kernel, len(t_pieces)), args, outs, flops=96 * own * width * third)


def hidden_kernel(x0_ref, x1_ref, r0_ref, r1_ref, g0_ref, g1_ref, u0_ref, u1_ref, d0_ref, d1_ref, act_ref, dg_ref, du_ref, away_ref):
    step = 256
    for j in range(x0_ref.shape[0] // step):
        rows = slice(j * step, (j + 1) * step)
        x0, x1 = x0_ref[rows, :], x1_ref[rows, :]
        gate = matmul(x0, g0_ref[...]) + matmul(x1, g1_ref[...])
        up = matmul(x0, u0_ref[...]) + matmul(x1, u1_ref[...])
        d_act = mat_trans(r0_ref[rows, :], d0_ref[...]) + mat_trans(r1_ref[rows, :], d1_ref[...])
        sigma = jax.nn.sigmoid(gate)
        swish = gate * sigma
        act_ref[rows, :] = low(swish * up)
        dg_ref[rows, :] = low(d_act * up * (sigma * (1.0 + gate * (1.0 - sigma))))
        du_ref[rows, :] = low(d_act * swish)
    away_ref[...] = low(contract(act_ref[...], r1_ref[...]))


def tiled_call(kernel, steps, args, specs, outs, out_specs, scratch=(), flops=0, aliases=None):
    size = sum(a.size * a.dtype.itemsize for a in list(args) + list(outs))
    return pl.pallas_call(
        kernel,
        grid=(steps,),
        in_specs=specs,
        out_specs=out_specs,
        out_shape=outs,
        scratch_shapes=list(scratch),
        input_output_aliases=aliases or {},
        compiler_params=pltpu.CompilerParams(vmem_limit_bytes=VMEM_LIMIT),
        cost_estimate=pl.CostEstimate(flops=flops, bytes_accessed=size, transcendentals=0),
    )(*args)


def whole_spec(array):
    return pl.BlockSpec(array.shape, lambda i: (0,) * array.ndim)


def expert_hidden(rows_x, rows_g, own, other):
    slots, half = rows_x[0].shape
    hidden = own[0].shape[1]
    tile = HIDDEN_TILE
    by_column = pl.BlockSpec((half, tile), lambda i: (0, i))
    by_row = pl.BlockSpec((tile, half), lambda i: (i, 0))
    args = list(rows_x) + list(rows_g) + [own[0], other[0], own[1], other[1], own[2], other[2]]
    specs = [whole_spec(value) for value in args[:4]] + [by_column] * 4 + [by_row] * 2
    outs = [shaped((slots, hidden), BF)] * 3 + [shaped((hidden, half), BF)]
    out_specs = [pl.BlockSpec((slots, tile), lambda i: (0, i))] * 3 + [by_row]
    flops = 14 * slots * half * hidden
    return tiled_call(hidden_kernel, -(-hidden // tile), args, specs, outs, out_specs, flops=flops)


def back_kernel(per, dg_ref, du_ref, g0_ref, g1_ref, u0_ref, u1_ref, target_ref, left_ref, right_ref, *refs):
    out_refs, rows_ref = refs[:4], refs[4]
    steps = pl.num_programs(0) // 2
    own = pl.program_id(0) < steps

    @pl.when(own)
    def _():
        rows_ref[...] = low(mat_trans(dg_ref[...], g0_ref[...]) + mat_trans(du_ref[...], u0_ref[...]))

    @pl.when(jnp.logical_not(own))
    def _():
        rows_ref[...] = low(mat_trans(dg_ref[...], g1_ref[...]) + mat_trans(du_ref[...], u1_ref[...]))

    right = right_ref[...]
    for j in range(8):
        hot = low(lax.broadcasted_iota(jnp.int32, (CHUNK, per), 1) == target_ref[j * CHUNK : (j + 1) * CHUNK, :])
        out = matmul(hot, rows_ref[j * per : (j + 1) * per, :])
        out = low(out + mat_trans(left_ref[j * CHUNK : (j + 1) * CHUNK, :], right))
        out_refs[j // 2][(j % 2) * CHUNK : (j % 2 + 1) * CHUNK, :] = out


def expert_back(d_gate, d_up, own, other, target, left, right):
    slots, hidden = d_gate.shape
    rows, columns = left.shape
    width = right.shape[0]
    tile = 256
    steps = width // tile // 2
    near = pl.BlockSpec((tile, hidden), lambda i: (jnp.minimum(i, steps - 1), 0))
    far = pl.BlockSpec((tile, hidden), lambda i: (jnp.maximum(i - steps, 0), 0))
    args = [d_gate, d_up, own[0], other[0], own[1], other[1], target, left, right]
    specs = [whole_spec(d_gate), whole_spec(d_up)] + [near, far] * 2
    specs += [whole_spec(target), whole_spec(left), pl.BlockSpec((tile, columns), lambda i: (i, 0))]
    outs = [shaped((rows // 4, width), BF)] * 4
    out_specs = [pl.BlockSpec((rows // 4, tile), lambda i: (0, i))] * 4
    flops = 4 * slots * width * hidden + 2 * rows * width * (columns + slots // 8)
    return tiled_call(
        functools.partial(back_kernel, slots // 8), 2 * steps, args, specs, outs, out_specs,
        (pltpu.VMEM((slots, tile), BF),), flops=flops,
    )


def out_kernel(per, act_ref, share_ref, d0_ref, d1_ref, target_ref, left_ref, right_ref, *refs):
    out_refs, rows_ref = refs[:4], refs[4]
    steps = pl.num_programs(0) // 2
    own = pl.program_id(0) < steps

    @pl.when(own)
    def _():
        rows_ref[...] = low(matmul(act_ref[...], d0_ref[...]) * share_ref[...])

    @pl.when(jnp.logical_not(own))
    def _():
        rows_ref[...] = low(matmul(act_ref[...], d1_ref[...]) * share_ref[...])

    right = right_ref[...]
    for j in range(8):
        hot = low(lax.broadcasted_iota(jnp.int32, (CHUNK, per), 1) == target_ref[j * CHUNK : (j + 1) * CHUNK, :])
        out = matmul(hot, rows_ref[j * per : (j + 1) * per, :])
        out = low(out + mat_trans(left_ref[j * CHUNK : (j + 1) * CHUNK, :], right))
        out_refs[j // 2][(j % 2) * CHUNK : (j % 2 + 1) * CHUNK, :] = out


def expert_out(act, share, own, other, target, left, right):
    slots, hidden = act.shape
    rows, columns = left.shape
    width = right.shape[0]
    tile = 256
    steps = width // tile // 2
    args = [act, share, own[2], other[2], target, left, right]
    specs = [
        whole_spec(act), whole_spec(share),
        pl.BlockSpec((hidden, tile), lambda i: (0, jnp.minimum(i, steps - 1))),
        pl.BlockSpec((hidden, tile), lambda i: (0, jnp.maximum(i - steps, 0))),
        whole_spec(target), whole_spec(left), pl.BlockSpec((tile, columns), lambda i: (i, 0)),
    ]
    outs = [shaped((rows // 4, width), BF)] * 4
    out_specs = [pl.BlockSpec((rows // 4, tile), lambda i: (0, i))] * 4
    flops = 2 * slots * width * hidden + 2 * rows * width * (columns + slots // 8)
    return tiled_call(
        functools.partial(out_kernel, slots // 8), 2 * steps, args, specs, outs, out_specs,
        (pltpu.VMEM((slots, tile), BF),), flops=flops,
    )


def shared_kernel(part, count, *refs):
    t_refs, g_refs, (pre_ref, act_ref, out_ref, acc_t, acc_g) = refs[:count], refs[count:-5], refs[-5:]
    pad = act_ref.shape[1]
    for j in range(8):
        rows = slice(j * CHUNK, (j + 1) * CHUNK)
        by_tok = contract(pre_ref[rows, :], pair(t_refs, j))
        by_grad = contract(act_ref[rows, :], pair(g_refs, j))
        acc_t[...] = by_tok if j == 0 else acc_t[...] + by_tok
        acc_g[...] = by_grad if j == 0 else acc_g[...] + by_grad
    parts = [acc_t[:part, :], acc_t[pad : pad + part, :], acc_g[:part, :]]
    spare = -3 * part % 128
    if spare:
        parts.append(jnp.zeros((spare, acc_t.shape[1]), F32))
    out_ref[...] = low(jnp.concatenate(parts, axis=0).T[:, : 3 * part])


def shared_gradient(t_pieces, g_pieces, pre, act, part):
    own, width = t_pieces[0].shape
    args = list(t_pieces) + list(g_pieces) + [pre, act]
    outs = [shaped((width, 3 * part), BF)]
    scratch = (pltpu.VMEM((pre.shape[1], width), F32), pltpu.VMEM((act.shape[1], width), F32))
    flops = 32 * own * width * (pre.shape[1] + act.shape[1])
    return whole_call(functools.partial(shared_kernel, part, len(t_pieces)), args, outs, scratch, flops=flops)[0]


def local(
    tokens, lengths, routes, gates, norm_in, latent_gain, norm_mid, w_query, w_latent, w_expand, w_output,
    shared_gate, shared_up, shared_down, expert_gate, expert_up, expert_down, cotangent,
):
    micro = lengths.shape[0]
    own_rows, width = tokens.shape
    rows = own_rows // micro
    experts = lax.axis_size("expert")
    ndp = lax.axis_size("dp")
    two = ndp == 2
    cap = rows * TOP * 4 // (3 * experts)
    blocks = experts * micro
    all_rows = experts * own_rows
    devices = ndp * experts
    shard = width // devices
    lat_rows = w_expand.shape[0]
    lat_cols = w_latent.shape[1]
    ff_s = shared_gate.shape[1]
    ff_part = ff_s // experts
    ff_pad = -(-ff_part // 128) * 128
    half = width // 2
    me = lax.axis_index("expert")
    dp = lax.axis_index("dp")
    core, x, z = me % 2, (me // 2) % 2, me // 4

    def turn(value):
        if not two:
            return value
        swapped = jnp.concatenate([value[..., half:], value[..., :half]], axis=-1)
        return jnp.where(dp == 1, swapped, value)

    def dp_swap(value):
        return lax.ppermute(value, "dp", [(0, 1), (1, 0)])

    clock = Clock(dp_swap)

    def lane(value):
        return [(dp_swap, value)] if two else []

    def dp_gather(value, axis):
        return lax.all_gather(value, "dp", axis=axis, tiled=True)

    def dp_scatter(value, axis=0):
        return lax.psum_scatter(value, "dp", scatter_dimension=axis, tiled=True)

    def cut(value, k):
        return value[k * own_rows : (k + 1) * own_rows]

    number = jnp.arange(experts, dtype=jnp.int32)
    near_z, near_x, near_c = number % 4, (number // 4) % 2, number // 8
    row_index = ((z + 4 - near_z) % 4) * 4 + (near_x ^ x) * 2 + (near_c ^ core)
    few_index = jnp.concatenate([row_index[:4], row_index[8:12]])
    n_z, n_x, n_c = number // 4, (number // 2) % 2, number % 2
    block_index = ((z + 4 - n_z) % 4) * 4 + (n_x ^ x) * 2 + (n_c ^ core)

    pairs = HEADS // 2
    groups = shard // lat_rows
    piece = w_query.reshape(shard, pairs, 2, HD + RD).transpose(1, 0, 2, 3)
    piece = jnp.concatenate(
        [
            piece[..., :HD].reshape(pairs, shard, 2 * HD),
            piece[..., HD:].reshape(pairs, shard, 2 * RD),
            w_output.reshape(pairs, O_COLS, shard).transpose(0, 2, 1),
            w_expand.reshape(lat_rows, pairs, groups, E_COLS).transpose(1, 2, 0, 3).reshape(pairs, shard, E_COLS),
        ],
        axis=2,
    )
    piece = piece.reshape(4, 2, shard, W_COLS)
    kept, away = at(piece, core, 1), at(piece, 1 - core, 1)

    by_expert = jnp.sum(jnp.where(routes.T[None] == number[:, None, None], gates.T[None], 0.0), axis=1)
    gate_high = low(by_expert)
    gate_low = low(by_expert - wide(gate_high))

    def as_row(value):
        return jnp.pad(value.reshape(1, -1), ((0, 0), (0, own_rows - value.size)))

    small_rows = 48
    lat_gain_rows = lax.dynamic_update_slice(jnp.zeros((LAT,), BF), latent_gain, ((dp * experts + me) * lat_rows,))
    small = jnp.concatenate(
        [
            as_row(jnp.concatenate([norm_in, norm_mid])), lat_gain_rows.reshape(4, 128), as_row(low(lengths)),
            jnp.zeros((10, own_rows), BF), gate_high, gate_low,
        ],
        axis=0,
    )

    s_piece = jnp.concatenate(
        [
            shared_gate.reshape(shard, experts, ff_part).transpose(1, 0, 2),
            shared_up.reshape(shard, experts, ff_part).transpose(1, 0, 2),
            shared_down.reshape(experts, ff_part, shard).transpose(0, 2, 1),
        ],
        axis=2,
    ).reshape(4, 2, 2, shard, 3 * ff_part)
    own_expert = (expert_gate[0], expert_up[0], expert_down[0])
    x0 = tokens
    g0 = low(turn(cotangent))

    if two:
        fetched = [clock.add(value) for value in (own_expert[2], own_expert[0], own_expert[1])]
        wide_lat = jnp.pad(w_latent, ((0, 0), (0, 640 - lat_cols)))
        low_rows = jnp.pad(small, ((0, shard - small_rows), (0, 0)))
        lat = jnp.concatenate([wide_lat[:, :384], jnp.concatenate([wide_lat[:, 384:], low_rows], axis=1)], axis=0)
    else:
        lat = small
    s_kept, s_away = at(s_piece, core, 2), at(s_piece, 1 - core, 2)
    clock.slot(feed=0.65)
    moved, _, _, _ = clock.slot((core_swap, away), (core_swap, s_away), (z_up, x0), feed=0.59)
    x1 = moved[2]
    s_piece = jnp.stack([s_kept, moved[1]], axis=2)
    w_own = jnp.where(
        core == 0, jnp.concatenate([kept, moved[0]], axis=1), jnp.concatenate([moved[0], kept], axis=1)
    )
    if two:
        w_own = jnp.concatenate([w_own, jnp.broadcast_to(lat, (4,) + lat.shape)], axis=2)
    s_kept, s_away = at(s_piece, x, 1), at(s_piece, 1 - x, 1)
    moved, _, _, _ = clock.slot(
        (z_two, at(w_own, (z + 2) % 4, 0)),
        (z_up, at(w_own, (z + 1) % 4, 0)),
        (z_down, at(w_own, (z + 3) % 4, 0)),
        (x_swap, s_away),
        feed=1.17,
    )
    w_own = jnp.stack([at(w_own, z, 0), moved[1], moved[0], moved[2]])
    s_piece = jnp.stack([s_kept, moved[3]], axis=1)
    if two:
        lats = w_own[..., W_COLS:]
        facts = lats[:, shard : shard + small_rows, 256:]
    else:
        facts = jnp.stack([lat, z_up(lat), z_two(lat), z_down(lat)])

    moved, _, _, _ = clock.slot(
        (x_swap, w_own), *lane(w_own), (z_up, x1), (z_up, g0), (core_swap, lats if two else facts)
    )
    w_x, x2, g1, lat_other = moved[0], *moved[-3:]
    facts_few = jnp.concatenate([facts, lat_other[:, shard : shard + small_rows, 256:] if two else lat_other])
    lengths_few = facts_few[:, 5, : lengths.size].astype(jnp.int32).reshape(-1)
    scalars = jnp.concatenate([jnp.stack([dp, z, x, core]).astype(jnp.int32), lengths_few])
    table = jnp.asarray(angle_table(rows))
    s_two, s_up, s_down = (at(s_piece, (z + k) % 4, 0) for k in (2, 1, 3))
    if two:
        w_y = moved[1]
        moved, _, _, _ = clock.slot(
            (x_swap, w_y[:2]), (dp_swap, w_x[2:]), (z_up, x2),
            (core_swap, jnp.concatenate([w_x[..., W_COLS:], w_y[..., W_COLS:]])),
            (core_swap, jnp.concatenate([x0, x1])),
        )
        w_far, x3, lat_other_xy, cx01 = moved[:2], *moved[2:]
        lat_far = jnp.concatenate([w_far[0][..., W_COLS:], w_far[1][..., W_COLS:]])
        moved, _, _, _ = clock.slot(
            (core_swap, lat_far), (core_swap, jnp.concatenate([x2, x3])), (z_up, s_up), feed=0.5
        )
        cx23, s_up = moved[1:]
        weights = [w_own, w_x, w_y] + w_far
        layout_of = ((0, 0, 0), (1, 0, 0), (0, 1, 0), (1, 1, 0), (1, 1, 2))
        w_lat = [lat_other, lat_other_xy, moved[0]]
        w_exp = gains = gain_lat = jnp.zeros((8, 128), F32)
        route_from = [w_own, w_x, lat_other, lat_other_xy]
        route_lanes = (W_COLS + 256, W_COLS + 256, 256, 256)
    else:
        x3, s_up = z_up(x2), z_up(s_up)
        cx01, cx23 = core_swap(jnp.concatenate([x0, x1])), core_swap(jnp.concatenate([x2, x3]))
        near, far = dp_gather(w_own[None], 0), dp_gather(w_x[None], 0)
        weights = [near[i] for i in range(ndp)] + [far[i] for i in range(ndp)]
        layout_of = tuple((side, j, 0) for side in range(2) for j in range(ndp))
        w_lat = lax.all_gather(w_latent, ("dp", "expert"), axis=0)
        w_lat = [w_lat[i][None] for i in range(devices)]
        facts = lax.all_gather(small, ("dp", "expert"), axis=0)
        gains = wide(facts[:, 0, : 2 * shard]).reshape(devices, 2, shard).transpose(1, 0, 2).reshape(2, width)
        gain_lat = wide(facts[:, 1:5]).sum(axis=0).reshape(1, LAT)
        route_from = jnp.take(lax.dynamic_slice_in_dim(facts, dp * experts, experts, 0), row_index, axis=0)
        route_from = [route_from[4 * i : 4 * i + 4] for i in range(4)]
        route_lanes = (0, 0, 0, 0)
        w_exp = jnp.concatenate([value[..., Q_COLS + O_COLS :] for value in weights], axis=0)
        w_exp = w_exp.reshape(2, ndp, 4, 2 * shard, E_COLS).transpose(1, 2, 0, 3, 4)
        w_exp = w_exp.reshape(devices // 2, -1, E_COLS)
        chips = jnp.arange(devices // 2, dtype=jnp.int32)
        chip_index = chips // 8 * 8 + ((z + 4 - chips // 2 % 4) % 4) * 2 + (chips % 2 ^ x)
        w_exp = reorder([w_exp], chip_index)[0]
        w_exp = w_exp.reshape(devices, groups, lat_rows, E_COLS).transpose(0, 2, 1, 3).reshape(LAT, groups * E_COLS)
    slots = blocks * cap
    route = functools.partial(routing, first=(shard if two else 0) + 16, lanes=route_lanes, slots=cap)

    x_pieces = [x0, x1, x2, x3, cx01, cx23]
    moved, _, _, made = clock.slot(
        (x_swap, g0), (z_up, g1), (z_down, g0),
        feed=1.0,
        work=[
            (
                lambda *a: attention_forward(*a[:3], layout_of, *a[3:], split=two),
                scalars, x_pieces, weights, w_lat, w_exp, gains, gain_lat, table,
            )
        ],
    )
    gx0, g2, g3 = moved
    (part_near, part_far), saved = made[0]
    gain_in, gain_mid, gain_lat = saved[-3:]

    moved, _, _, _ = clock.slot((core_swap, part_far), (z_two, s_two), (z_down, s_down), feed=0.65)
    s_two, s_down = moved[1:]
    s_piece = jnp.stack([at(s_piece, z, 0), s_up, s_two, s_down]).reshape(experts, shard, 3 * ff_part)
    g_near = jnp.concatenate([g0, g1, g2, g3])
    terms = [wide(cut(part_near, k)) + wide(cut(moved[0], k)) for k in range(4)]
    moved, _, _, made = clock.slot(
        (z_down, low(terms[3])), (x_swap, g1), work=[(route, me.reshape(1), route_from)], feed=0.67
    )
    gx1 = moved[1]
    target_row, gate_row, target_col = made[0]
    moved, _, _, _ = clock.slot(
        (z_down, low(terms[2] + wide(moved[0]))), (x_swap, g2), (core_swap, g_near), feed=0.67
    )
    gx2, cg_near = moved[1:]
    moved, _, _, _ = clock.slot((z_down, low(terms[1] + wide(moved[0]))), (x_swap, g3), feed=0.67)
    gx3 = moved[1]
    xf = wide(tokens)
    mid = xf + terms[0] + wide(moved[0])
    scale_mid = rms_scale(mid)
    t0 = turn(low(mid * scale_mid * gain_mid))

    g_far = jnp.concatenate([gx0, gx1, gx2, gx3])
    join = lambda *pieces: jnp.concatenate(pieces, axis=0)
    moved, _, _, made = clock.slot(
        (z_up, t0), (x_swap, t0), work=[(join, *fetched[0][2])] if two else [], feed=0.67
    )
    t1, tx0 = moved
    down_got = made
    moved, _, _, _ = clock.slot((z_up, t1), (x_swap, t1), (core_swap, g_far), feed=0.67)
    t2, tx1, cg_far = moved
    g_pieces = [g0, g1, g2, g3, gx0, gx1, gx2, gx3, cg_near, cg_far]
    part = experts // 2
    moved, _, _, made = clock.slot(
        (z_up, t2), (x_swap, t2), *lane(s_piece[:part]), (core_swap, tx0),
        work=[(functools.partial(enter_grad, slots=slots), g_pieces, target_row, gate_row)],
    )
    t3, tx2 = moved[:2]
    s_got, ctx0 = moved[2:-1], moved[-1]
    *rows_g, share = made[0]
    t_near = jnp.concatenate([t0, t1, t2, t3])
    moved, _, _, made = clock.slot(
        (x_swap, t3), (core_swap, t_near), *lane(s_piece[part:]), (core_swap, tx1),
        work=[(join, *fetched[1][2])] if two else [],
    )
    tx3, ct_near = moved[:2]
    s_got, ctx1 = s_got + moved[2:-1], moved[-1]
    gate_got = made
    if two:
        s_pieces = [s_piece, jnp.concatenate(s_got)]
    else:
        s_pieces = jnp.split(dp_gather(s_piece[None], 0), ndp)
        s_pieces = [value.reshape(s_piece.shape) for value in s_pieces]
    moved, _, _, made = clock.slot(
        (core_swap, tx2), (core_swap, tx3), feed=0.4,
        work=[(lambda *a: shared_weights(a, block_index, ff_pad), *s_pieces)],
    )
    s_both, s_down_w = made[0]
    t_pieces = [t0, t1, t2, t3, tx0, tx1, tx2, tx3, ct_near, ctx0, ctx1, *moved]

    _, _, _, made = clock.slot(
        work=[
            (functools.partial(dispatch, slots=slots), t_pieces, target_row),
            (hidden_shared, t_pieces, g_pieces, s_both, s_down_w),
        ],
        feed=3.0,
    )
    rows_x, (s_act, d_s_pre) = made
    if two:
        assert all(entry[1] == entry[0].shape[0] for entry in fetched)
        own, other = own_expert, [gate_got[0], join(*fetched[2][2]), down_got[0]]
    else:
        full = [dp_gather(own_expert[0], 0), dp_gather(own_expert[1], 0), dp_gather(own_expert[2], 1)]
        own = [full[0][:half], full[1][:half], full[2][:, :half]]
        other = [full[0][half:], full[1][half:], full[2][:, half:]]
    _, _, _, made = clock.slot(work=[(expert_hidden, rows_x, rows_g, own, other)])
    e_act, d_gate, d_up, d_down_away = made[0]
    if two:
        sent = [clock.add(d_down_away)]

    _, _, _, made = clock.slot(
        work=[(expert_back, d_gate, d_up, own, other, target_col, d_s_pre, s_both)], feed=1.42
    )
    near, near_x, far, far_x = made[0]
    moved, _, _, made = clock.slot((core_swap, far_x), work=[(contract, rows_x[1], d_gate)], feed=0.35)
    if two:
        sent.append(clock.add(low(made[0])))
    away = [low(wide(cut(near_x, k)) + wide(cut(moved[0], k))) for k in range(4)]
    moved, _, _, made = clock.slot(
        (x_swap, away[3]), (core_swap, far),
        feed=0.75,
        work=[(functools.partial(shared_gradient, part=ff_part), t_pieces, g_pieces, d_s_pre, s_act)],
    )
    d_shared = made[0].reshape(ndp, experts, shard, 3 * ff_part)
    home = [wide(cut(near, k)) + wide(cut(moved[1], k)) for k in range(4)]
    moved, _, _, made = clock.slot(
        (x_swap, away[2]), (z_down, low(home[3] + wide(moved[0]))),
        feed=0.9,
        work=[(expert_out, e_act, share, own, other, target_col, s_act, s_down_w)],
    )
    o_near, o_near_x, o_far, o_far_x = made[0]
    s_away = d_shared[-1]
    moved, _, _, made = clock.slot(
        (x_swap, away[1]), (z_down, low(home[2] + wide(moved[0]) + wide(moved[1]))), (core_swap, o_far_x),
        *lane(s_away[:part]),
        work=[(contract, rows_x[1], d_up), (contract, e_act, rows_g[0])],
    )
    d_down_home = made[1]
    if two:
        sent.append(clock.add(low(made[0])))
    s_got = moved[3:]
    o_away = [low(wide(cut(o_near_x, k)) + wide(cut(moved[2], k))) for k in range(4)]
    moved, _, _, made = clock.slot(
        (x_swap, away[0]), (z_down, low(home[1] + wide(moved[0]) + wide(moved[1]))), (core_swap, o_far),
        *lane(s_away[part:]),
        work=[(contract, rows_x[0], d_gate)],
    )
    d_gate_home = made[0]
    s_got += moved[3:]
    o_home = [wide(cut(o_near, k)) + wide(cut(moved[2], k)) for k in range(4)]
    if two:
        d_shared = low(wide(d_shared[0]) + wide(jnp.concatenate(s_got)))
    else:
        d_shared = dp_scatter(d_shared)[0]
    d_shared = d_shared.reshape(4, 2, 2, shard, 3 * ff_part)
    d_mid_normed = turn(home[0] + wide(moved[0]) + wide(moved[1]))
    d_mid_in, d_gain_mid = rms_back(d_mid_normed, mid, scale_mid, gain_mid)
    d_mid = cotangent + d_mid_in

    a0 = low(d_mid)
    s_kept, s_away = at(d_shared, x, 1), at(d_shared, 1 - x, 1)
    moved, _, _, made = clock.slot(
        (z_up, a0), (x_swap, o_away[3]), lasting=1.45, work=[(contract, rows_x[0], d_up)]
    )
    a1, ox3 = moved
    d_up_home = made[0]
    moved, _, _, _ = clock.slot((z_up, a1), (x_swap, o_away[2]), fed_before=clock.lasting)
    a2, ox2 = moved
    moved, _, _, _ = clock.slot((z_up, a2), (x_swap, o_away[1]), feed=0.67)
    a3, ox1 = moved
    moved, _, _, _ = clock.slot(
        (core_swap, jnp.concatenate([a0, a1, a2, a3])), (x_swap, s_away),
        (z_down, low(o_home[3] + wide(ox3))), feed=0.6,
    )
    a_pieces = [a0, a1, a2, a3, moved[0]]
    d_shared = jnp.stack([s_kept, moved[1]], axis=1)
    o_sum = low(o_home[2] + wide(ox2) + wide(moved[2]))
    backward = functools.partial(attention_backward, lat_rows=lat_rows)
    moved, _, _, made = clock.slot(
        (z_two, at(d_shared, (z + 2) % 4, 0)), (z_up, at(d_shared, (z + 1) % 4, 0)),
        (z_down, at(d_shared, (z + 3) % 4, 0)), (z_down, o_sum),
        feed=1.6,
        work=[(backward, scalars, x_pieces, a_pieces, saved, d_gain_mid.reshape(1, width), table)],
    )
    d_shared = jnp.stack([at(d_shared, z, 0), moved[1], moved[0], moved[2]])
    o_sum = low(o_home[1] + wide(ox1) + wide(moved[3]))
    d_norm, d_head, d_wl = made[0]
    same_x = [[i for i in range(experts) if i // 2 % 2 == side] for side in range(2)]
    d_normed = lax.psum_scatter(d_norm, "expert", scatter_dimension=0, axis_index_groups=same_x, tiled=True)

    if not two:
        d_head = d_head.reshape(ndp, 4, 2, 2 * shard, W_COLS)
        d_wl = d_wl.reshape(ndp, 4, 2, 2, shard, -1)
    s_kept, s_away = at(d_shared, core, 2), at(d_shared, 1 - core, 2)

    def add_received(home, *pieces):
        return home + wide(jnp.concatenate(pieces))

    if two:
        moved, _, _, made = clock.slot(
            (x_swap, d_head[4:8]), (dp_swap, d_head[12:]), (core_swap, d_wl[1]), (core_swap, s_away),
            work=[(add_received, d_down_home, *sent[0][2])],
        )
        d_down = made[0]
        first = (wide(d_head[:4]) + wide(moved[0])).reshape(ndp, 2, 2 * shard, W_COLS)
        second = (wide(d_head[8:12]) + wide(moved[1])).reshape(2, 2, 2 * shard, W_COLS)
        d_wl = (wide(d_wl[0]) + wide(moved[2])).reshape(ndp, 4, 2, shard, -1)
        d_shared = jnp.stack([s_kept, moved[3]], axis=2)
        moved, _, _, made = clock.slot(
            (dp_swap, low(at(first, 1 - dp, 0))), (x_swap, low(at(second, 1 - x, 1))),
            (x_swap, low(at(d_wl, 1 - x, 2))), (z_down, o_sum), feed=0.45,
            work=[(add_received, d_gate_home, *sent[1][2])],
        )
        d_gate_all = made[0]
        o_last = o_home[0] + wide(moved[3])
        first = at(first, dp, 0) + wide(moved[0])
        second = at(second, x, 1) + wide(moved[1])
        d_wl = at(d_wl, x, 2) + wide(moved[2])
        d_head = low(jnp.concatenate([first, second]))
    else:
        d_head = wide(at(d_head, x, 2)) + wide(x_swap(at(d_head, 1 - x, 2)))
        d_head = dp_scatter(low(d_head))[0]
        d_wl = wide(at(d_wl, core, 3)) + wide(core_swap(at(d_wl, 1 - core, 3)))
        d_wl = at(d_wl, x, 2) + wide(x_swap(low(at(d_wl, 1 - x, 2))))
        d_shared = jnp.stack([s_kept, core_swap(s_away)], axis=2)
        o_last = o_home[0] + wide(z_down(o_sum))
    d_shared = d_shared.reshape(experts, shard, 3 * ff_part)
    moved, _, _, _ = clock.slot(
        (z_two, at(d_head, (z + 2) % 4, 0)), (z_down, at(d_head, (z + 3) % 4, 0)),
        (z_up, at(d_head, (z + 1) % 4, 0)),
        *(lane(low(at(d_wl, 1 - dp, 0))) if two else []), feed=3.0,
    )
    d_head = jnp.stack([at(d_head, z, 0), moved[1], moved[0], moved[2]]).reshape(4, 2, shard, W_COLS)
    d_wl = at(d_wl, dp, 0) + wide(moved[3]) if two else wide(dp_scatter(low(d_wl))[0])
    moved, _, ended, made = clock.slot(
        (core_swap, at(d_head, 1 - core, 1)), (z_two, low(at(d_wl, (z + 2) % 4, 0))),
        (z_down, low(at(d_wl, (z + 3) % 4, 0))), (z_up, low(at(d_wl, (z + 1) % 4, 0))), (x_swap, o_away[0]),
        end=[d_normed], work=[(add_received, d_up_home, *sent[2][2])] if two else [],
    )
    d_up_all = made[0] if two else None
    out = low(mid + turn(o_last + wide(moved[4])))
    d_head = jnp.stack([at(d_head, core, 1), moved[0]], axis=1).reshape(pairs, shard, W_COLS)
    d_wl = at(d_wl, z, 0) + wide(moved[1]) + wide(moved[2]) + wide(moved[3])
    d_normed = wide(ended[0])

    if two:
        assert all(entry[1] == entry[0].shape[0] for entry in sent)
        d_expert = [d_gate_all, d_up_all, d_down]
    else:
        d_expert = [
            wide(dp_scatter(low(jnp.concatenate([contract(value, d) for value in rows_x]))))
            for d in (d_gate, d_up)
        ]
        d_expert.append(wide(dp_scatter(low(jnp.concatenate([contract(e_act, value) for value in rows_g], axis=1)), 1)))
    d_in, _ = rms_back(d_normed, xf, rms_scale(xf), gain_in)
    d_tokens = d_mid + d_in
    d_shared = wide(reorder([d_shared], block_index)[0])
    grad_sg, grad_su = (
        d_shared[:, :, i * ff_part : (i + 1) * ff_part].transpose(1, 0, 2).reshape(shard, ff_s) for i in range(2)
    )
    grad_sd = d_shared[:, :, 2 * ff_part :].transpose(0, 2, 1).reshape(ff_s, shard)
    pair_number = jnp.arange(pairs, dtype=jnp.int32)
    pair_index = ((pair_number // 2 + 4 - z) % 4) * 2 + (pair_number % 2 ^ core)
    if two:
        grad_wq, grad_wo, grad_we = unpack(d_head, pair_index, lat_rows)
        grad_wo = grad_wo.T
    else:
        d_head = wide(reorder([d_head], pair_index)[0])
        grad_wq = jnp.concatenate(
            [
                d_head[..., : 2 * HD].reshape(pairs, shard, 2, HD),
                d_head[..., 2 * HD : Q_COLS].reshape(pairs, shard, 2, RD),
            ],
            axis=3,
        )
        grad_wq = grad_wq.transpose(1, 0, 2, 3).reshape(shard, HEADS * (HD + RD))
        grad_wo = d_head[..., Q_COLS : Q_COLS + O_COLS].transpose(0, 2, 1).reshape(HEADS * VD, shard)
        grad_we = d_head[..., Q_COLS + O_COLS :].reshape(pairs, groups, lat_rows, E_COLS).transpose(2, 0, 1, 3)
        grad_we = grad_we.reshape(lat_rows, HEADS * (HD + VD))
    return (
        out,
        d_tokens,
        d_wl[:, lat_cols],
        d_wl[:lat_rows, lat_cols + 2],
        d_wl[:, lat_cols + 1],
        grad_wq,
        d_wl[:, :lat_cols],
        grad_we,
        grad_wo,
        grad_sg,
        grad_su,
        grad_sd,
        d_expert[0][None],
        d_expert[1][None],
        d_expert[2][None],
    )


def solution(mesh):
    rows = P(("dp", "expert"), None)
    vector = P(("dp", "expert"))
    columns = P(None, ("dp", "expert"))
    by_row = P("expert", "dp", None)
    by_column = P("expert", None, "dp")
    return jax.shard_map(
        local,
        mesh=mesh,
        in_specs=(
            rows, rows, rows, rows, vector, vector, vector, rows, rows, rows, columns, rows, rows, columns, by_row,
            by_row, by_column, rows,
        ),
        out_specs=(
            rows, rows, vector, vector, vector, rows, rows, rows, columns, rows, rows, columns, by_row, by_row,
            by_column,
        ),
        check_vma=False,
    )
```

```python
import functools

import jax
import jax.numpy as jnp
import ml_dtypes
import numpy as np
from jax import lax
from jax.experimental import pallas as pl
from jax.experimental.pallas import tpu as pltpu
from jax.sharding import PartitionSpec as P

HEADS = 16
HD = 128
RD = 64
VD = 128
LAT = 512
TOP = 6
EPS = 1e-06
CHUNK = 256
SCALE = (HD + RD) ** (-0.5)
BF = jnp.bfloat16
F32 = jnp.float32
VMEM_LIMIT = 60 * 1024 * 1024
Q_COLS = 2 * (HD + RD)
O_COLS = 2 * VD
E_COLS = 128
LAT_AT = Q_COLS
ROT_AT = Q_COLS + LAT
PROJ = ROT_AT + 128
W_COLS = Q_COLS + O_COLS + E_COLS
HIDDEN_TILE = 256


def matmul(left, right):
    return jnp.dot(left, right, preferred_element_type=F32)


def mat_trans(left, right):
    return lax.dot_general(left, right, (((1,), (1,)), ((), ())), preferred_element_type=F32)


def contract(left, right):
    return lax.dot_general(left, right, (((0,), (0,)), ((), ())), preferred_element_type=F32)


def rms_scale(values):
    return lax.rsqrt(jnp.mean(values * values, axis=-1, keepdims=True) + EPS)


def rms_back(incoming, values, scale, gain):
    scaled = incoming * gain
    inner = jnp.mean(scaled * values, axis=-1, keepdims=True)
    grad_in = scale * (scaled - values * scale * scale * inner)
    grad_gain = jnp.sum(incoming * values * scale, axis=0)
    return (grad_in, grad_gain)


def low(value):
    return value.astype(BF)


def wide(value):
    return value.astype(F32)


def move(value, to):
    return lax.ppermute(value, "expert", [(i, to(i)) for i in range(16)])


def z_up(value):
    return move(value, lambda i: (i + 4) % 16)


def z_down(value):
    return move(value, lambda i: (i + 12) % 16)


def z_two(value):
    return move(value, lambda i: (i + 8) % 16)


def x_swap(value):
    return move(value, lambda i: i ^ 2)


def core_swap(value):
    return move(value, lambda i: i ^ 1)


class Clock:
    def __init__(self, go):
        self.last = ()
        self.go = go
        self.queue = []

    def add(self, array):
        self.queue.append([array, 0, []])
        return self.queue[-1]

    def next_rows(self, size):
        moves, entries = [], []
        for entry in self.queue:
            array, start, _ = entry
            total = array.shape[0]
            line = array.size // total * array.dtype.itemsize
            count = round(size / line / 32) * 32
            if start == total or count < 64:
                continue
            stop = start + count
            stop = total if total - stop < 64 else stop
            entry[1] = stop
            moves.append((self.go, array[start:stop]))
            entries.append(entry)
            size -= (stop - start) * line
        return moves, entries

    def slot(self, *moves, begin=(), end=(), work=(), feed=0, lasting=0, fed_before=()):
        later, later_entries = self.next_rows(lasting * 1e6)
        begin = list(begin) + later
        waited = [entry[2][place] for entry, place in fed_before]
        end = waited + list(end)
        fed, entries = self.next_rows(feed * 1e6)
        moves = fed + list(moves)
        count, late = len(moves), len(moves) + len(begin)
        args, tree = jax.tree.flatten([list(rest) for _, *rest in work])
        values = [value for _, value in moves + list(begin)]
        tied = lax.optimization_barrier(tuple(values + args) + self.last)
        moved = [go(value) for (go, _), value in zip(moves, tied)]
        begun = [go(value) for (go, _), value in zip(begin, tied[count:])]
        args = jax.tree.unflatten(tree, tied[late : late + len(args)])
        made = [job[0](*some) for job, some in zip(work, args)]
        flat, tree = jax.tree.flatten(made)
        self.last = lax.optimization_barrier(tuple(moved) + tuple(end) + tuple(flat))
        moved, ended = list(self.last[:count]), list(self.last[count : count + len(end)])
        for entry in entries:
            entry[2].append(moved.pop(0))
        for entry, place in fed_before:
            entry[2][place] = ended.pop(0)
        self.lasting = []
        for entry in later_entries:
            self.lasting.append((entry, len(entry[2])))
            entry[2].append(begun.pop(len(begun) - len(later_entries) + len(self.lasting) - 1))
        return moved, begun, ended, jax.tree.unflatten(tree, self.last[count + len(end) :])


    def tie(self, value):
        return lax.optimization_barrier((value,) + self.last)[0]


def joined(entry):
    assert entry[1] == entry[0].shape[0]
    return jnp.concatenate(entry[2], axis=0)


def at(value, index, axis):
    return lax.dynamic_index_in_dim(value, index, axis, keepdims=False)


def whole_call(kernel, args, outs, scratch=(), flops=0, scalars=None):
    size = sum(a.size * a.dtype.itemsize for a in list(args) + list(outs))
    vmem = pl.BlockSpec(memory_space=pltpu.VMEM)
    specs = [vmem] * len(args)
    if scalars is not None:
        args = [scalars] + list(args)
        specs = [pl.BlockSpec(memory_space=pltpu.SMEM)] + specs
    return pl.pallas_call(
        kernel,
        in_specs=specs,
        out_specs=[vmem] * len(outs),
        out_shape=list(outs),
        scratch_shapes=list(scratch),
        compiler_params=pltpu.CompilerParams(vmem_limit_bytes=VMEM_LIMIT),
        cost_estimate=pl.CostEstimate(flops=flops, bytes_accessed=size, transcendentals=0),
    )(*args)


def shaped(shape, kind):
    return jax.ShapeDtypeStruct(shape, kind)


def reorder_kernel(count, parts, index_ref, *refs):
    for in_ref, out_ref in zip(refs[: len(refs) // 2], refs[len(refs) // 2 :]):
        pad = out_ref.shape[2] // parts
        width = in_ref.shape[2] // parts
        for i in range(count):
            value = in_ref[index_ref[i]]
            if pad == width:
                out_ref[i] = value
            else:
                spare = jnp.zeros((value.shape[0], pad - width), value.dtype)
                for part in range(parts):
                    cut = value[:, part * width : (part + 1) * width]
                    out_ref[i, :, part * pad : (part + 1) * pad] = jnp.concatenate([cut, spare], axis=1)


def shared_kernel_in(count, parts, index_ref, *refs):
    in_refs, (both_ref, down_ref) = refs[:-2], refs[-2:]
    pad = down_ref.shape[1]
    for k, in_ref in enumerate(in_refs):
        rows, columns = in_ref.shape[1], in_ref.shape[2] // parts
        spare = jnp.zeros((rows, pad - columns), in_ref.dtype)
        for i in range(count):
            value = in_ref[index_ref[i]]
            line = slice((k * count + i) * rows, (k * count + i + 1) * rows)
            for part in range(parts):
                cut = jnp.concatenate([value[:, part * columns : (part + 1) * columns], spare], axis=1)
                if part < parts - 1:
                    both_ref[line, part * pad : (part + 1) * pad] = cut
                else:
                    down_ref[line, :] = cut


def shared_weights(arrays, index, pad):
    rows = sum(a.shape[0] * a.shape[1] for a in arrays)
    outs = [shaped((rows, 2 * pad), BF), shaped((rows, pad), BF)]
    return whole_call(functools.partial(shared_kernel_in, index.shape[0], 3), arrays, outs, scalars=index)


def reorder(arrays, index, parts=1, pad=0):
    count = index.shape[0]
    outs = [shaped(a.shape[:2] + (a.shape[2] if not pad else parts * pad,), a.dtype) for a in arrays]
    return whole_call(functools.partial(reorder_kernel, count, parts), arrays, outs, scalars=index)


def unpack_kernel(index_ref, in_ref, wq_ref, wo_ref, we_ref):
    rows = we_ref.shape[0]
    for a in range(in_ref.shape[0]):
        value = wide(in_ref[index_ref[a]])
        parts = [value[:, :HD], value[:, 2 * HD : 2 * HD + RD], value[:, HD : 2 * HD], value[:, 2 * HD + RD : Q_COLS]]
        wq_ref[:, a * Q_COLS : (a + 1) * Q_COLS] = jnp.concatenate(parts, axis=1)
        wo_ref[:, a * O_COLS : (a + 1) * O_COLS] = value[:, Q_COLS : Q_COLS + O_COLS]
        for g in range(4):
            we_ref[:, (4 * a + g) * E_COLS : (4 * a + g + 1) * E_COLS] = value[g * rows : (g + 1) * rows, Q_COLS + O_COLS :]


def unpack(blocks, index, rows):
    pairs, shard, _ = blocks.shape
    outs = [
        shaped((shard, pairs * Q_COLS), F32), shaped((shard, pairs * O_COLS), F32), shaped((rows, 4 * pairs * E_COLS), F32)
    ]
    return whole_call(unpack_kernel, [blocks], outs, scalars=index)


def swap_halves(values):
    lane = lax.broadcasted_iota(jnp.int32, values.shape, 1)
    return jnp.where(
        lane % RD < RD // 2, pltpu.roll(values, 2 * RD - RD // 2, 1), pltpu.roll(values, RD // 2, 1)
    )


def probabilities(q_main, q_rot, k_main, k_rot, allowed):
    scores = (mat_trans(q_main, k_main) + mat_trans(q_rot, k_rot)) * SCALE
    scores = jnp.where(allowed, scores, -1e30)
    expo = jnp.exp(scores - jnp.max(scores, axis=-1, keepdims=True))
    return expo / jnp.sum(expo, axis=-1, keepdims=True)


def allowed_pairs(id_col, id_row):
    shape = (id_col.shape[0], id_row.shape[1])
    key = lax.broadcasted_iota(jnp.int32, shape, 1)
    query = lax.broadcasted_iota(jnp.int32, shape, 0)
    return (id_col == id_row) & (key <= query)


def angle_table(rows):
    freq = np.power(np.float32(10000.0), np.float32(-2.0) * np.arange(RD // 2, dtype=np.float32) / np.float32(RD))
    theta = np.arange(rows, dtype=np.float32)[:, None] * freq.astype(np.float32)
    cosine, sine = np.cos(theta), np.sin(theta)
    terms = []
    for value in (np.concatenate([cosine] * 4, axis=1), np.concatenate([-sine, sine, -sine, sine], axis=1)):
        rest = value.astype(np.float32)
        for _ in range(3):
            term = rest.astype(ml_dtypes.bfloat16)
            terms.append(term)
            rest = rest - term.astype(np.float32)
    return np.concatenate(terms, axis=1)


def chunk_layout(facts_ref, j, rows, shape):
    count = CHUNK // rows
    number = lax.broadcasted_iota(jnp.int32, shape, 0 if shape[0] == CHUNK else 1)
    block, place = number // rows, number % rows
    doc, start, ends = 0, 0, [0] * count
    for k in range(3):
        lengths = [facts_ref[4 + (j * count + b) * 4 + k] for b in range(count)]
        ends = [end + length for end, length in zip(ends, lengths)]
        end, length = ends[-1], lengths[-1]
        for b in range(count - 2, -1, -1):
            end = jnp.where(block == b, ends[b], end)
            length = jnp.where(block == b, lengths[b], length)
        passed = place >= end
        doc = doc + passed.astype(jnp.int32)
        start = start + jnp.where(passed, length, 0)
    return place - start, doc + 4 * block


def chunk_tables(facts_ref, table_ref, j):
    rows = table_ref.shape[0]
    position, id_col = chunk_layout(facts_ref, j, rows, (CHUNK, 1))
    id_row = chunk_layout(facts_ref, j, rows, (1, CHUNK))[1]
    hot = low(lax.broadcasted_iota(jnp.int32, (CHUNK, rows), 1) == position)
    terms = matmul(hot, table_ref[...])
    cosine = terms[:, :128] + terms[:, 128:256] + terms[:, 256:384]
    sine = terms[:, 384:512] + terms[:, 512:640] + terms[:, 640:]
    return cosine, sine, allowed_pairs(id_col, id_row)


def pair(refs, j):
    pieces, start = [], 0
    for ref in refs:
        low_row, high_row = max(start, CHUNK * j), min(start + ref.shape[0], CHUNK * (j + 1))
        if low_row < high_row:
            pieces.append(ref[low_row - start : high_row - start, :])
        start += ref.shape[0]
    return pieces[0] if len(pieces) == 1 else jnp.concatenate(pieces, axis=0)


def forward_kernel(ndp, layout_of, pieces, count, split, place_ref, *refs):
    x_refs, refs = refs[:pieces], refs[pieces:]
    w_refs, refs = refs[: len(layout_of)], refs[len(layout_of) :]
    wl_refs, refs = refs[:count], refs[count:]
    we_ref, gains_ref, lg_ref, table_ref = refs[:4]
    near_ref, far_ref, q_ref, kr_ref, lat_ref, kv_ref, att_ref, wp_ref, wo_ref, exp_ref, gain_ref, mid_ref, lgo_ref = refs[4:]
    other_rows = [(ref, i) for ref in wl_refs for i in range(ref.shape[0])]
    dp, z, x, core = place_ref[0], place_ref[1], place_ref[2], place_ref[3]
    block = w_refs[0].shape[1]
    shard = block // 2
    lat_rows = jnp.zeros((4, 128), F32)
    spare = jnp.zeros((shard, 128 - RD), BF)
    turn = 0
    for w_ref, (far, j, first) in zip(w_refs, layout_of):
        y = j ^ dp if ndp == 2 else j
        for k in range(w_ref.shape[0]):
            row = ((y * 4 + lax.rem(z + 4 - first - k, 4)) * 2 + (x ^ far)) * block
            row = pl.multiple_of(row, block)
            wp_ref[pl.ds(row, block), :Q_COLS] = w_ref[k, :, :Q_COLS]
            wo_ref[pl.ds(row, block), :] = w_ref[k, :, Q_COLS : Q_COLS + O_COLS]
            if not split:
                continue
            here = pl.multiple_of(row + core * shard, shard)
            there = pl.multiple_of(row + (1 - core) * shard, shard)
            for at_row, lat in ((here, w_ref[k, :, W_COLS:]), (there, other_rows[turn][0][other_rows[turn][1]])):
                wp_ref[pl.ds(at_row, shard), LAT_AT : LAT_AT + 384] = lat[:shard, :]
                wp_ref[pl.ds(at_row, shard), LAT_AT + 384 :] = lat[shard:, :256]
            here_rows, there_rows = (
                wide(lat[shard : shard + 16, 256:]) for lat in (w_ref[k, :, W_COLS:], other_rows[turn][0][other_rows[turn][1]])
            )
            left = jnp.where(core == 0, here_rows[:1, :], there_rows[:1, :])
            right = jnp.where(core == 0, there_rows[:1, :], here_rows[:1, :])
            gain_ref[:, pl.ds(row, block)] = jnp.concatenate([left[:, :shard], right[:, :shard]], axis=1)
            mid_ref[:, pl.ds(row, block)] = jnp.concatenate([left[:, shard:], right[:, shard:]], axis=1)
            lat_rows = lat_rows + here_rows[1:5, :] + there_rows[1:5, :]
            turn += 1
            small = shard // 4
            for c in range(2):
                for g in range(4):
                    at_row = pl.multiple_of(row // 4 + c * small, small)
                    exp_ref[pl.ds(at_row, small), g * HD : (g + 1) * HD] = w_ref[
                        k, c * shard + g * small : c * shard + (g + 1) * small, Q_COLS + O_COLS : W_COLS
                    ]
    if not split:
        for i, (wl_ref, _) in enumerate(other_rows):
            wp_ref[i * shard : (i + 1) * shard, LAT_AT:] = jnp.concatenate([wl_ref[i, :shard, :], spare], axis=1)
        exp_ref[...] = we_ref[...]
        gain_ref[...] = gains_ref[:1, :]
        mid_ref[...] = gains_ref[1:2, :]
        lgo_ref[...] = lg_ref[...]
    else:
        lgo_ref[...] = jnp.concatenate([lat_rows[i : i + 1, :] for i in range(4)], axis=1)
    gain, lat_gain = gain_ref[...], lgo_ref[...]
    for j in range(4):
        rows = slice(CHUNK * j, CHUNK * (j + 1))
        xf = wide(pair(x_refs, j))
        normed = low(xf * rms_scale(xf) * gain)
        proj = matmul(normed, wp_ref[...])
        cosine, sine, allowed = chunk_tables(place_ref, table_ref, j)
        q_mix = proj[:, 2 * HD : Q_COLS]
        k_mix = proj[:, ROT_AT:]
        q_rot = low(q_mix * cosine + swap_halves(q_mix) * sine)
        k_rot = k_mix * cosine + swap_halves(k_mix) * sine
        k_turned = low(pltpu.roll(k_rot, RD, 1))
        k_rot = low(k_rot)
        q_main = low(proj[:, : 2 * HD])
        lat = proj[:, LAT_AT:ROT_AT]
        lat_ref[rows, :] = lat
        compressed = low(lat * rms_scale(lat) * lat_gain)
        expanded = low(matmul(compressed, exp_ref[...]))
        q_ref[rows, : 2 * HD] = q_main
        q_ref[rows, 2 * HD :] = q_rot
        kr_ref[rows, :] = k_rot
        kv_ref[rows, :] = expanded
        attended = []
        for head, k_side in ((0, k_rot), (1, k_turned)):
            k_main = expanded[:, 2 * head * HD : (2 * head + 1) * HD]
            values = expanded[:, (2 * head + 1) * HD : (2 * head + 2) * HD]
            probs = probabilities(q_main[:, head * HD : (head + 1) * HD], q_rot, k_main, k_side, allowed)
            attended.append(low(matmul(low(probs), values)))
        attended = jnp.concatenate(attended, axis=1)
        att_ref[rows, :] = attended
        put_half(near_ref, far_ref, j, 4, low(mat_trans(attended, wo_ref[...])))


def put_half(near_ref, far_ref, j, count, value):
    ref = near_ref if j < count // 2 else far_ref
    j = j % (count // 2)
    ref[j * CHUNK : (j + 1) * CHUNK, :] = value


def attention_forward(place, x_pieces, weights, layout_of, w_lat, w_exp, gains, lat_gain, table, split):
    own, width = x_pieces[0].shape
    rows = 8 * own
    args = list(x_pieces) + list(weights) + list(w_lat) + [w_exp, gains, lat_gain, table]
    outs = [shaped((rows // 2, width), BF)] * 2 + [
        shaped((rows, Q_COLS), BF),
        shaped((rows, 128), BF),
        shaped((rows, LAT), F32),
        shaped((rows, 4 * HD), BF),
        shaped((rows, O_COLS), BF),
        shaped((width, PROJ), BF),
        shaped((width, O_COLS), BF),
        shaped((LAT, 4 * HD), BF),
        shaped((1, width), F32),
        shaped((1, width), F32),
        shaped((1, LAT), F32),
    ]
    kernel = functools.partial(forward_kernel, lax.axis_size("dp"), layout_of, len(x_pieces), len(w_lat), split)
    flops = 2 * rows * width * (PROJ + O_COLS)
    out = whole_call(kernel, args, outs, flops=flops, scalars=place)
    return out[:2], out[2:]


def backward_kernel(pieces, count, lat_rows, place_ref, *refs):
    x_refs, g_refs, refs = refs[:pieces], refs[pieces : pieces + count], refs[pieces + count :]
    q_ref, kr_ref, lat_ref, kv_ref, att_ref, wp_ref, wo_ref, we_ref, gain_ref, mid_ref, lg_ref, dm_ref = refs[:12]
    table_ref, dn_ref, dw_ref, dl_ref, de_ref, acc_q, acc_o, acc_e, dg_ref, dlg_ref = refs[12:]
    split = len(dw_ref.shape) > 2
    dp, z, x, core = place_ref[0], place_ref[1], place_ref[2], place_ref[3]
    own = x_refs[0].shape[0]
    gain, w_exp, lat_gain = gain_ref[...], we_ref[...], lg_ref[...]

    def add(acc, value, first):
        acc[...] = value if first else acc[...] + value

    for j in range(4):
        rows = slice(CHUNK * j, CHUNK * (j + 1))
        xf = wide(pair(x_refs, j))
        whitened = xf * rms_scale(xf)
        normed = low(whitened * gain)
        lat = lat_ref[rows, :]
        lat_scale = rms_scale(lat)
        white_lat = lat * lat_scale
        grad = pair(g_refs, j)
        cosine, sine, allowed = chunk_tables(place_ref, table_ref, j)
        d_att = low(matmul(grad, wo_ref[...]))
        q_rot, k_rot = q_ref[rows, 2 * HD :], kr_ref[rows, :]
        k_turned = low(pltpu.roll(wide(k_rot), RD, 1))
        d_main, d_expanded = [], []
        dq_mix = None
        dk_mix = None
        for head, k_side in ((0, k_rot), (1, k_turned)):
            q_main = q_ref[rows, head * HD : (head + 1) * HD]
            k_main = kv_ref[rows, 2 * head * HD : (2 * head + 1) * HD]
            values = kv_ref[rows, (2 * head + 1) * HD : (2 * head + 2) * HD]
            probs = probabilities(q_main, q_rot, k_main, k_side, allowed)
            d_out = d_att[:, head * HD : (head + 1) * HD]
            d_prob = mat_trans(d_out, values)
            d_values = contract(low(probs), d_out)
            d_scores = low(probs * (d_prob - jnp.sum(probs * d_prob, axis=-1, keepdims=True)))
            d_main.append(matmul(d_scores, k_main) * SCALE)
            d_expanded += [contract(d_scores, q_main) * SCALE, d_values]
            dq_one = matmul(d_scores, k_side)
            dk_one = contract(d_scores, q_rot)
            dq_mix = dq_one if head == 0 else dq_mix + dq_one
            dk_mix = dk_one if head == 0 else dk_mix + pltpu.roll(dk_one, RD, 1)
        dq_mix = dq_mix * SCALE
        dk_mix = dk_mix * SCALE
        dq_mix = dq_mix * cosine - swap_halves(dq_mix) * sine
        dk_mix = dk_mix * cosine - swap_halves(dk_mix) * sine
        dk_mix = jnp.where(lax.broadcasted_iota(jnp.int32, dk_mix.shape, 1) < RD, dk_mix, 0.0)
        d_expanded = low(jnp.concatenate(d_expanded, axis=1))
        d_comp = mat_trans(d_expanded, w_exp)
        scaled = d_comp * lat_gain
        d_lat = lat_scale * (scaled - white_lat * jnp.mean(scaled * white_lat, axis=-1, keepdims=True))
        d_proj = low(jnp.concatenate(d_main + [dq_mix, d_lat, dk_mix], axis=1))
        d_normed = mat_trans(d_proj, wp_ref[...])
        part = low(d_normed)
        for k in range(2):
            piece = 2 * j + k
            place = lax.rem(z + 4 - piece % 4, 4) * 2 + (core ^ (piece // 4))
            dn_ref[pl.ds(pl.multiple_of(place * own, own), own), :] = part[k * own : (k + 1) * own, :]
        add(dg_ref, jnp.sum(d_normed * whitened, axis=0, keepdims=True), j == 0)
        add(dlg_ref, jnp.sum(d_comp * white_lat, axis=0, keepdims=True), j == 0)
        add(acc_q, contract(d_proj, normed), j == 0)
        add(acc_o, contract(att_ref[rows, :], grad), j == 0)
        add(acc_e, contract(low(white_lat * lat_gain), d_expanded), j == 0)
    shard = acc_q.shape[1] * lat_rows // LAT
    lane = lax.broadcasted_iota(jnp.int32, (LAT, acc_q.shape[1]), 1)
    line = lax.broadcasted_iota(jnp.int32, (LAT, acc_q.shape[1]), 0)
    spread = low((line // lat_rows == lane // shard) & (line % lat_rows == lane % shard))
    spread = matmul(low(jnp.broadcast_to(dlg_ref[...], (8, LAT))), spread)[:1, :]
    acc_q[ROT_AT + RD : ROT_AT + RD + 8, :] = jnp.concatenate(
        [dg_ref[...], dm_ref[...], spread, jnp.zeros((5, acc_q.shape[1]), F32)], axis=0
    )
    if not split:
        dw_ref[:, :Q_COLS] = low(acc_q[:Q_COLS, :].T)
        dw_ref[:, Q_COLS : Q_COLS + O_COLS] = low(acc_o[...].T)
        dl_ref[...] = low(acc_q[Q_COLS:, :].T)
        de_ref[...] = low(acc_e[...])
        return
    block = 2 * shard
    for number in range(acc_q.shape[1] // block):
        y, zz, xx = number // 8, number // 2 % 4, number % 2
        lanes = slice(number * block, (number + 1) * block)
        slot = (x ^ xx) * 4 + y * 2 + zz if zz < 2 else 8 + (dp ^ y) * 4 + (zz - 2) * 2 + xx
        dw_ref[slot, :, :Q_COLS] = low(acc_q[:Q_COLS, lanes].T)
        dw_ref[slot, :, Q_COLS : Q_COLS + O_COLS] = low(acc_o[:, lanes].T)
        for c in range(2):
            for g in range(4):
                row = c * shard + g * lat_rows
                i = number * 2 + c
                dw_ref[slot, row : row + lat_rows, Q_COLS + O_COLS :] = low(
                    acc_e[i * lat_rows : (i + 1) * lat_rows, g * HD : (g + 1) * HD]
                )
        both = low(acc_q[Q_COLS:, lanes].T)
        for c in range(2):
            dl_ref[core ^ c, number, :, :] = both[c * shard : (c + 1) * shard, :]


def attention_backward(place, x_pieces, g_pieces, saved, d_gain_mid, table, lat_rows):
    own, width = x_pieces[0].shape
    q, kr, lat, kv, att, wp, wo, w_exp, gain, mid, lat_gain = saved
    args = list(x_pieces) + list(g_pieces)
    args += [q, kr, lat, kv, att, wp, wo, w_exp, gain, mid, lat_gain, d_gain_mid, table]
    outs = [
        shaped((8 * own, width), BF),
        shaped((width, W_COLS), BF),
        shaped((width, PROJ - Q_COLS), BF),
        shaped((LAT, 4 * HD) if lat_rows % 16 else (16, 128), BF),
    ]
    shard = width * lat_rows // LAT
    if not lat_rows % 16:
        outs[1] = shaped((width // (2 * shard), 2 * shard, W_COLS), BF)
        outs[2] = shaped((2, width // (2 * shard), shard, PROJ - Q_COLS), BF)
    scratch = (
        pltpu.VMEM((PROJ, width), F32), pltpu.VMEM((O_COLS, width), F32), pltpu.VMEM((LAT, 4 * HD), F32),
        pltpu.VMEM((1, width), F32), pltpu.VMEM((1, LAT), F32),
    )
    flops = 2 * 8 * own * width * (2 * PROJ + 2 * O_COLS)
    kernel = functools.partial(backward_kernel, len(x_pieces), len(g_pieces), lat_rows)
    d_norm, d_head, d_wl, d_we = whole_call(kernel, args, outs, scratch, flops=flops, scalars=place)
    if lat_rows % 16:
        d_we = d_we.reshape(width // shard, lat_rows, 4, E_COLS).transpose(0, 2, 1, 3).reshape(width, E_COLS)
        d_head = jnp.concatenate([d_head[:, : Q_COLS + O_COLS], d_we], axis=1)
    return d_norm, d_head, d_wl


def routing_kernel(first, lanes, slots, me_ref, *refs):
    in_refs, (row_ref, gate_ref, col_ref) = refs[:4], refs[4:]
    mine = lax.broadcasted_iota(jnp.int32, (16, 128), 0) == me_ref[0]
    gates = []
    for ref, lane in zip(in_refs, lanes):
        for k in range(4):
            both = wide(ref[k, first : first + 32, lane : lane + 128])
            gates.append(jnp.sum(jnp.where(mine, both[:16, :] + both[16:, :], 0.0), axis=0, keepdims=True))
    gates = jnp.concatenate(gates, axis=0)
    routed = gates > 0.0
    line = lax.broadcasted_iota(jnp.int32, (128, 128), 0)
    column = lax.broadcasted_iota(jnp.int32, (128, 128), 1)
    before = low((line <= column) & (line // 64 == column // 64))
    count = matmul(low(routed), before)
    source = lax.broadcasted_iota(jnp.int32, (16, 128), 0)
    token = lax.broadcasted_iota(jnp.int32, (16, 128), 1)
    block = ((source % 2) * 2 + token // 64).astype(F32)
    target = jnp.where(routed, block * slots + count - 1.0, -1.0)
    turned = target.T
    for k in range(16):
        part = slice((k % 2) * 128, (k % 2 + 1) * 128)
        row_ref[k // 2, :, part] = target[k : k + 1, :].astype(jnp.int32)
        gate_ref[k // 2, :, part] = gates[k : k + 1, :]
        col_ref[k * 128 : (k + 1) * 128, :] = turned[:, k : k + 1].astype(jnp.int32)


def routing(me, arrays, first, lanes, slots):
    outs = [shaped((8, 1, CHUNK), jnp.int32), shaped((8, 1, CHUNK), F32), shaped((8 * CHUNK, 1), jnp.int32)]
    return whole_call(functools.partial(routing_kernel, first, lanes, slots), arrays, outs, scalars=me)


def enter_grad_kernel(slots, *refs):
    g_refs, (target_ref, gate_ref, rg0_ref, rg1_ref, rs_ref) = refs[:-5], refs[-5:]
    half = rg0_ref.shape[1]
    for j in range(8):
        grad = pair(g_refs, j)
        chosen = lax.broadcasted_iota(jnp.int32, (slots, CHUNK), 0) == target_ref[j]
        share = jnp.sum(jnp.where(chosen, gate_ref[j], 0.0), axis=1, keepdims=True)
        rs_ref[j * slots : (j + 1) * slots, :] = share
        value = low(matmul(low(chosen), grad) * share)
        rg0_ref[j * slots : (j + 1) * slots, :] = value[:, :half]
        rg1_ref[j * slots : (j + 1) * slots, :] = value[:, half:]


def dispatch_kernel(slots, *refs):
    t_refs, (target_ref, rx0_ref, rx1_ref) = refs[:-3], refs[-3:]
    half = rx0_ref.shape[1]
    for j in range(8):
        chosen = lax.broadcasted_iota(jnp.int32, (slots, CHUNK), 0) == target_ref[j]
        value = low(matmul(low(chosen), pair(t_refs, j)))
        rx0_ref[j * slots : (j + 1) * slots, :] = value[:, :half]
        rx1_ref[j * slots : (j + 1) * slots, :] = value[:, half:]


def hidden_shared_kernel(count, *refs):
    t_refs, g_refs, (sgu_ref, sd_ref, act_ref, pre_ref) = refs[:count], refs[count:-4], refs[-4:]
    third = sd_ref.shape[1]
    for j in range(8):
        rows = slice(j * CHUNK, (j + 1) * CHUNK)
        both = matmul(pair(t_refs, j), sgu_ref[...])
        gate_pre, up = both[:, :third], both[:, third:]
        d_act = matmul(pair(g_refs, j), sd_ref[...])
        sigma = jax.nn.sigmoid(gate_pre)
        swish = gate_pre * sigma
        act_ref[rows, :] = low(swish * up)
        pre_ref[rows, :third] = low(d_act * up * (sigma * (1.0 + gate_pre * (1.0 - sigma))))
        pre_ref[rows, third:] = low(d_act * swish)


def enter_grad(g_pieces, target, gate, slots):
    own, width = g_pieces[0].shape
    args = list(g_pieces) + [target, gate]
    outs = [shaped((slots, width // 2), BF)] * 2 + [shaped((slots, 1), F32)]
    flops = 32 * own * width * (slots // 8)
    return whole_call(functools.partial(enter_grad_kernel, slots // 8), args, outs, flops=flops)


def dispatch(t_pieces, target, slots):
    own, width = t_pieces[0].shape
    args = list(t_pieces) + [target]
    outs = [shaped((slots, width // 2), BF)] * 2
    flops = 32 * own * width * (slots // 8)
    return whole_call(functools.partial(dispatch_kernel, slots // 8), args, outs, flops=flops)


def hidden_shared(t_pieces, g_pieces, s_both, s_down):
    own, width = t_pieces[0].shape
    third = s_down.shape[1]
    args = list(t_pieces) + list(g_pieces) + [s_both, s_down]
    outs = [shaped((16 * own, third), BF), shaped((16 * own, 2 * third), BF)]
    return whole_call(functools.partial(hidden_shared_kernel, len(t_pieces)), args, outs, flops=96 * own * width * third)


def hidden_kernel(x0_ref, x1_ref, r0_ref, r1_ref, g0_ref, g1_ref, u0_ref, u1_ref, d0_ref, d1_ref, act_ref, dg_ref, du_ref, away_ref):
    step = 256
    for j in range(x0_ref.shape[0] // step):
        rows = slice(j * step, (j + 1) * step)
        x0, x1 = x0_ref[rows, :], x1_ref[rows, :]
        gate = matmul(x0, g0_ref[...]) + matmul(x1, g1_ref[...])
        up = matmul(x0, u0_ref[...]) + matmul(x1, u1_ref[...])
        d_act = mat_trans(r0_ref[rows, :], d0_ref[...]) + mat_trans(r1_ref[rows, :], d1_ref[...])
        sigma = jax.nn.sigmoid(gate)
        swish = gate * sigma
        act_ref[rows, :] = low(swish * up)
        dg_ref[rows, :] = low(d_act * up * (sigma * (1.0 + gate * (1.0 - sigma))))
        du_ref[rows, :] = low(d_act * swish)
    away_ref[...] = low(contract(act_ref[...], r1_ref[...]))


def tiled_call(kernel, steps, args, specs, outs, out_specs, scratch=(), flops=0, aliases=None):
    size = sum(a.size * a.dtype.itemsize for a in list(args) + list(outs))
    return pl.pallas_call(
        kernel,
        grid=(steps,),
        in_specs=specs,
        out_specs=out_specs,
        out_shape=outs,
        scratch_shapes=list(scratch),
        input_output_aliases=aliases or {},
        compiler_params=pltpu.CompilerParams(vmem_limit_bytes=VMEM_LIMIT),
        cost_estimate=pl.CostEstimate(flops=flops, bytes_accessed=size, transcendentals=0),
    )(*args)


def whole_spec(array):
    return pl.BlockSpec(array.shape, lambda i: (0,) * array.ndim)


def expert_hidden(rows_x, rows_g, own, other):
    slots, half = rows_x[0].shape
    hidden = own[0].shape[1]
    tile = HIDDEN_TILE
    by_column = pl.BlockSpec((half, tile), lambda i: (0, i))
    by_row = pl.BlockSpec((tile, half), lambda i: (i, 0))
    args = list(rows_x) + list(rows_g) + [own[0], other[0], own[1], other[1], own[2], other[2]]
    specs = [whole_spec(value) for value in args[:4]] + [by_column] * 4 + [by_row] * 2
    outs = [shaped((slots, hidden), BF)] * 3 + [shaped((hidden, half), BF)]
    out_specs = [pl.BlockSpec((slots, tile), lambda i: (0, i))] * 3 + [by_row]
    flops = 14 * slots * half * hidden
    return tiled_call(hidden_kernel, -(-hidden // tile), args, specs, outs, out_specs, flops=flops)


def back_kernel(per, dg_ref, du_ref, g0_ref, g1_ref, u0_ref, u1_ref, target_ref, left_ref, right_ref, *refs):
    out_refs, rows_ref = refs[:4], refs[4]
    steps = pl.num_programs(0) // 2
    own = pl.program_id(0) < steps

    @pl.when(own)
    def _():
        rows_ref[...] = low(mat_trans(dg_ref[...], g0_ref[...]) + mat_trans(du_ref[...], u0_ref[...]))

    @pl.when(jnp.logical_not(own))
    def _():
        rows_ref[...] = low(mat_trans(dg_ref[...], g1_ref[...]) + mat_trans(du_ref[...], u1_ref[...]))

    right = right_ref[...]
    for j in range(8):
        hot = low(lax.broadcasted_iota(jnp.int32, (CHUNK, per), 1) == target_ref[j * CHUNK : (j + 1) * CHUNK, :])
        out = matmul(hot, rows_ref[j * per : (j + 1) * per, :])
        out = low(out + mat_trans(left_ref[j * CHUNK : (j + 1) * CHUNK, :], right))
        out_refs[j // 2][(j % 2) * CHUNK : (j % 2 + 1) * CHUNK, :] = out


def expert_back(d_gate, d_up, own, other, target, left, right):
    slots, hidden = d_gate.shape
    rows, columns = left.shape
    width = right.shape[0]
    tile = 256
    steps = width // tile // 2
    near = pl.BlockSpec((tile, hidden), lambda i: (jnp.minimum(i, steps - 1), 0))
    far = pl.BlockSpec((tile, hidden), lambda i: (jnp.maximum(i - steps, 0), 0))
    args = [d_gate, d_up, own[0], other[0], own[1], other[1], target, left, right]
    specs = [whole_spec(d_gate), whole_spec(d_up)] + [near, far] * 2
    specs += [whole_spec(target), whole_spec(left), pl.BlockSpec((tile, columns), lambda i: (i, 0))]
    outs = [shaped((rows // 4, width), BF)] * 4
    out_specs = [pl.BlockSpec((rows // 4, tile), lambda i: (0, i))] * 4
    flops = 4 * slots * width * hidden + 2 * rows * width * (columns + slots // 8)
    return tiled_call(
        functools.partial(back_kernel, slots // 8), 2 * steps, args, specs, outs, out_specs,
        (pltpu.VMEM((slots, tile), BF),), flops=flops,
    )


def out_kernel(per, act_ref, share_ref, d0_ref, d1_ref, target_ref, left_ref, right_ref, *refs):
    out_refs, rows_ref = refs[:4], refs[4]
    steps = pl.num_programs(0) // 2
    own = pl.program_id(0) < steps

    @pl.when(own)
    def _():
        rows_ref[...] = low(matmul(act_ref[...], d0_ref[...]) * share_ref[...])

    @pl.when(jnp.logical_not(own))
    def _():
        rows_ref[...] = low(matmul(act_ref[...], d1_ref[...]) * share_ref[...])

    right = right_ref[...]
    for j in range(8):
        hot = low(lax.broadcasted_iota(jnp.int32, (CHUNK, per), 1) == target_ref[j * CHUNK : (j + 1) * CHUNK, :])
        out = matmul(hot, rows_ref[j * per : (j + 1) * per, :])
        out = low(out + mat_trans(left_ref[j * CHUNK : (j + 1) * CHUNK, :], right))
        out_refs[j // 2][(j % 2) * CHUNK : (j % 2 + 1) * CHUNK, :] = out


def expert_out(act, share, own, other, target, left, right):
    slots, hidden = act.shape
    rows, columns = left.shape
    width = right.shape[0]
    tile = 256
    steps = width // tile // 2
    args = [act, share, own[2], other[2], target, left, right]
    specs = [
        whole_spec(act), whole_spec(share),
        pl.BlockSpec((hidden, tile), lambda i: (0, jnp.minimum(i, steps - 1))),
        pl.BlockSpec((hidden, tile), lambda i: (0, jnp.maximum(i - steps, 0))),
        whole_spec(target), whole_spec(left), pl.BlockSpec((tile, columns), lambda i: (i, 0)),
    ]
    outs = [shaped((rows // 4, width), BF)] * 4
    out_specs = [pl.BlockSpec((rows // 4, tile), lambda i: (0, i))] * 4
    flops = 2 * slots * width * hidden + 2 * rows * width * (columns + slots // 8)
    return tiled_call(
        functools.partial(out_kernel, slots // 8), 2 * steps, args, specs, outs, out_specs,
        (pltpu.VMEM((slots, tile), BF),), flops=flops,
    )


def shared_kernel(part, count, *refs):
    t_refs, g_refs, (pre_ref, act_ref, out_ref, acc_t, acc_g) = refs[:count], refs[count:-5], refs[-5:]
    pad = act_ref.shape[1]
    for j in range(8):
        rows = slice(j * CHUNK, (j + 1) * CHUNK)
        by_tok = contract(pre_ref[rows, :], pair(t_refs, j))
        by_grad = contract(act_ref[rows, :], pair(g_refs, j))
        acc_t[...] = by_tok if j == 0 else acc_t[...] + by_tok
        acc_g[...] = by_grad if j == 0 else acc_g[...] + by_grad
    parts = [acc_t[:part, :], acc_t[pad : pad + part, :], acc_g[:part, :]]
    spare = -3 * part % 128
    if spare:
        parts.append(jnp.zeros((spare, acc_t.shape[1]), F32))
    out_ref[...] = low(jnp.concatenate(parts, axis=0).T[:, : 3 * part])


def shared_gradient(t_pieces, g_pieces, pre, act, part):
    own, width = t_pieces[0].shape
    args = list(t_pieces) + list(g_pieces) + [pre, act]
    outs = [shaped((width, 3 * part), BF)]
    scratch = (pltpu.VMEM((pre.shape[1], width), F32), pltpu.VMEM((act.shape[1], width), F32))
    flops = 32 * own * width * (pre.shape[1] + act.shape[1])
    return whole_call(functools.partial(shared_kernel, part, len(t_pieces)), args, outs, scratch, flops=flops)[0]


def local(
    tokens, lengths, routes, gates, norm_in, latent_gain, norm_mid, w_query, w_latent, w_expand, w_output,
    shared_gate, shared_up, shared_down, expert_gate, expert_up, expert_down, cotangent,
):
    micro = lengths.shape[0]
    own_rows, width = tokens.shape
    rows = own_rows // micro
    experts = lax.axis_size("expert")
    ndp = lax.axis_size("dp")
    two = ndp == 2
    cap = rows * TOP * 4 // (3 * experts)
    blocks = experts * micro
    all_rows = experts * own_rows
    devices = ndp * experts
    shard = width // devices
    lat_rows = w_expand.shape[0]
    lat_cols = w_latent.shape[1]
    ff_s = shared_gate.shape[1]
    ff_part = ff_s // experts
    ff_pad = -(-ff_part // 128) * 128
    half = width // 2
    me = lax.axis_index("expert")
    dp = lax.axis_index("dp")
    core, x, z = me % 2, (me // 2) % 2, me // 4

    def turn(value):
        if not two:
            return value
        swapped = jnp.concatenate([value[..., half:], value[..., :half]], axis=-1)
        return jnp.where(dp == 1, swapped, value)

    def dp_swap(value):
        return lax.ppermute(value, "dp", [(0, 1), (1, 0)])

    clock = Clock(dp_swap)

    def lane(value):
        return [(dp_swap, value)] if two else []

    def dp_gather(value, axis):
        return lax.all_gather(value, "dp", axis=axis, tiled=True)

    def dp_scatter(value, axis=0):
        return lax.psum_scatter(value, "dp", scatter_dimension=axis, tiled=True)

    def cut(value, k):
        return value[k * own_rows : (k + 1) * own_rows]

    number = jnp.arange(experts, dtype=jnp.int32)
    near_z, near_x, near_c = number % 4, (number // 4) % 2, number // 8
    row_index = ((z + 4 - near_z) % 4) * 4 + (near_x ^ x) * 2 + (near_c ^ core)
    few_index = jnp.concatenate([row_index[:4], row_index[8:12]])
    n_z, n_x, n_c = number // 4, (number // 2) % 2, number % 2
    block_index = ((z + 4 - n_z) % 4) * 4 + (n_x ^ x) * 2 + (n_c ^ core)

    pairs = HEADS // 2
    groups = shard // lat_rows
    piece = w_query.reshape(shard, pairs, 2, HD + RD).transpose(1, 0, 2, 3)
    piece = jnp.concatenate(
        [
            piece[..., :HD].reshape(pairs, shard, 2 * HD),
            piece[..., HD:].reshape(pairs, shard, 2 * RD),
            w_output.reshape(pairs, O_COLS, shard).transpose(0, 2, 1),
            w_expand.reshape(lat_rows, pairs, groups, E_COLS).transpose(1, 2, 0, 3).reshape(pairs, shard, E_COLS),
        ],
        axis=2,
    )
    piece = piece.reshape(4, 2, shard, W_COLS)
    kept, away = at(piece, core, 1), at(piece, 1 - core, 1)

    by_expert = jnp.sum(jnp.where(routes.T[None] == number[:, None, None], gates.T[None], 0.0), axis=1)
    gate_high = low(by_expert)
    gate_low = low(by_expert - wide(gate_high))

    def as_row(value):
        return jnp.pad(value.reshape(1, -1), ((0, 0), (0, own_rows - value.size)))

    small_rows = 48
    lat_gain_rows = lax.dynamic_update_slice(jnp.zeros((LAT,), BF), latent_gain, ((dp * experts + me) * lat_rows,))
    small = jnp.concatenate(
        [
            as_row(jnp.concatenate([norm_in, norm_mid])), lat_gain_rows.reshape(4, 128), as_row(low(lengths)),
            jnp.zeros((10, own_rows), BF), gate_high, gate_low,
        ],
        axis=0,
    )

    s_piece = jnp.concatenate(
        [
            shared_gate.reshape(shard, experts, ff_part).transpose(1, 0, 2),
            shared_up.reshape(shard, experts, ff_part).transpose(1, 0, 2),
            shared_down.reshape(experts, ff_part, shard).transpose(0, 2, 1),
        ],
        axis=2,
    ).reshape(4, 2, 2, shard, 3 * ff_part)
    own_expert = (expert_gate[0], expert_up[0], expert_down[0])
    x0 = tokens
    g0 = low(turn(cotangent))

    if two:
        fetched = [clock.add(value) for value in (own_expert[2], own_expert[0], own_expert[1])]
        wide_lat = jnp.pad(w_latent, ((0, 0), (0, 640 - lat_cols)))
        low_rows = jnp.pad(small, ((0, shard - small_rows), (0, 0)))
        lat = jnp.concatenate([wide_lat[:, :384], jnp.concatenate([wide_lat[:, 384:], low_rows], axis=1)], axis=0)
    else:
        lat = small
    s_kept, s_away = at(s_piece, core, 2), at(s_piece, 1 - core, 2)
    x1 = clock.slot((z_up, x0), feed=0.65)[0][0]
    moved, _, _, _ = clock.slot((core_swap, away), (core_swap, s_away), feed=0.15)
    s_piece = jnp.stack([s_kept, moved[1]], axis=2)
    w_own = jnp.where(
        core == 0, jnp.concatenate([kept, moved[0]], axis=1), jnp.concatenate([moved[0], kept], axis=1)
    )
    if two:
        w_own = jnp.concatenate([w_own, jnp.broadcast_to(lat, (4,) + lat.shape)], axis=2)
    s_kept, s_away = at(s_piece, x, 1), at(s_piece, 1 - x, 1)
    moved, _, _, _ = clock.slot(
        (z_two, at(w_own, (z + 2) % 4, 0)),
        (z_up, at(w_own, (z + 1) % 4, 0)),
        (z_down, at(w_own, (z + 3) % 4, 0)),
        (x_swap, s_away),
        feed=1.17,
    )
    w_own = jnp.stack([at(w_own, z, 0), moved[1], moved[0], moved[2]])
    s_piece = jnp.stack([s_kept, moved[3]], axis=1)
    if two:
        lats = w_own[..., W_COLS:]
        facts = lats[:, shard : shard + small_rows, 256:]
    else:
        facts = jnp.stack([lat, z_up(lat), z_two(lat), z_down(lat)])

    moved, _, _, _ = clock.slot(
        (x_swap, w_own), *lane(w_own), (z_up, x1), (z_up, g0), (core_swap, lats if two else facts)
    )
    w_x, x2, g1, lat_other = moved[0], *moved[-3:]
    facts_few = jnp.concatenate([facts, lat_other[:, shard : shard + small_rows, 256:] if two else lat_other])
    lengths_few = facts_few[:, 5, : lengths.size].astype(jnp.int32).reshape(-1)
    scalars = jnp.concatenate([jnp.stack([dp, z, x, core]).astype(jnp.int32), lengths_few])
    table = jnp.asarray(angle_table(rows))
    s_two, s_up, s_down = (at(s_piece, (z + k) % 4, 0) for k in (2, 1, 3))
    if two:
        w_y = moved[1]
        moved, _, _, _ = clock.slot(
            (x_swap, w_y[:2]), (dp_swap, w_x[2:]), (z_up, x2),
            (core_swap, jnp.concatenate([w_x[..., W_COLS:], w_y[..., W_COLS:]])),
            (core_swap, jnp.concatenate([x0, x1])),
        )
        w_far, x3, lat_other_xy, cx01 = moved[:2], *moved[2:]
        lat_far = jnp.concatenate([w_far[0][..., W_COLS:], w_far[1][..., W_COLS:]])
        moved, _, _, _ = clock.slot(
            (core_swap, lat_far), (core_swap, jnp.concatenate([x2, x3])), (z_up, s_up), (z_down, s_down), feed=0.55
        )
        cx23, s_up, s_down = moved[1:]
        weights = [w_own, w_x, w_y] + w_far
        layout_of = ((0, 0, 0), (1, 0, 0), (0, 1, 0), (1, 1, 0), (1, 1, 2))
        w_lat = [lat_other, lat_other_xy, moved[0]]
        w_exp = gains = gain_lat = jnp.zeros((8, 128), F32)
        route_from = [w_own, w_x, lat_other, lat_other_xy]
        route_lanes = (W_COLS + 256, W_COLS + 256, 256, 256)
    else:
        x3, s_up, s_down = z_up(x2), z_up(s_up), z_down(s_down)
        cx01, cx23 = core_swap(jnp.concatenate([x0, x1])), core_swap(jnp.concatenate([x2, x3]))
        near, far = dp_gather(w_own[None], 0), dp_gather(w_x[None], 0)
        weights = [near[i] for i in range(ndp)] + [far[i] for i in range(ndp)]
        layout_of = tuple((side, j, 0) for side in range(2) for j in range(ndp))
        w_lat = lax.all_gather(w_latent, ("dp", "expert"), axis=0)
        w_lat = [w_lat[i][None] for i in range(devices)]
        facts = lax.all_gather(small, ("dp", "expert"), axis=0)
        gains = wide(facts[:, 0, : 2 * shard]).reshape(devices, 2, shard).transpose(1, 0, 2).reshape(2, width)
        gain_lat = wide(facts[:, 1:5]).sum(axis=0).reshape(1, LAT)
        route_from = jnp.take(lax.dynamic_slice_in_dim(facts, dp * experts, experts, 0), row_index, axis=0)
        route_from = [route_from[4 * i : 4 * i + 4] for i in range(4)]
        route_lanes = (0, 0, 0, 0)
        w_exp = jnp.concatenate([value[..., Q_COLS + O_COLS :] for value in weights], axis=0)
        w_exp = w_exp.reshape(2, ndp, 4, 2 * shard, E_COLS).transpose(1, 2, 0, 3, 4)
        w_exp = w_exp.reshape(devices // 2, -1, E_COLS)
        chips = jnp.arange(devices // 2, dtype=jnp.int32)
        chip_index = chips // 8 * 8 + ((z + 4 - chips // 2 % 4) % 4) * 2 + (chips % 2 ^ x)
        w_exp = reorder([w_exp], chip_index)[0]
        w_exp = w_exp.reshape(devices, groups, lat_rows, E_COLS).transpose(0, 2, 1, 3).reshape(LAT, groups * E_COLS)
    slots = blocks * cap
    route = functools.partial(routing, first=(shard if two else 0) + 16, lanes=route_lanes, slots=cap)

    x_pieces = [x0, x1, x2, x3, cx01, cx23]
    moved, _, _, made = clock.slot(
        (x_swap, g0), (z_up, g1), (z_down, g0),
        feed=1.0,
        work=[
            (
                lambda *a: attention_forward(*a[:3], layout_of, *a[3:], split=two),
                scalars, x_pieces, weights, w_lat, w_exp, gains, gain_lat, table,
            )
        ],
    )
    gx0, g2, g3 = moved
    (part_near, part_far), saved = made[0]
    gain_in, gain_mid, gain_lat = saved[-3:]

    moved, _, _, _ = clock.slot((core_swap, part_far), (z_two, s_two), feed=0.55)
    s_two = moved[1]
    s_piece = jnp.stack([at(s_piece, z, 0), s_up, s_two, s_down]).reshape(experts, shard, 3 * ff_part)
    g_near = jnp.concatenate([g0, g1, g2, g3])
    terms = [wide(cut(part_near, k)) + wide(cut(moved[0], k)) for k in range(4)]
    moved, _, _, made = clock.slot(
        (z_down, low(terms[3])), (x_swap, g1), work=[(route, me.reshape(1), route_from)], feed=0.67
    )
    gx1 = moved[1]
    target_row, gate_row, target_col = made[0]
    moved, _, _, _ = clock.slot(
        (z_down, low(terms[2] + wide(moved[0]))), (x_swap, g2), (core_swap, g_near), feed=0.67
    )
    gx2, cg_near = moved[1:]
    moved, _, _, _ = clock.slot((z_down, low(terms[1] + wide(moved[0]))), (x_swap, g3), feed=0.45)
    gx3 = moved[1]
    xf = wide(tokens)
    mid = xf + terms[0] + wide(moved[0])
    scale_mid = rms_scale(mid)
    t0 = turn(low(mid * scale_mid * gain_mid))

    g_far = jnp.concatenate([gx0, gx1, gx2, gx3])
    join = lambda *pieces: jnp.concatenate(pieces, axis=0)
    moved, _, _, made = clock.slot(
        (z_up, t0), (x_swap, t0), work=[(join, *fetched[0][2])] if two else [], feed=0.67
    )
    t1, tx0 = moved
    down_got = made
    moved, _, _, _ = clock.slot((z_up, t1), (x_swap, t1), (core_swap, g_far), feed=0.67)
    t2, tx1, cg_far = moved
    g_pieces = [g0, g1, g2, g3, gx0, gx1, gx2, gx3, cg_near, cg_far]
    part = experts // 2
    moved, _, _, made = clock.slot(
        (z_up, t2), (x_swap, t2), *lane(s_piece[:part]), (core_swap, tx0),
        work=[(functools.partial(enter_grad, slots=slots), g_pieces, target_row, gate_row)],
    )
    t3, tx2 = moved[:2]
    s_got, ctx0 = moved[2:-1], moved[-1]
    *rows_g, share = made[0]
    t_near = jnp.concatenate([t0, t1, t2, t3])
    moved, _, _, made = clock.slot(
        (x_swap, t3), (core_swap, t_near), *lane(s_piece[part:]), (core_swap, tx1),
        work=[(join, *fetched[1][2])] if two else [],
    )
    tx3, ct_near = moved[:2]
    s_got, ctx1 = s_got + moved[2:-1], moved[-1]
    gate_got = made
    if two:
        s_pieces = [s_piece, jnp.concatenate(s_got)]
    else:
        s_pieces = jnp.split(dp_gather(s_piece[None], 0), ndp)
        s_pieces = [value.reshape(s_piece.shape) for value in s_pieces]
    moved, _, _, made = clock.slot(
        (core_swap, tx2), (core_swap, tx3), feed=0.55,
        work=[(lambda *a: shared_weights(a, block_index, ff_pad), *s_pieces)],
    )
    s_both, s_down_w = made[0]
    t_pieces = [t0, t1, t2, t3, tx0, tx1, tx2, tx3, ct_near, ctx0, ctx1, *moved]

    _, _, _, made = clock.slot(
        work=[
            (functools.partial(dispatch, slots=slots), t_pieces, target_row),
            (hidden_shared, t_pieces, g_pieces, s_both, s_down_w),
        ],
        feed=3.0,
    )
    rows_x, (s_act, d_s_pre) = made
    if two:
        assert all(entry[1] == entry[0].shape[0] for entry in fetched)
        own, other = own_expert, [gate_got[0], join(*fetched[2][2]), down_got[0]]
    else:
        full = [dp_gather(own_expert[0], 0), dp_gather(own_expert[1], 0), dp_gather(own_expert[2], 1)]
        own = [full[0][:half], full[1][:half], full[2][:, :half]]
        other = [full[0][half:], full[1][half:], full[2][:, half:]]
    _, _, _, made = clock.slot(work=[(expert_hidden, rows_x, rows_g, own, other)])
    e_act, d_gate, d_up, d_down_away = made[0]
    if two:
        sent = [clock.add(d_down_away)]

    _, _, _, made = clock.slot(
        work=[(expert_back, d_gate, d_up, own, other, target_col, d_s_pre, s_both)], feed=1.42
    )
    near, near_x, far, far_x = made[0]
    moved, _, _, made = clock.slot((core_swap, far_x), work=[(contract, rows_x[1], d_gate)], feed=0.35)
    if two:
        sent.append(clock.add(low(made[0])))
    away = [low(wide(cut(near_x, k)) + wide(cut(moved[0], k))) for k in range(4)]
    moved, _, _, made = clock.slot(
        (x_swap, away[3]), (core_swap, far),
        feed=0.75,
        work=[(functools.partial(shared_gradient, part=ff_part), t_pieces, g_pieces, d_s_pre, s_act)],
    )
    d_shared = made[0].reshape(ndp, experts, shard, 3 * ff_part)
    home = [wide(cut(near, k)) + wide(cut(moved[1], k)) for k in range(4)]
    moved, _, _, made = clock.slot(
        (x_swap, away[2]), (z_down, low(home[3] + wide(moved[0]))),
        feed=0.9,
        work=[(expert_out, e_act, share, own, other, target_col, s_act, s_down_w)],
    )
    o_near, o_near_x, o_far, o_far_x = made[0]
    s_away = d_shared[-1]
    moved, _, _, made = clock.slot(
        (x_swap, away[1]), (z_down, low(home[2] + wide(moved[0]) + wide(moved[1]))), (core_swap, o_far_x),
        *lane(s_away[:part]),
        work=[(contract, rows_x[1], d_up), (contract, e_act, rows_g[0])],
    )
    d_down_home = made[1]
    if two:
        sent.append(clock.add(low(made[0])))
    s_got = moved[3:]
    o_away = [low(wide(cut(o_near_x, k)) + wide(cut(moved[2], k))) for k in range(4)]
    moved, _, _, made = clock.slot(
        (x_swap, away[0]), (z_down, low(home[1] + wide(moved[0]) + wide(moved[1]))), (core_swap, o_far),
        *lane(s_away[part:]),
        work=[(contract, rows_x[0], d_gate)],
    )
    d_gate_home = made[0]
    s_got += moved[3:]
    o_home = [wide(cut(o_near, k)) + wide(cut(moved[2], k)) for k in range(4)]
    if two:
        d_shared = low(wide(d_shared[0]) + wide(jnp.concatenate(s_got)))
    else:
        d_shared = dp_scatter(d_shared)[0]
    d_shared = d_shared.reshape(4, 2, 2, shard, 3 * ff_part)
    d_mid_normed = turn(home[0] + wide(moved[0]) + wide(moved[1]))
    d_mid_in, d_gain_mid = rms_back(d_mid_normed, mid, scale_mid, gain_mid)
    d_mid = cotangent + d_mid_in

    a0 = low(d_mid)
    s_kept, s_away = at(d_shared, x, 1), at(d_shared, 1 - x, 1)
    moved, _, _, made = clock.slot(
        (z_up, a0), (x_swap, o_away[3]), lasting=1.45, work=[(contract, rows_x[0], d_up)]
    )
    a1, ox3 = moved
    d_up_home = made[0]
    moved, _, _, _ = clock.slot((z_up, a1), (x_swap, o_away[2]), fed_before=clock.lasting)
    a2, ox2 = moved
    moved, _, _, _ = clock.slot((z_up, a2), (x_swap, o_away[1]), feed=0.67)
    a3, ox1 = moved
    moved, _, _, _ = clock.slot(
        (core_swap, jnp.concatenate([a0, a1, a2, a3])), (x_swap, s_away),
        (z_down, low(o_home[3] + wide(ox3))), feed=0.6,
    )
    a_pieces = [a0, a1, a2, a3, moved[0]]
    d_shared = jnp.stack([s_kept, moved[1]], axis=1)
    o_sum = low(o_home[2] + wide(ox2) + wide(moved[2]))
    backward = functools.partial(attention_backward, lat_rows=lat_rows)
    moved, _, _, made = clock.slot(
        (z_two, at(d_shared, (z + 2) % 4, 0)), (z_up, at(d_shared, (z + 1) % 4, 0)),
        (z_down, at(d_shared, (z + 3) % 4, 0)), (z_down, o_sum),
        feed=1.6,
        work=[(backward, scalars, x_pieces, a_pieces, saved, d_gain_mid.reshape(1, width), table)],
    )
    d_shared = jnp.stack([at(d_shared, z, 0), moved[1], moved[0], moved[2]])
    o_sum = low(o_home[1] + wide(ox1) + wide(moved[3]))
    d_norm, d_head, d_wl = made[0]
    same_x = [[i for i in range(experts) if i // 2 % 2 == side] for side in range(2)]
    d_normed = lax.psum_scatter(d_norm, "expert", scatter_dimension=0, axis_index_groups=same_x, tiled=True)

    if not two:
        d_head = d_head.reshape(ndp, 4, 2, 2 * shard, W_COLS)
        d_wl = d_wl.reshape(ndp, 4, 2, 2, shard, -1)
    s_kept, s_away = at(d_shared, core, 2), at(d_shared, 1 - core, 2)

    def add_received(home, *pieces):
        return home + wide(jnp.concatenate(pieces))

    if two:
        moved, _, _, made = clock.slot(
            (x_swap, d_head[4:8]), (dp_swap, d_head[12:]), (core_swap, d_wl[1]), (core_swap, s_away),
            work=[(add_received, d_down_home, *sent[0][2])],
        )
        d_down = made[0]
        first = (wide(d_head[:4]) + wide(moved[0])).reshape(ndp, 2, 2 * shard, W_COLS)
        second = (wide(d_head[8:12]) + wide(moved[1])).reshape(2, 2, 2 * shard, W_COLS)
        d_wl = (wide(d_wl[0]) + wide(moved[2])).reshape(ndp, 4, 2, shard, -1)
        d_shared = jnp.stack([s_kept, moved[3]], axis=2)
        moved, _, _, made = clock.slot(
            (dp_swap, low(at(first, 1 - dp, 0))), (x_swap, low(at(second, 1 - x, 1))),
            (x_swap, low(at(d_wl, 1 - x, 2))), (z_down, o_sum), feed=0.45,
            work=[(add_received, d_gate_home, *sent[1][2])],
        )
        d_gate_all = made[0]
        o_last = o_home[0] + wide(moved[3])
        first = at(first, dp, 0) + wide(moved[0])
        second = at(second, x, 1) + wide(moved[1])
        d_wl = at(d_wl, x, 2) + wide(moved[2])
        d_head = low(jnp.concatenate([first, second]))
    else:
        d_head = wide(at(d_head, x, 2)) + wide(x_swap(at(d_head, 1 - x, 2)))
        d_head = dp_scatter(low(d_head))[0]
        d_wl = wide(at(d_wl, core, 3)) + wide(core_swap(at(d_wl, 1 - core, 3)))
        d_wl = at(d_wl, x, 2) + wide(x_swap(low(at(d_wl, 1 - x, 2))))
        d_shared = jnp.stack([s_kept, core_swap(s_away)], axis=2)
        o_last = o_home[0] + wide(z_down(o_sum))
    d_shared = d_shared.reshape(experts, shard, 3 * ff_part)
    moved, _, _, _ = clock.slot(
        (z_two, at(d_head, (z + 2) % 4, 0)), (z_down, at(d_head, (z + 3) % 4, 0)),
        (z_up, at(d_head, (z + 1) % 4, 0)),
        *(lane(low(at(d_wl, 1 - dp, 0))) if two else []), feed=3.0,
    )
    d_head = jnp.stack([at(d_head, z, 0), moved[1], moved[0], moved[2]]).reshape(4, 2, shard, W_COLS)
    d_wl = at(d_wl, dp, 0) + wide(moved[3]) if two else wide(dp_scatter(low(d_wl))[0])
    moved, _, ended, made = clock.slot(
        (core_swap, at(d_head, 1 - core, 1)), (z_two, low(at(d_wl, (z + 2) % 4, 0))),
        (z_down, low(at(d_wl, (z + 3) % 4, 0))), (z_up, low(at(d_wl, (z + 1) % 4, 0))), (x_swap, o_away[0]),
        end=[d_normed], work=[(add_received, d_up_home, *sent[2][2])] if two else [],
    )
    d_up_all = made[0] if two else None
    out = low(mid + turn(o_last + wide(moved[4])))
    d_head = jnp.stack([at(d_head, core, 1), moved[0]], axis=1).reshape(pairs, shard, W_COLS)
    d_wl = at(d_wl, z, 0) + wide(moved[1]) + wide(moved[2]) + wide(moved[3])
    d_normed = wide(ended[0])

    if two:
        assert all(entry[1] == entry[0].shape[0] for entry in sent)
        d_expert = [d_gate_all, d_up_all, d_down]
    else:
        d_expert = [
            wide(dp_scatter(low(jnp.concatenate([contract(value, d) for value in rows_x]))))
            for d in (d_gate, d_up)
        ]
        d_expert.append(wide(dp_scatter(low(jnp.concatenate([contract(e_act, value) for value in rows_g], axis=1)), 1)))
    d_in, _ = rms_back(d_normed, xf, rms_scale(xf), gain_in)
    d_tokens = d_mid + d_in
    d_shared = wide(reorder([d_shared], block_index)[0])
    grad_sg, grad_su = (
        d_shared[:, :, i * ff_part : (i + 1) * ff_part].transpose(1, 0, 2).reshape(shard, ff_s) for i in range(2)
    )
    grad_sd = d_shared[:, :, 2 * ff_part :].transpose(0, 2, 1).reshape(ff_s, shard)
    pair_number = jnp.arange(pairs, dtype=jnp.int32)
    pair_index = ((pair_number // 2 + 4 - z) % 4) * 2 + (pair_number % 2 ^ core)
    if two:
        grad_wq, grad_wo, grad_we = unpack(d_head, pair_index, lat_rows)
        grad_wo = grad_wo.T
    else:
        d_head = wide(reorder([d_head], pair_index)[0])
        grad_wq = jnp.concatenate(
            [
                d_head[..., : 2 * HD].reshape(pairs, shard, 2, HD),
                d_head[..., 2 * HD : Q_COLS].reshape(pairs, shard, 2, RD),
            ],
            axis=3,
        )
        grad_wq = grad_wq.transpose(1, 0, 2, 3).reshape(shard, HEADS * (HD + RD))
        grad_wo = d_head[..., Q_COLS : Q_COLS + O_COLS].transpose(0, 2, 1).reshape(HEADS * VD, shard)
        grad_we = d_head[..., Q_COLS + O_COLS :].reshape(pairs, groups, lat_rows, E_COLS).transpose(2, 0, 1, 3)
        grad_we = grad_we.reshape(lat_rows, HEADS * (HD + VD))
    return (
        out,
        d_tokens,
        d_wl[:, lat_cols],
        d_wl[:lat_rows, lat_cols + 2],
        d_wl[:, lat_cols + 1],
        grad_wq,
        d_wl[:, :lat_cols],
        grad_we,
        grad_wo,
        grad_sg,
        grad_su,
        grad_sd,
        d_expert[0][None],
        d_expert[1][None],
        d_expert[2][None],
    )


def solution(mesh):
    rows = P(("dp", "expert"), None)
    vector = P(("dp", "expert"))
    columns = P(None, ("dp", "expert"))
    by_row = P("expert", "dp", None)
    by_column = P("expert", None, "dp")
    return jax.shard_map(
        local,
        mesh=mesh,
        in_specs=(
            rows, rows, rows, rows, vector, vector, vector, rows, rows, rows, columns, rows, rows, columns, by_row,
            by_row, by_column, rows,
        ),
        out_specs=(
            rows, rows, vector, vector, vector, rows, rows, rows, columns, rows, rows, columns, by_row, by_row,
            by_column,
        ),
        check_vma=False,
    )
```
